32 devices in a mesh: dp: 8 (over y, x, core), mp: 4 (over z).
Axes of the slice: x: 2, y: 2, z: 4, core: 2. Of those that a mesh axis runs over, the one named last changes fastest.
Arguments:
- patches: bfloat16 [16928, 768], P('dp'), may hold values from -6 to 6
- script_ids: int32 [32], P('dp'), may hold values from 0 to 7, as said below
- lengths: int32 [32], P('dp'), may hold values from 1 to 529, as said below
- script_embed: bfloat16 [8, 768], replicated, may hold values from -3 to 3
- norm1_gain: float32 [768], replicated, may hold values from 0.5 to 1.5
- norm1_shift: float32 [768], replicated, may hold values from -2 to 2
- query_key_value_weight: bfloat16 [768, 3, 768], P(None, None, 'mp'), may hold values from -0.21875 to 0.21875
- b_qv: float32 [2, 768], P(None, 'mp'), may hold values from -2 to 2
- attention_out_weight: bfloat16 [768, 768], P('mp'), may hold values from -0.875 to 0.875
- attention_out_bias: float32 [768], replicated, may hold values from -2 to 2
- norm2_gain: float32 [768], replicated, may hold values from 0.5 to 1.5
- norm2_shift: float32 [768], replicated, may hold values from -2 to 2
- up_weight: bfloat16 [768, 3072], P(None, 'mp'), may hold values from -0.21875 to 0.21875
- up_proj_bias: float32 [3072], P('mp'), may hold values from -2 to 2
- down_weight: bfloat16 [3072, 768], P('mp'), may hold values from -0.109375 to 0.109375
- down_proj_bias: float32 [768], replicated, may hold values from -2 to 2
- out_grad: bfloat16 [16928, 768], P('dp'), may hold values from -6 to 6
Outputs:
- block_out: float32 [16928, 768], P(('dp', 'mp'))
- patch_grad: float32 [16928, 768], P(('dp', 'mp'))
- embed_grad: float32 [8, 768], P(None, ('dp', 'mp'))
- norm1_gain_grad: float32 [768], P(('dp', 'mp'))
- norm1_shift_grad: float32 [768], P(('dp', 'mp'))
- qkv_grad: float32 [768, 3, 768], P('dp', None, 'mp')
- qv_bias_grad: float32 [2, 768], P(None, ('mp', 'dp'))
- out_proj_grad: float32 [768, 768], P('mp', 'dp')
- out_bias_grad: float32 [768], P(('dp', 'mp'))
- norm2_gain_grad: float32 [768], P(('dp', 'mp'))
- norm2_shift_grad: float32 [768], P(('dp', 'mp'))
- up_grad: float32 [768, 3072], P('dp', 'mp')
- up_bias_grad: float32 [3072], P(('mp', 'dp'))
- down_grad: float32 [3072, 768], P('mp', 'dp')
- down_bias_grad: float32 [768], P(('dp', 'mp'))
The draws below stay inside these ranges and needn't reach their ends.
Inputs may be any that keep to these rules, and one draw needn't show every extreme that they name: `script_ids`: at least one strip has script group 0. `lengths`: in every draw some strip has all 529 slots live.
All inputs are finite; a program needn't handle non-finite values.
Results may differ from the reference program's by a relative error of at most 0.02.
Values may be sent and summed in bfloat16 or wider, within the bound.
No kernel may reach another device: no remote copies, remote signals or barrier semaphores. Data moves between devices by JAX's collectives and lax.ppermute only.
A program may use at most 128 MiB of HBM per device.

```python
import jax
import jax.numpy as jnp
from jax import lax

D = 768
HEADS = 12
HD = 64
FF = 3072
LEN = 529
NSCRIPT = 8
STRIP_DEV = 4
STRIPS = 32
TOKENS = 16928
N_DP = 8


def strip_layout(key):
    base = jax.random.fold_in(key, 11)
    kind_key, dense_key, sparse_key, place_key = jax.random.split(base, 4)
    kinds = jax.random.randint(kind_key, (STRIPS,), 0, NSCRIPT)
    chosen = jax.random.randint(place_key, (), 0, STRIPS)
    marked = jnp.arange(STRIPS, dtype=jnp.int32) == chosen
    kinds = jnp.where(marked, 0, kinds)
    dense = jax.random.randint(dense_key, (STRIPS,), LEN - LEN // 8, LEN + 1)
    sparse = jax.random.randint(sparse_key, (STRIPS,), 1, LEN // 2 + 1)
    lens = jnp.where(kinds < 3, dense, sparse)
    lens = jnp.where(marked, LEN, lens)
    return (kinds.astype(jnp.int32), lens.astype(jnp.int32))


def draw_script_ids(key, part):
    return strip_layout(key)[0]


def draw_lengths(key, part):
    return strip_layout(key)[1]


def shard_levels(stream_key, extent, pieces, low, high):
    factor_of, own = 1.0, jax.random.fold_in(stream_key, 6)
    for axis_at, blocks in pieces:
        draws = jnp.exp(jax.random.uniform(jax.random.fold_in(own, axis_at), (blocks,), jnp.float32, low / len(pieces), high / len(pieces)))
        factor_of = factor_of * jnp.repeat(draws, extent[axis_at] // blocks).reshape([-1 if axis == axis_at else 1 for axis in range(len(extent))])
    return factor_of


def scatter_about(stream_key, extent, deviation, reach, shards=(), held_as=jnp.bfloat16):
    factor_of = shard_levels(stream_key, extent, shards, -0.22, 0.18) if shards else 1.0
    values = jax.random.normal(stream_key, extent, jnp.float32) * deviation * factor_of
    return jnp.minimum(jnp.maximum(values, -reach), reach).astype(held_as)


def setup_inputs(seed: int = 0) -> dict:
    streams_of = jax.random.split(jax.random.key(seed), 18)
    patches = scatter_about(streams_of[0], (TOKENS, D), 1.0, 6.0, ((0, 8),))
    script_ids = draw_script_ids(jax.random.fold_in(streams_of[17], 71), 0)
    lengths = draw_lengths(jax.random.fold_in(streams_of[17], 71), 0)
    script_embed = scatter_about(streams_of[3], (NSCRIPT, D), 0.5, 3.0)
    norm1_gain = jnp.clip(1.0 + 0.1 * jax.random.normal(streams_of[4], (D,), jnp.float32), 0.5, 1.5)
    norm1_shift = scatter_about(streams_of[5], (D,), 0.3, 2.0, (), jnp.float32)
    query_key_value_weight = scatter_about(streams_of[6], (D, 3, D), D ** -0.5, 0.21875, ((2, 4),))
    b_qv = scatter_about(streams_of[7], (2, D), 0.3, 2.0, ((1, 4),), jnp.float32)
    attention_out_weight = scatter_about(streams_of[8], (D, D), (D // 16) ** -0.5, 0.875, ((0, 4),))
    attention_out_bias = scatter_about(streams_of[9], (D,), 0.3, 2.0, (), jnp.float32)
    norm2_gain = jnp.clip(1.0 + 0.1 * jax.random.normal(streams_of[10], (D,), jnp.float32), 0.5, 1.5)
    norm2_shift = scatter_about(streams_of[11], (D,), 0.3, 2.0, (), jnp.float32)
    up_weight = scatter_about(streams_of[12], (D, FF), D ** -0.5, 0.21875, ((1, 4),))
    up_proj_bias = scatter_about(streams_of[13], (FF,), 0.3, 2.0, ((0, 4),), jnp.float32)
    down_weight = scatter_about(streams_of[14], (FF, D), FF ** -0.5, 0.109375, ((0, 4),))
    down_proj_bias = scatter_about(streams_of[15], (D,), 0.3, 2.0, (), jnp.float32)
    out_grad = scatter_about(streams_of[16], (TOKENS, D), 1.0, 6.0, ((0, 8),))
    return dict(patches=patches, script_ids=script_ids, lengths=lengths, script_embed=script_embed, norm1_gain=norm1_gain, norm1_shift=norm1_shift, query_key_value_weight=query_key_value_weight, b_qv=b_qv, attention_out_weight=attention_out_weight, attention_out_bias=attention_out_bias, norm2_gain=norm2_gain, norm2_shift=norm2_shift, up_weight=up_weight, up_proj_bias=up_proj_bias, down_weight=down_weight, down_proj_bias=down_proj_bias, out_grad=out_grad)


HIGHEST_ACCURACY = lax.Precision.HIGHEST
EPS = 1e-05

@jax.custom_vjp
def low(v):
    return lax.optimization_barrier(v.astype(jnp.bfloat16)).astype(jnp.float32)

@jax.custom_vjp
def low_back(v):
    return v

def low_keep(v):
    return (low(v), None)

def low_pass(kept, grad):
    return (grad,)

def back_keep(v):
    return (v, None)

def back_low(kept, grad):
    return (low(grad),)
low.defvjp(low_keep, low_pass)
low_back.defvjp(back_keep, back_low)

def norm(rows, gain, shift):
    center = rows - lax.optimization_barrier(jnp.mean(rows, axis=-1, keepdims=True))
    return center * lax.rsqrt(lax.optimization_barrier(jnp.mean(center * center, axis=-1, keepdims=True)) + EPS) * gain + shift

def group_layer(params, rows, added, group_lengths):
    gain1, shift1, query_key_value_weight, b_qv, attention_out_weight, attention_out_bias, gain2, shift2, up_weight, up_proj_bias, down_weight, down_proj_bias = params
    count = rows.shape[0]
    residual_stream = rows + added[:, None, :]
    first_normalized = low(norm(residual_stream, gain1, shift1))
    projected_rows = jnp.einsum('qow,wjb->qojb', first_normalized, query_key_value_weight, precision=HIGHEST_ACCURACY)
    query = low(low_back(projected_rows[:, :, 0] + b_qv[0])).reshape(count, LEN, HEADS, HD)
    keys = low(low_back(projected_rows[:, :, 1])).reshape(count, LEN, HEADS, HD)
    values = low(low_back(projected_rows[:, :, 2] + b_qv[1])).reshape(count, LEN, HEADS, HD)
    scores = jnp.einsum('sqhd,skhd->shqk', query, keys, precision=HIGHEST_ACCURACY) * 0.125
    live = jnp.arange(LEN, dtype=jnp.int32)[None, None, None, :] < group_lengths[:, None, None, None]
    scores = low_back(jnp.where(live, scores, -1e+30))
    top = lax.optimization_barrier(jnp.max(scores, axis=-1, keepdims=True))
    expo = jnp.exp(scores - top)
    probs = low(expo / lax.optimization_barrier(jnp.sum(expo, axis=-1, keepdims=True)))
    attention_mixed = jnp.einsum('shqk,skhd->sqhd', probs, values, precision=HIGHEST_ACCURACY).reshape(count, LEN, D)
    attention_mixed = low(low_back(attention_mixed))
    middle_activation = residual_stream + low_back(jnp.einsum('rtc,cx->rtx', attention_mixed, attention_out_weight, precision=HIGHEST_ACCURACY) + attention_out_bias)
    second_normalized = low(norm(middle_activation, gain2, shift2))
    preactivation = low_back(jnp.einsum('onc,cj->onj', second_normalized, up_weight, precision=HIGHEST_ACCURACY) + up_proj_bias)
    hidden_units = low(jax.nn.gelu(preactivation))
    return middle_activation + low_back(jnp.einsum('rtc,cx->rtx', hidden_units, down_weight, precision=HIGHEST_ACCURACY) + down_proj_bias)

def reference(patches, script_ids, lengths, script_embed, norm1_gain, norm1_shift, query_key_value_weight, b_qv, attention_out_weight, attention_out_bias, norm2_gain, norm2_shift, up_weight, up_proj_bias, down_weight, down_proj_bias, out_grad):

    def full(patches_f, embed_f, *params):
        pick = (script_ids[:, None] == jnp.arange(NSCRIPT, dtype=jnp.int32)[None, :]).astype(jnp.float32)
        added = jnp.dot(pick, embed_f, precision=HIGHEST_ACCURACY)
        rows = patches_f.reshape(N_DP, STRIP_DEV, LEN, D)
        grouped = added.reshape(N_DP, STRIP_DEV, D)
        group_lens = lengths.reshape(N_DP, STRIP_DEV)

        def step(items):
            return group_layer(params, items[0], items[1], items[2])
        return lax.map(jax.checkpoint(step), (rows, grouped, group_lens)).reshape(N_DP * STRIP_DEV * LEN, D)
    inputs = (patches.astype(jnp.float32), script_embed.astype(jnp.float32), norm1_gain.astype(jnp.float32), norm1_shift.astype(jnp.float32), query_key_value_weight.astype(jnp.float32), b_qv.astype(jnp.float32), attention_out_weight.astype(jnp.float32), attention_out_bias.astype(jnp.float32), norm2_gain.astype(jnp.float32), norm2_shift.astype(jnp.float32), up_weight.astype(jnp.float32), up_proj_bias.astype(jnp.float32), down_weight.astype(jnp.float32), down_proj_bias.astype(jnp.float32))
    block, pullback = jax.vjp(full, *inputs)
    grads = pullback(out_grad.astype(jnp.float32))
    return (block, grads[0], grads[1], grads[2], grads[3], grads[4], grads[5], grads[6], grads[7], grads[8], grads[9], grads[10], grads[11], grads[12], grads[13])
```

```python
import numpy as np
import jax
import jax.numpy as jnp
from jax import lax
from jax.sharding import PartitionSpec as P

HD = 64
EPS = 1e-05
MASKED = -1e30
BF16 = jnp.bfloat16
F32 = jnp.float32


def layer_norm(rows, gain, shift):
    center = rows - jnp.mean(rows, axis=-1, keepdims=True)
    scale = lax.rsqrt(jnp.mean(center * center, axis=-1, keepdims=True) + EPS)
    normalized = center * scale
    return (normalized * gain + shift, normalized, scale)


def norm_back(grad_out, normalized, scale, gain):
    scaled = grad_out * gain
    first_mean = jnp.mean(scaled, axis=-1, keepdims=True)
    second_mean = jnp.mean(scaled * normalized, axis=-1, keepdims=True)
    return scale * (scaled - first_mean - normalized * second_mean)


def masked_scores(query, keys, length):
    scores = jnp.einsum("qhd,khd->hqk", query, keys, preferred_element_type=F32) * 0.125
    live = lax.broadcasted_iota(jnp.int32, (1, 1, keys.shape[0]), 2) < length
    return jnp.where(live, scores, MASKED)


def attention_forward(query, keys, values, length):
    scores = masked_scores(query, keys, length)
    top = jnp.max(scores, axis=-1, keepdims=True)
    expo = jnp.exp(scores - top)
    total = jnp.sum(expo, axis=-1, keepdims=True)
    probs = (expo / total).astype(BF16)
    mixed = jnp.einsum("hqk,khd->qhd", probs, values, preferred_element_type=F32)
    return (mixed.astype(BF16), top + jnp.log(total))


def attention_backward(query, keys, values, length, logsum, grad_mixed):
    scores = masked_scores(query, keys, length)
    probs = jnp.exp(scores - logsum)
    grad_probs = jnp.einsum("qhd,khd->hqk", grad_mixed, values, preferred_element_type=F32)
    inner = jnp.sum(probs * grad_probs, axis=-1, keepdims=True)
    grad_scores = (probs * (grad_probs - inner)).astype(BF16)
    grad_query = jnp.einsum("hqk,khd->qhd", grad_scores, keys, preferred_element_type=F32) * 0.125
    grad_key = jnp.einsum("hqk,qhd->khd", grad_scores, query, preferred_element_type=F32) * 0.125
    grad_value = jnp.einsum("hqk,qhd->khd", probs.astype(BF16), grad_mixed, preferred_element_type=F32)
    return tuple(g.astype(BF16) for g in (grad_query, grad_key, grad_value))


class Ring:
    def __init__(self, dp, mp):
        self.dp, self.mp = dp, mp
        bits = list(range(1, dp.bit_length() - 1))
        self.orders = (bits, bits[::-1])
        self.stages = [[(i, i ^ (1 << self.orders[i & 1][t])) for i in range(dp)] for t in range(len(bits))]
        self.pair = [(i, i ^ 1) for i in range(dp)]
        halves = []
        for order in self.orders:
            masks = [0]
            for bit in order:
                masks = masks + [m | (1 << bit) for m in masks]
            halves.append(masks)
        self.masks = np.array([halves[0] + [1 ^ m for m in halves[1]], halves[1] + [1 ^ m for m in halves[0]]], np.int32)

    def shift(self, s):
        return [(i, (i + s) % self.mp) for i in range(self.mp)]

    def gather(self, piece, extra):
        rows = piece.shape[0] - extra
        got = [lax.ppermute(piece, "mp", self.shift(s)) for s in range(1, self.mp)]
        held = jnp.stack([g[:rows] for g in got])
        for stage in self.stages:
            held = jnp.concatenate([held, lax.ppermute(held, "dp", stage)], axis=1)
        return held, lax.ppermute(held, "dp", self.pair), [g[rows:] for g in got]

    def scatter(self, low_half, high_half):
        got = lax.ppermute(high_half, "dp", self.pair)
        held = low_half
        for stage in self.stages[::-1]:
            half = held.shape[1] // 2
            send = (held[:, half:].astype(F32) + got[:, half:].astype(F32)).astype(held.dtype)
            keep = (held[:, :half].astype(F32) + got[:, :half].astype(F32)).astype(held.dtype)
            got, held = lax.ppermute(send, "dp", stage), keep
        held = (held.astype(F32) + got.astype(F32)).astype(held.dtype)
        parts = [lax.ppermute(held[s], "mp", self.shift(-s)) for s in range(1, self.mp)]
        return sum([p.astype(F32) for p in parts], held[0].astype(F32))


def on_device(
    patches,
    script_ids,
    lengths,
    script_embed,
    norm1_gain,
    norm1_shift,
    query_key_value_weight,
    b_qv,
    attention_out_weight,
    attention_out_bias,
    norm2_gain,
    norm2_shift,
    up_weight,
    up_proj_bias,
    down_weight,
    down_proj_bias,
    out_grad,
):
    dp, mp = lax.axis_size("dp"), lax.axis_size("mp")
    ring = Ring(dp, mp)
    here, across = lax.axis_index("dp"), lax.axis_index("mp")
    rows_all, width = patches.shape
    rows = rows_all // mp
    share = width // dp
    head_cols = query_key_value_weight.shape[2]
    hidden_cols = up_weight.shape[1]
    heads = head_cols // HD
    kinds = script_embed.shape[0]

    order = jnp.where((here & 1) == 0, ring.masks[0], ring.masks[1]) ^ here
    source = (order[:, None] * share + jnp.arange(share, dtype=jnp.int32)[None, :]).reshape(width)
    place = (lax.broadcasted_iota(jnp.int32, (width, width), 0) == source[None, :]).astype(BF16)

    own_att = jnp.concatenate([query_key_value_weight.reshape(width, 3 * head_cols), attention_out_weight.T], axis=1)
    own_up, own_down = up_weight, down_weight.T

    def share_of(block):
        return lax.dynamic_slice_in_dim(block, here * share, share, 0)

    def split3(v):
        high = v.astype(BF16)
        rest = v - high.astype(F32)
        mid = rest.astype(BF16)
        return [high, mid, (rest - mid.astype(F32)).astype(BF16)]

    bias_row = jnp.concatenate([b_qv[0], b_qv[1], jnp.zeros((own_att.shape[1] - 2 * head_cols,), F32)])
    bias_rows = jnp.stack(split3(bias_row) + split3(up_proj_bias))
    extra = 16
    bias_rows = jnp.pad(bias_rows, ((0, extra - 6), (0, 0)))
    att0, att1, biases = ring.gather(jnp.concatenate([share_of(own_att), bias_rows], axis=0), extra)
    up0, up1, _ = ring.gather(share_of(own_up), 0)
    down0, down1, _ = ring.gather(share_of(own_down), 0)

    def reorder(block):
        return jnp.dot(place.T, block, preferred_element_type=F32).astype(BF16)

    def whole(own, half0, half1):
        return jnp.concatenate([reorder(own)[None], jnp.concatenate([half0, half1], axis=1)], axis=0)

    att_w, up_w, down_w = whole(own_att, att0, att1), whole(own_up, up0, up1), whole(own_down, down0, down1)
    bias_all = jnp.stack([bias_rows] + biases).astype(F32)
    att_bias = bias_all[:, 0] + bias_all[:, 1] + bias_all[:, 2]
    up_bias = bias_all[:, 3] + bias_all[:, 4] + bias_all[:, 5]

    def put(v):
        parts = jnp.concatenate(split3(v), axis=0)
        return sum(jnp.split(jnp.dot(parts, place, preferred_element_type=F32), 3))

    script = lax.dynamic_slice_in_dim(script_ids, across, 1, 0)[0]
    length = lax.dynamic_slice_in_dim(lengths, across, 1, 0)[0]
    added = lax.dynamic_slice_in_dim(script_embed, script, 1, 0)[0].astype(F32)
    gain1, shift1, gain2, shift2, out_bias, down_bias, added = put(
        jnp.stack([norm1_gain, norm1_shift, norm2_gain, norm2_shift, attention_out_bias, down_proj_bias, added])
    )
    own_rows = lax.dynamic_slice_in_dim(patches, across * rows, rows, 0)
    own_out = lax.dynamic_slice_in_dim(out_grad, across * rows, rows, 0)
    out_low = jnp.dot(own_out, place, preferred_element_type=F32).astype(BF16)
    out_rows = out_low.astype(F32)
    stream = jnp.dot(own_rows, place, preferred_element_type=F32) + added[None, :]

    norm_one, normed_one, scale_one = layer_norm(stream, gain1, shift1)
    low_one = norm_one.astype(BF16)
    proj = jnp.einsum("td,sdf->tsf", low_one, att_w[:, :, : 3 * head_cols], preferred_element_type=F32)
    proj = proj.reshape(rows, mp, 3, head_cols)
    zero = jnp.zeros((mp, head_cols), F32)
    qkv_bias = jnp.stack([att_bias[:, :head_cols], zero, att_bias[:, head_cols : 2 * head_cols]], axis=1)
    proj = (proj + qkv_bias[None]).astype(BF16)
    query, keys, values = (proj[:, :, i].reshape(rows, mp * heads, HD) for i in range(3))
    mixed, logsum = attention_forward(query, keys, values, length)
    mixed = mixed.reshape(rows, mp, head_cols)
    out_w = att_w[:, :, 3 * head_cols :]
    attn = jnp.einsum("tsf,sdf->td", mixed, out_w, preferred_element_type=F32)
    middle = stream + (attn + out_bias)
    norm_two, normed_two, scale_two = layer_norm(middle, gain2, shift2)
    low_two = norm_two.astype(BF16)
    pre = jnp.einsum("td,sdf->stf", low_two, up_w, preferred_element_type=F32) + up_bias[:, None, :]
    hidden = jax.nn.gelu(pre).astype(BF16)
    block = middle + (jnp.einsum("stf,sdf->td", hidden, down_w, preferred_element_type=F32) + down_bias)

    def split_features(v):
        return v[:, : width // 2], v[:, width // 2 :]

    def weight_grad(left, right):
        return [jnp.einsum("td,stf->sdf", half, right, preferred_element_type=F32).astype(BF16) for half in split_features(left)]

    grad_down = ring.scatter(*weight_grad(out_low, hidden))
    grad_hidden = jnp.einsum("td,sdf->stf", out_low, down_w, preferred_element_type=F32)
    grad_pre = jax.vjp(jax.nn.gelu, pre)[1](grad_hidden)[0].astype(BF16)
    grad_up = ring.scatter(*weight_grad(low_two, grad_pre))
    up_bias_sum = jnp.sum(grad_pre, axis=1, dtype=F32)
    grad_two = jnp.einsum("stf,sdf->td", grad_pre, up_w, preferred_element_type=F32)
    grad_mid = out_rows + norm_back(grad_two, normed_two, scale_two, gain2)
    low_mid = grad_mid.astype(BF16)
    grad_mixed = jnp.einsum("td,sdf->tsf", low_mid, out_w, preferred_element_type=F32).astype(BF16)
    grads = attention_backward(query, keys, values, length, logsum, grad_mixed.reshape(rows, mp * heads, HD))
    grad_proj = jnp.stack([g.reshape(rows, mp, head_cols) for g in grads], axis=2).reshape(rows, mp, 3 * head_cols)
    both = [
        jnp.concatenate(
            [
                jnp.einsum("td,tsf->sdf", one, grad_proj, preferred_element_type=F32).astype(BF16),
                jnp.einsum("td,tsf->sdf", mid, mixed, preferred_element_type=F32).astype(BF16),
            ],
            axis=2,
        )
        for one, mid in zip(split_features(low_one), split_features(low_mid))
    ]
    grad_att = ring.scatter(*both)
    proj_sum = jnp.sum(grad_proj, axis=0, dtype=F32).reshape(mp, 3, head_cols)
    grad_one = jnp.einsum("tsf,sdf->td", grad_proj, att_w[:, :, : 3 * head_cols], preferred_element_type=F32)
    own_stream = grad_mid + norm_back(grad_one, normed_one, scale_one, gain1)

    kind = (lax.broadcasted_iota(jnp.int32, (kinds, 1), 0) == script).astype(F32)
    rows_of = jnp.concatenate(
        [
            jnp.sum(grad_one * normed_one, axis=0)[None],
            jnp.sum(grad_one, axis=0)[None],
            jnp.sum(low_mid.astype(F32), axis=0)[None],
            jnp.sum(grad_two * normed_two, axis=0)[None],
            jnp.sum(grad_two, axis=0)[None],
            jnp.sum(out_rows, axis=0)[None],
            kind * jnp.sum(own_stream, axis=0)[None],
        ],
        axis=0,
    )
    n_vec = rows_of.shape[0]
    sub = head_cols // dp
    qv = jnp.stack([proj_sum[:, 0], proj_sum[:, 2]], axis=1).reshape(mp * 2, dp, sub)
    qv = jnp.pad(qv, ((0, 0), (0, 0), (0, share - sub))).reshape(mp * 2, width)
    small = jnp.concatenate([rows_of, put(jnp.concatenate([up_bias_sum, qv], axis=0))], axis=0).T
    got = lax.ppermute(small[width // 2 :], "dp", ring.pair)
    held = small[: width // 2]
    for stage in ring.stages[::-1]:
        held = held + got
        half = held.shape[0] // 2
        got, held = lax.ppermute(held[half:], "dp", stage), held[:half]
    held = held + got
    parts = [held] + [lax.ppermute(held, "mp", ring.shift(-s)) for s in range(1, mp)]
    vectors = sum(p[:, :n_vec] for p in parts)
    vectors = lax.dynamic_slice_in_dim(vectors, across * (share // mp), share // mp, 0).T
    up_bias_grad = sum(p[:, n_vec + s] for s, p in enumerate(parts))
    qv_grad = sum(p[:sub, n_vec + mp + 2 * s : n_vec + mp + 2 * s + 2] for s, p in enumerate(parts)).T

    def back(v):
        high = v.astype(BF16)
        low = (v - high.astype(F32)).astype(BF16)
        return jnp.dot(high, place.T, preferred_element_type=F32) + jnp.dot(low, place.T, preferred_element_type=F32)

    return (
        back(block),
        back(own_stream),
        vectors[6:],
        vectors[0],
        vectors[1],
        grad_att[:, : 3 * head_cols].reshape(share, 3, head_cols),
        qv_grad,
        grad_att[:, 3 * head_cols :].T,
        vectors[2],
        vectors[3],
        vectors[4],
        grad_up,
        up_bias_grad,
        grad_down.T,
        vectors[5],
    )


def solution(mesh):
    placed = (
        P("dp", None),
        P("dp"),
        P("dp"),
        P(),
        P(),
        P(),
        P(None, None, "mp"),
        P(None, "mp"),
        P("mp", None),
        P(),
        P(),
        P(),
        P(None, "mp"),
        P("mp"),
        P("mp", None),
        P(),
        P("dp", None),
    )
    return jax.shard_map(
        on_device,
        mesh=mesh,
        in_specs=placed,
        out_specs=(
            P(("dp", "mp"), None),
            P(("dp", "mp"), None),
            P(None, ("dp", "mp")),
            P(("dp", "mp")),
            P(("dp", "mp")),
            P("dp", None, "mp"),
            P(None, ("mp", "dp")),
            P("mp", "dp"),
            P(("dp", "mp")),
            P(("dp", "mp")),
            P(("dp", "mp")),
            P("dp", "mp"),
            P(("mp", "dp")),
            P("mp", "dp"),
            P(("dp", "mp")),
        ),
        check_vma=False,
    )
```

```python
import functools
import types

import numpy as np
import jax
import jax.numpy as jnp
from jax import lax
from jax.experimental import pallas as pl
from jax.experimental.pallas import tpu as pltpu
from jax.sharding import PartitionSpec as P

HD = 64
DP, MP, PAIR = "dp", "mp", "pair"
ALL, STEP, REST, SCALAR = "all", "step", "rest", "scalar"
EPS = 1e-05
MASKED = -1e30
BF16 = jnp.bfloat16
F32 = jnp.float32


LOG2E = 1.4426950408889634
LN2 = 0.6931471805599453


def layer_norm(rows, gain, shift):
    center = rows - jnp.mean(rows, axis=-1, keepdims=True)
    scale = lax.rsqrt(jnp.mean(center * center, axis=-1, keepdims=True) + EPS)
    normalized = center * scale
    return (normalized * gain + shift, normalized, scale)


def norm_back(grad_out, normalized, scale, gain):
    scaled = grad_out * gain
    first_mean = jnp.mean(scaled, axis=-1, keepdims=True)
    second_mean = jnp.mean(scaled * normalized, axis=-1, keepdims=True)
    return scale * (scaled - first_mean - normalized * second_mean)


def mm(a, b):
    return lax.dot_general(a, b, (((1,), (0,)), ((), ())), preferred_element_type=F32)


def mm_t(a, b):
    return lax.dot_general(a, b, (((1,), (1,)), ((), ())), preferred_element_type=F32)


def start_kernel(across, script_ids, rows_in, rows_out, embed, *refs):
    vectors, (place, stream, low_one, low_out, tail) = refs[:6], refs[6:]
    width = rows_in.shape[1]
    kind = lax.broadcasted_iota(jnp.int32, embed.shape, 0) == script_ids[across[0]]
    added = jnp.sum(jnp.where(kind, embed[...].astype(F32), 0.0), axis=0, keepdims=True)
    table = jnp.concatenate([v[...].reshape(1, width) for v in vectors] + [added, jnp.zeros((1, width), F32)], axis=0)
    order = place[...]
    table = sum(mm(piece, order) for piece in split3(table))
    tail[...] = table
    x = mm(rows_in[...], order) + table[6:7]
    stream[...] = x
    low_one[...] = layer_norm(x, table[4:5], table[5:6])[0].astype(BF16)
    low_out[...] = mm(rows_out[...], order).astype(BF16)


def split3(v):
    high = v.astype(BF16)
    rest = v - high.astype(F32)
    mid = rest.astype(BF16)
    return [high, mid, (rest - mid.astype(F32)).astype(BF16)]


def attention_kernel(cols, has_own, across, lengths, one, *refs):
    own, (low, high, bias, proj_out, lse_out, mixed_out) = (refs[0], refs[1:]) if has_own else (None, refs)
    rows = one.shape[0]
    half = one.shape[1] // 2
    heads = cols // HD

    def body(w0, w1):
        a = one[...]
        p = mm(a[:, :half], w0) + mm(a[:, half:], w1) + bias[0]
        p = p.astype(BF16)
        proj_out[0] = p
        dead = jnp.where(lax.broadcasted_iota(jnp.int32, (rows, 1), 0) < lengths[across[0]], 0.0, MASKED)
        ones = jnp.where(lax.broadcasted_iota(jnp.int32, (rows, HD), 1) == 0, 1.0, 0.0).astype(BF16)
        lse_out[0] = jnp.zeros(lse_out.shape[1:], F32)
        outs = []
        for h in range(heads):
            q, k, v = (p[:, i * cols + h * HD : i * cols + (h + 1) * HD] for i in range(3))
            scores = mm_t(k, q) * (0.125 * LOG2E) + dead
            top = jnp.max(scores, axis=0, keepdims=True)
            expo = jnp.exp2(scores - top).astype(BF16)
            both = mm(jnp.concatenate([v, ones], axis=1).T, expo)
            total = both[HD : HD + 1]
            lse_out[0, h : h + 1] = top + jnp.log2(total)
            outs.append((both[:HD] * (1.0 / total)).T.astype(BF16))
        mixed_out[0] = jnp.concatenate(outs, axis=1)

    run(has_own, body, own, low, high, slice(0, 3 * cols))


def run(has_own, body, own, low, high, cols):
    if has_own:
        half = low.shape[1]

        @pl.when(pl.program_id(0) == 0)
        def _():
            body(own[:half, cols], own[half:, cols])

        @pl.when(pl.program_id(0) > 0)
        def _():
            body(low[0, :, cols], high[0, :, cols])

    else:
        body(low[0, :, cols], high[0, :, cols])


def out_kernel(cols, hidden, mixed_a, mixed_b, x, own, low, high, up_own, up_low, up_high, tail, mid_out, two_out, total):
    step = pl.program_id(0)
    half = x.shape[1] // 2
    one, two = slice(3 * cols, None), slice(hidden, None)

    def body(heads, w0, w1, u0, u1):
        split = w0.shape[1]
        total[:, :half] += mm_t(heads[:, :split], w0) + mm_t(heads[:, split:], u0)
        total[:, half:] += mm_t(heads[:, :split], w1) + mm_t(heads[:, split:], u1)

    @pl.when(step == 0)
    def _():
        total[...] = x[...] + tail[0:1]
        body(mixed_a[0], own[:half, one], own[half:, one], up_own[:half, two], up_own[half:, two])

    @pl.when(step > 0)
    def _():
        body(jnp.where(step < 2, mixed_a[0], mixed_b[0]), low[0, :, one], high[0, :, one], up_low[0, :, two], up_high[0, :, two])

    @pl.when(step == pl.num_programs(0) - 1)
    def _():
        mid = total[...]
        mid_out[...] = mid
        two_out[...] = layer_norm(mid, tail[1:2], tail[2:3])[0].astype(BF16)


def feature_grad(left, right, grad0, grad1, at):
    half = grad0.shape[1]
    out = lax.dot_general(left, right, (((0,), (0,)), ((), ())), preferred_element_type=F32).astype(BF16)
    grad0[0, :, at] = out[:half]
    grad1[0, :, at] = out[half:]


def mlp_kernel(last, two, out_low, *refs):
    if last:
        (own, low, high, down_own, down_low, down_high, bias, block_in, two_in, mid, tail), refs = refs[:11], refs[11:]
        grad0, grad1, bias_sum, block_sum, grad_mid_out, low_mid_out, sums, hid, grad_pre, two_sum = refs
    else:
        (low, high, down_low, down_high, bias), refs = refs[:5], refs[5:]
        grad0, grad1, bias_sum, block_sum, two_sum, hid, grad_pre = refs
    step = pl.program_id(0)
    rows, width = two.shape
    half = width // 2
    cols = hid.shape[1]
    c0, c1 = 0.7978845608028654, 0.7978845608028654 * 0.044715

    @pl.when(step == 0)
    def _():
        if last:
            block_sum[...] = block_in[...]
            two_sum[...] = two_in[...]
        else:
            block_sum[...] = jnp.zeros(block_sum.shape, F32)
            two_sum[...] = jnp.zeros(two_sum.shape, F32)

    def body(w0, w1, d0, d1):
        for at in (slice(0, rows // 2), slice(rows // 2, rows)):
            v = mm(two[at, :half], w0) + mm(two[at, half:], w1) + bias[0]
            square = v * v
            t = jnp.tanh(v * (c0 + c1 * square))
            grow = 0.5 + 0.5 * t
            hid[at] = (v * grow).astype(BF16)
            slope = grow + v * (0.5 - 0.5 * t * t) * (c0 + 3 * c1 * square)
            grad_pre[at] = ((mm(out_low[at, :half], d0) + mm(out_low[at, half:], d1)) * slope).astype(BF16)
        hidden, grad = hid[...], grad_pre[...]
        bias_sum[0] = jnp.sum(grad.astype(F32), axis=0, keepdims=True)
        feature_grad(out_low[...], hidden, grad0, grad1, slice(0, cols))
        feature_grad(two[...], grad, grad0, grad1, slice(cols, 2 * cols))
        block_sum[:, :half] += mm_t(hidden, d0)
        block_sum[:, half:] += mm_t(hidden, d1)
        two_sum[:, :half] += mm_t(grad, w0)
        two_sum[:, half:] += mm_t(grad, w1)

    ours = slice(0, cols)
    if last:

        @pl.when(step == 0)
        def _():
            body(own[:half, ours], own[half:, ours], down_own[:half], down_own[half:])

        @pl.when(step > 0)
        def _():
            body(low[0, :, ours], high[0, :, ours], down_low[0], down_high[0])

    else:
        body(low[0, :, ours], high[0, :, ours], down_low[0], down_high[0])

    if last:

        @pl.when(step == pl.num_programs(0) - 1)
        def _():
            grad = two_sum[...]
            _, normalized, scale = layer_norm(mid[...], tail[1:2], tail[2:3])
            rows_out = out_low[...].astype(F32)
            grad_mid = rows_out + norm_back(grad, normalized, scale, tail[1:2])
            low_mid = grad_mid.astype(BF16)
            grad_mid_out[...] = grad_mid
            low_mid_out[...] = low_mid
            sums[0:1] = jnp.sum(low_mid.astype(F32), axis=0, keepdims=True)
            sums[1:2] = jnp.sum(grad * normalized, axis=0, keepdims=True)
            sums[2:3] = jnp.sum(grad, axis=0, keepdims=True)
            sums[3:4] = jnp.sum(rows_out, axis=0, keepdims=True)


def attention_back_kernel(cols, hidden, has_own, across, lengths, one, low_mid, *refs):
    own, up_own, refs = (refs[0], refs[1], refs[2:]) if has_own else (None, None, refs)
    low, high, up_low, up_high, proj, mixed, lse, proj_out, grad0, grad1, sums = refs
    rows = one.shape[0]
    half = one.shape[1] // 2
    heads = cols // HD
    first, second = slice(3 * cols, None), slice(hidden, None)

    def body(w0, w1, u0, u1):
        a = low_mid[...]
        grad_mixed = mm(a[:, :half], jnp.concatenate([w0, u0], axis=1)) + mm(a[:, half:], jnp.concatenate([w1, u1], axis=1))
        grad_mixed = grad_mixed.astype(BF16)
        p = proj[0]
        dead = jnp.where(lax.broadcasted_iota(jnp.int32, (rows, 1), 0) < lengths[across[0]], 0.0, MASKED)
        grads = [[], [], []]
        for h in range(heads):
            q, k, v = (p[:, i * cols + h * HD : i * cols + (h + 1) * HD] for i in range(3))
            out = grad_mixed[:, h * HD : (h + 1) * HD]
            probs = jnp.exp2((mm_t(k, q) * (0.125 * LOG2E) + dead) - lse[0, h : h + 1])
            grad_probs = mm_t(v, out)
            inner = jnp.sum(probs * grad_probs, axis=0, keepdims=True)
            grad_scores = (probs * (grad_probs - inner)).astype(BF16)
            grads[2].append(mm(probs.astype(BF16), out).astype(BF16))
            grads[1].append((mm(grad_scores, q) * 0.125).astype(BF16))
            grads[0].append((mm(k.T, grad_scores) * 0.125).T.astype(BF16))
        grad = jnp.concatenate(grads[0] + grads[1] + grads[2], axis=1)
        proj_out[0] = grad
        sums[0] = jnp.sum(grad.astype(F32), axis=0, keepdims=True)
        for left, right, at in ((one, grad, slice(0, 3 * cols)), (low_mid, mixed[0], slice(3 * cols, 4 * cols))):
            out = lax.dot_general(left[...], right, (((0,), (0,)), ((), ())), preferred_element_type=F32).astype(BF16)
            grad0[0, :, at] = out[:half]
            grad1[0, :, at] = out[half:]

    if has_own:

        @pl.when(pl.program_id(0) == 0)
        def _():
            body(own[:half, first], own[half:, first], up_own[:half, second], up_own[half:, second])

        @pl.when(pl.program_id(0) > 0)
        def _():
            body(low[0, :, first], high[0, :, first], up_low[0, :, second], up_high[0, :, second])

    else:
        body(low[0, :, first], high[0, :, first], up_low[0, :, second], up_high[0, :, second])


def unplace(value, place):
    high = value.astype(BF16)
    low = (value - high.astype(F32)).astype(BF16)
    return mm_t(high, place) + mm_t(low, place)


def first_kernel(cols, grad_a, grad_b, own, low, high, x, grad_mid, place, tail, rows_out, sums, total):
    step = pl.program_id(0)
    half = x.shape[1] // 2

    @pl.when(step == 0)
    def _():
        total[...] = jnp.zeros(total.shape, F32)

    def body(w0, w1):
        grad = jnp.where(step < 2, grad_a[0], grad_b[0])
        total[:, :half] += mm_t(grad, w0)
        total[:, half:] += mm_t(grad, w1)

    run(True, body, own, low, high, slice(0, 3 * cols))

    @pl.when(step == pl.num_programs(0) - 1)
    def _():
        grad = total[...]
        _, normalized, scale = layer_norm(x[...], tail[4:5], tail[5:6])
        stream = grad_mid[...] + norm_back(grad, normalized, scale, tail[4:5])
        sums[0:1] = jnp.sum(grad * normalized, axis=0, keepdims=True)
        sums[1:2] = jnp.sum(grad, axis=0, keepdims=True)
        sums[2:3] = jnp.sum(stream, axis=0, keepdims=True)
        rows_out[...] = unplace(stream, place[...])[: rows_out.shape[0]]


def block_kernel(mid, block_sum, place, tail, rows_out):
    rows_out[...] = unplace(mid[...] + tail[3:4] + block_sum[...], place[...])[: rows_out.shape[0]]


def blocked(kernel, inputs, outputs, scratch, steps, flops, transcendentals=0, at=0):
    def spec(shape, kind):
        if kind == SCALAR:
            return pl.BlockSpec(memory_space=pltpu.SMEM)
        zeros = (0,) * (len(shape) - 1)
        if kind == ALL:
            return pl.BlockSpec(shape, lambda s: (0,) + zeros, pipeline_mode=pl.Buffered(1))
        back = {STEP: 0, REST: 1 - at}.get(kind, kind)
        return pl.BlockSpec((1,) + shape[1:], lambda s: (jnp.clip(s - back, 0, shape[0] - 1),) + zeros)

    arrays = [a for a, _ in inputs]
    nbytes = sum(a.size * a.dtype.itemsize for a in arrays) + sum(int(np.prod(s)) * jnp.dtype(d).itemsize for s, d, _ in outputs)
    return pl.pallas_call(
        kernel,
        grid=(steps,),
        in_specs=[spec(a.shape, k) for a, k in inputs],
        out_specs=[spec(s, k) for s, _, k in outputs],
        out_shape=[jax.ShapeDtypeStruct(s, d) for s, d, _ in outputs],
        scratch_shapes=scratch,
        compiler_params=pltpu.CompilerParams(dimension_semantics=("arbitrary",), vmem_limit_bytes=VMEM_LIMIT),
        cost_estimate=pl.CostEstimate(flops=int(flops), bytes_accessed=nbytes, transcendentals=int(transcendentals)),
    )(*arrays)


CHUNK = 32
VMEM_LIMIT = 20 * 1024 * 1024


class Leaving:
    def __init__(self, bag):
        self._bag = bag

    def __getattr__(self, name):
        return vars(self._bag).pop(name)


class Bag(types.SimpleNamespace):
    @property
    def out(self):
        return Leaving(self)


class Ring:
    def __init__(self, dp, mp):
        self.dp, self.mp = dp, mp
        bits = list(range(1, dp.bit_length() - 1))
        self.orders = (bits, bits[::-1])
        self.stages = [[(i, i ^ (1 << self.orders[i & 1][t])) for i in range(dp)] for t in range(len(bits))]
        cut = (len(self.stages) + 1) // 2
        self.rounds = [self.stages[:cut], self.stages[cut:]]
        self.pair = [(i, i ^ 1) for i in range(dp)]
        self.blocks = [[(i, i ^ (1 << b)) for i in range(mp)] for b in range(mp.bit_length() - 1)][::-1]
        self.block_masks = [0]
        for b in reversed(range(mp.bit_length() - 1)):
            self.block_masks += [m ^ (1 << b) for m in self.block_masks]
        halves = []
        for order in self.orders:
            masks = [0]
            for bit in order:
                masks = masks + [m | (1 << bit) for m in masks]
            halves.append(masks)
        self.masks = np.array([halves[0] + [1 ^ m for m in halves[1]], halves[1] + [1 ^ m for m in halves[0]]], np.int32)


class Gather:
    def __init__(self, ring, piece, share):
        self.share = share
        self.v = Bag(held=piece[None])
        self.left = [(MP, [s]) for s in ring.blocks] + [(DP, g) for g in ring.rounds] + [(PAIR, [ring.pair])]

    def step(self):
        axis, stages = self.left.pop(0)
        if axis == PAIR:
            self.v.high = lax.ppermute(self.v.held, DP, stages[0])
            return
        held = self.v.held
        for stage in stages:
            held = jnp.concatenate([held, lax.ppermute(held, axis, stage)], axis=0 if axis == MP else 1)
        if axis == MP and self.left[0][0] != MP:
            if held.shape[1] > self.share:
                self.v.extra = held[:, self.share :]
            held = held[1:, : self.share]
        self.v.held = held

    def specs(self, own):
        return ([(own, ALL)] if own is not None else []) + [(self.v.held, REST), (self.v.high, REST)]


class Scatter:
    def __init__(self, ring, low_half, high_half):
        self.v = Bag(held=low_half, send=high_half)
        self.axis, self.stage = DP, ring.pair
        self.left = [(DP, 1, group[::-1]) for group in ring.rounds[::-1]]

    def go(self):
        self.v.got = lax.ppermute(self.v.out.send, self.axis, self.stage)

    def add(self, at, size, dim):
        a, b = (lax.slice_in_dim(v, at, at + size, axis=dim).astype(F32) for v in (self.v.held, self.v.got))
        return (a + b).astype(self.v.held.dtype)

    def fold(self):
        self.axis, dim, stages = self.left.pop(0)
        for i, stage in enumerate(stages):
            if i:
                self.go()
            self.stage = stage
            size = self.v.held.shape[dim] // 2
            self.v = Bag(send=self.add(size, size, dim), held=self.add(0, size, dim))

    def settle(self):
        return self.add(0, self.v.held.shape[0], 0)

    def take_rest(self, rest, stage):
        self.v = Bag(held=self.settle(), got=rest)
        self.left = [(MP, 0, [stage])]
        self.fold()

    def total(self):
        return self.v.held[0].astype(F32) + self.v.got[0].astype(F32)


def meet(live, *moving):
    bags = [live] + [m.v for m in moving]
    for bag, values in zip(bags, lax.optimization_barrier([vars(b) for b in bags])):
        vars(bag).update(values)


def on_device(
    patches,
    script_ids,
    lengths,
    script_embed,
    norm1_gain,
    norm1_shift,
    query_key_value_weight,
    b_qv,
    attention_out_weight,
    attention_out_bias,
    norm2_gain,
    norm2_shift,
    up_weight,
    up_proj_bias,
    down_weight,
    down_proj_bias,
    out_grad,
):
    dp, mp = lax.axis_size(DP), lax.axis_size(MP)
    ring = Ring(dp, mp)
    here, across = lax.axis_index(DP), lax.axis_index(MP)
    rows_all, width = patches.shape
    rows = rows_all // mp
    share = width // dp
    head_cols = query_key_value_weight.shape[2]
    hidden_cols = up_weight.shape[1]
    heads = head_cols // HD
    kinds = script_embed.shape[0]

    order = jnp.where((here & 1) == 0, ring.masks[0], ring.masks[1]) ^ here
    source = (order[:, None] * share + jnp.arange(share, dtype=jnp.int32)[None, :]).reshape(width)
    place = (lax.broadcasted_iota(jnp.int32, (width, width), 0) == source[None, :]).astype(BF16)
    mine = (
        lax.broadcasted_iota(jnp.int32, (share, width), 1) == here * share + lax.broadcasted_iota(jnp.int32, (share, width), 0)
    ).astype(BF16)

    def take(rows_of, block, features):
        out = lax.dot_general(rows_of, block, (((1,), (features,)), ((), ())), preferred_element_type=F32)
        return out.astype(BF16)

    def put(v):
        parts = jnp.concatenate(split3(v), axis=0)
        return sum(jnp.split(jnp.dot(parts, place, preferred_element_type=F32), 3))

    qkv_cols = 3 * head_cols
    behind = -qkv_cols % 128
    att_own = query_key_value_weight.reshape(width, qkv_cols)
    out_a, out_b = attention_out_weight[:behind], attention_out_weight[behind:]
    att_cols, up_cols_all = qkv_cols + behind, hidden_cols + head_cols - behind
    zeros = jnp.zeros((head_cols,), F32)
    per_row = hidden_cols // head_cols
    flat = jnp.concatenate([b_qv[0], zeros, b_qv[1], zeros[:behind]] + [
        piece for i in range(per_row) for piece in (up_proj_bias[i * head_cols : (i + 1) * head_cols], jnp.zeros((att_cols - head_cols,), F32))
    ]).reshape(1 + per_row, att_cols)
    bias_rows = jnp.concatenate(split3(flat))
    n_bias = 1 + per_row
    bias_rows = jnp.pad(bias_rows, ((0, -bias_rows.shape[0] % 16), (0, 0)))

    padded = -(-rows // CHUNK) * CHUNK
    grow = ((0, padded - rows), (0, 0))
    real_rows, rows = rows, padded
    vmem = pltpu.VMEM
    dense = 2 * rows * width
    live = 2 * mp * heads * rows * rows * HD
    part = mp // 2
    which = across.reshape(1)

    q = Gather(ring, jnp.concatenate([jnp.concatenate([take(mine, att_own, 0), take(mine, out_a, 1)], axis=1), bias_rows]), share)
    q.step()
    now = Bag(
        up=jnp.concatenate([take(mine, up_weight, 0), take(mine, out_b, 1)], axis=1),
        rows=jnp.pad(lax.dynamic_slice_in_dim(patches, across * real_rows, real_rows, 0), grow),
        cotangent=jnp.pad(lax.dynamic_slice_in_dim(out_grad, across * real_rows, real_rows, 0), grow),
    )
    meet(now, q)
    q.step()
    now.place = place
    now.own_att = jnp.concatenate([take(place.T, att_own, 0), take(place.T, out_a, 1)], axis=1)
    meet(now, q)
    u = Gather(ring, now.out.up, share)
    q.step()
    u.step()
    now.stream, now.one, now.out_low, now.tail = blocked(
        start_kernel,
        [(which, SCALAR), (script_ids, SCALAR), (now.out.rows, ALL), (now.out.cotangent, ALL), (script_embed, ALL)]
        + [(v, ALL) for v in (attention_out_bias, norm2_gain, norm2_shift, down_proj_bias, norm1_gain, norm1_shift)]
        + [(now.place, ALL)],
        [((rows, width), F32, ALL), ((rows, width), BF16, ALL), ((rows, width), BF16, ALL), ((8, width), F32, ALL)],
        [],
        1,
        2 * dense * width,
    )
    meet(now, q, u)
    q.step()
    u.step()
    order_t = now.place.T
    now.own_up = jnp.concatenate([take(order_t, up_weight, 0), take(order_t, out_b, 1)], axis=1)
    bias_all = q.v.out.extra.astype(F32)
    bias_all = bias_all[:, :n_bias] + bias_all[:, n_bias : 2 * n_bias] + bias_all[:, 2 * n_bias : 3 * n_bias]
    now.qkv_bias = bias_all[:, 0:1, :qkv_cols]
    now.up_bias = bias_all[:, 1:, :head_cols].reshape(mp, 1, hidden_cols)
    now.down = take(mine, down_weight, 1)
    meet(now, q, u)
    n = Gather(ring, now.out.down, share)
    q.step()
    u.step()
    n.step()
    now.own_down = take(now.place.T, down_weight, 1)
    meet(now, q, u, n)
    u.step()
    n.step()

    def attention(at, own):
        return blocked(
            functools.partial(attention_kernel, head_cols, at == 0),
            [(which, SCALAR), (lengths, SCALAR), (now.one, ALL)] + q.specs(own) + [(now.qkv_bias, -at)],
            [((part, rows, qkv_cols), BF16, STEP), ((part, 8, rows), F32, STEP), ((part, rows, head_cols), BF16, STEP)],
            [],
            part,
            (dense * mp * qkv_cols + 2 * live) // 2,
            mp * heads * rows * rows // 2,
            at=at,
        )

    now.proj_b, now.lse_b, now.mixed_b = attention(part, None)
    now.proj_a, now.lse_a, now.mixed_a = attention(0, now.own_att)
    meet(now, q, u, n)
    u.step()
    n.step()
    meet(now, q, u, n)
    n.step()
    now.middle, now.two = blocked(
        functools.partial(out_kernel, head_cols, hidden_cols),
        [(now.mixed_a, STEP), (now.mixed_b, part), (now.stream, ALL)]
        + q.specs(now.own_att) + u.specs(now.own_up) + [(now.tail, ALL)],
        [((rows, width), F32, ALL), ((rows, width), BF16, ALL)],
        [vmem((rows, width), F32)],
        mp,
        dense * mp * head_cols,
    )
    meet(now, q, u, n)
    n.step()
    meet(now, q, u, n)

    def half_shape(cols):
        return ((part, width // 2, cols), BF16, STEP)

    def mlp(at, own_up, own_down, more, outputs, scratch):
        return blocked(
            functools.partial(mlp_kernel, at == 0),
            [(now.two, ALL), (now.out_low, ALL)] + u.specs(own_up) + n.specs(own_down) + [(now.up_bias, -at)] + more,
            [half_shape(2 * hidden_cols), half_shape(2 * hidden_cols), ((part, 1, hidden_cols), F32, STEP), ((rows, width), F32, ALL)] + outputs,
            [vmem((rows, hidden_cols), BF16), vmem((rows, hidden_cols), BF16)] + scratch,
            part,
            6 * dense * part * hidden_cols,
            rows * part * hidden_cols,
            at=at,
        )

    low_half, high_half, now.up_sum_b, now.block, now.two_sum = mlp(part, None, None, [], [((rows, width), F32, ALL)], [])
    mb = Scatter(ring, low_half, high_half)
    meet(now, q, u, n, mb)
    mb.go()
    low_half, high_half, now.up_sum_a, now.block, now.grad_mid, now.mid, now.mid_sums = mlp(
        0,
        now.own_up,
        now.out.own_down,
        [(now.block, ALL), (now.out.two_sum, ALL), (now.middle, ALL), (now.tail, ALL)],
        [((rows, width), F32, ALL), ((rows, width), BF16, ALL), ((8, width), F32, ALL)],
        [vmem((rows, width), F32)],
    )
    ma = Scatter(ring, low_half, high_half)
    meet(now, q, u, mb, ma)
    mb.fold()
    mb.go()
    ma.go()

    def attention_back(at, own, made):
        own_att, own_up = own
        q_specs, u_specs = q.specs(own_att), u.specs(own_up)
        weights = q_specs[:1] + u_specs[:1] + q_specs[1:] + u_specs[1:] if at == 0 else q_specs + u_specs
        return blocked(
            functools.partial(attention_back_kernel, head_cols, hidden_cols, at == 0),
            [(which, SCALAR), (lengths, SCALAR), (now.one, ALL), (now.mid, ALL)] + weights
            + [(a, STEP) for a in made],
            [((part, rows, qkv_cols), BF16, STEP), half_shape(4 * head_cols), half_shape(4 * head_cols), ((part, 1, qkv_cols), F32, STEP)],
            [],
            part,
            (dense * mp * 5 * head_cols + 5 * live) // 2,
            mp * heads * rows * rows // 2,
            at=at,
        )

    now.grad_b, low_half, high_half, now.proj_sum_b = attention_back(part, (None, None), (now.out.proj_b, now.out.mixed_b, now.out.lse_b))
    ab = Scatter(ring, low_half, high_half)
    meet(now, q, u, mb, ma, ab)
    for each in (ma, mb):
        each.fold()
        each.go()
    ab.go()
    now.grad_a, low_half, high_half, now.proj_sum_a = attention_back(0, (now.own_att, now.out.own_up), (now.out.proj_a, now.out.mixed_a, now.out.lse_a))
    aa = Scatter(ring, low_half, high_half)
    meet(now, q, mb, ma, ab, aa)
    aa.go()
    ab.fold()
    ab.go()
    ma.fold()
    ma.go()
    rest_m = lax.ppermute(mb.settle(), MP, ring.blocks[-1])
    meet(now, q, aa)
    aa.fold()
    aa.go()
    now.stream_grad, now.first_sums = blocked(
        functools.partial(first_kernel, head_cols),
        [(now.out.grad_a, STEP), (now.out.grad_b, part)] + q.specs(now.out.own_att)
        + [(a, ALL) for a in (now.stream, now.grad_mid, now.place, now.tail)],
        [((real_rows, width), F32, ALL), ((8, width), F32, ALL)],
        [vmem((rows, width), F32)],
        mp,
        dense * mp * qkv_cols,
    )
    now.rest_m = rest_m
    meet(now, ab, aa, ma)
    for each in (aa, ab):
        each.fold()
        each.go()
    ma.take_rest(now.out.rest_m, ring.blocks[0])
    ma.go()

    script = lax.dynamic_slice_in_dim(script_ids, across, 1, 0)[0]
    kind = (lax.broadcasted_iota(jnp.int32, (kinds, 1), 0) == script).astype(F32)
    first_sums = now.first_sums
    rows_of = jnp.concatenate([first_sums[0:2], now.mid_sums[0:4], kind * first_sums[2:3]], axis=0)
    n_vec = rows_of.shape[0]
    sub = head_cols // dp
    proj_sum = jnp.concatenate([now.proj_sum_a, now.proj_sum_b]).reshape(mp, 3, head_cols)
    qv = jnp.stack([proj_sum[:, 0], proj_sum[:, 2]], axis=1).reshape(mp * 2, dp, sub)
    qv = jnp.pad(qv, ((0, 0), (0, 0), (0, share - sub))).reshape(mp * 2, width)
    up_sum = jnp.concatenate([now.up_sum_a, now.up_sum_b])[:, 0]
    parts = jnp.concatenate(split3(jnp.concatenate([up_sum, qv], axis=0)), axis=0)
    cols = sum(jnp.split(jnp.dot(parts, now.place, preferred_element_type=F32), 3))
    small = jnp.concatenate([rows_of, cols], axis=0).T[None]
    ss = Scatter(ring, small[:, : width // 2], small[:, width // 2 :])
    ss.go()
    ss.fold()
    ss.go()
    (block,) = blocked(
        block_kernel,
        [(now.middle, ALL), (now.block, ALL), (now.place, ALL), (now.tail, ALL)],
        [((real_rows, width), F32, ALL)],
        [],
        1,
        2 * dense * width,
    )
    now = Bag(block=block, stream_grad=now.stream_grad)
    meet(now, aa, ab, ss)
    rest_a = lax.ppermute(ab.settle(), MP, ring.blocks[-1])
    while ss.left:
        ss.fold()
        ss.go()
    sums = ss.settle()
    sums = jnp.concatenate([sums, lax.ppermute(sums, MP, ring.blocks[0])], axis=0)
    now.rest_a, now.sums = rest_a, sums
    meet(now, aa, ma)
    aa.take_rest(now.rest_a, ring.blocks[0])
    aa.go()
    sums = now.sums
    parts = jnp.concatenate([sums, lax.ppermute(sums, MP, ring.blocks[1])], axis=0)
    vectors = sum(p[:, :n_vec] for p in parts)
    vectors = lax.dynamic_slice_in_dim(vectors, across * (share // mp), share // mp, 0).T
    up_bias_grad = sum(p[:, n_vec + s] for s, p in enumerate(parts))
    qv_grad = sum(p[:sub, n_vec + mp + 2 * s : n_vec + mp + 2 * s + 2] for s, p in enumerate(parts)).T
    mlp_total = ma.total()
    grad_down, grad_up = mlp_total[:, :hidden_cols], mlp_total[:, hidden_cols:]
    grad_att = aa.total()
    block, stream_grad = now.block, now.stream_grad

    return (
        block,
        stream_grad,
        vectors[6:],
        vectors[0],
        vectors[1],
        grad_att[:, : 3 * head_cols].reshape(share, 3, head_cols),
        qv_grad,
        grad_att[:, 3 * head_cols :].T,
        vectors[2],
        vectors[3],
        vectors[4],
        grad_up,
        up_bias_grad,
        grad_down.T,
        vectors[5],
    )


def solution(mesh):
    placed = (
        P(DP, None),
        P(DP),
        P(DP),
        P(),
        P(),
        P(),
        P(None, None, MP),
        P(None, MP),
        P(MP, None),
        P(),
        P(),
        P(),
        P(None, MP),
        P(MP),
        P(MP, None),
        P(),
        P(DP, None),
    )
    return jax.shard_map(
        on_device,
        mesh=mesh,
        in_specs=placed,
        out_specs=(
            P((DP, MP), None),
            P((DP, MP), None),
            P(None, (DP, MP)),
            P((DP, MP)),
            P((DP, MP)),
            P(DP, None, MP),
            P(None, (MP, DP)),
            P(MP, DP),
            P((DP, MP)),
            P((DP, MP)),
            P((DP, MP)),
            P(DP, MP),
            P((MP, DP)),
            P(MP, DP),
            P((DP, MP)),
        ),
        check_vma=False,
    )
```

```python
import functools
import types

import numpy as np
import jax
import jax.numpy as jnp
from jax import lax
from jax.experimental import pallas as pl
from jax.experimental.pallas import tpu as pltpu
from jax.sharding import PartitionSpec as P

HD = 64
DP, MP, PAIR = "dp", "mp", "pair"
ALL, STEP, REST, SCALAR = "all", "step", "rest", "scalar"
EPS = 1e-05
MASKED = -1e30
BF16 = jnp.bfloat16
F32 = jnp.float32


LOG2E = 1.4426950408889634
LN2 = 0.6931471805599453


def layer_norm(rows, gain, shift):
    center = rows - jnp.mean(rows, axis=-1, keepdims=True)
    scale = lax.rsqrt(jnp.mean(center * center, axis=-1, keepdims=True) + EPS)
    normalized = center * scale
    return (normalized * gain + shift, normalized, scale)


def norm_back(grad_out, normalized, scale, gain):
    scaled = grad_out * gain
    first_mean = jnp.mean(scaled, axis=-1, keepdims=True)
    second_mean = jnp.mean(scaled * normalized, axis=-1, keepdims=True)
    return scale * (scaled - first_mean - normalized * second_mean)


def mm(a, b):
    return lax.dot_general(a, b, (((1,), (0,)), ((), ())), preferred_element_type=F32)


def mm_t(a, b):
    return lax.dot_general(a, b, (((1,), (1,)), ((), ())), preferred_element_type=F32)


def start_kernel(across, script_ids, rows_in, rows_out, embed, *refs):
    vectors, (place, stream, low_one, low_out, tail) = refs[:6], refs[6:]
    width = rows_in.shape[1]
    kind = lax.broadcasted_iota(jnp.int32, embed.shape, 0) == script_ids[across[0]]
    added = jnp.sum(jnp.where(kind, embed[...].astype(F32), 0.0), axis=0, keepdims=True)
    table = jnp.concatenate([v[...].reshape(1, width) for v in vectors] + [added, jnp.zeros((1, width), F32)], axis=0)
    order = place[...]
    table = sum(mm(piece, order) for piece in split3(table))
    tail[...] = table
    x = mm(rows_in[...], order) + table[6:7]
    stream[...] = x
    low_one[...] = layer_norm(x, table[4:5], table[5:6])[0].astype(BF16)
    low_out[...] = mm(rows_out[...], order).astype(BF16)


def split3(v):
    high = v.astype(BF16)
    rest = v - high.astype(F32)
    mid = rest.astype(BF16)
    return [high, mid, (rest - mid.astype(F32)).astype(BF16)]


def attention_kernel(cols, has_own, across, lengths, one, *refs):
    own, (low, high, bias, proj_out, lse_out, mixed_out) = (refs[0], refs[1:]) if has_own else (None, refs)
    rows = one.shape[0]
    half = one.shape[1] // 2
    heads = cols // HD

    def body(w0, w1):
        a = one[...]
        p = mm(a[:, :half], w0) + mm(a[:, half:], w1) + bias[0]
        p = p.astype(BF16)
        proj_out[0] = p
        dead = jnp.where(lax.broadcasted_iota(jnp.int32, (rows, 1), 0) < lengths[across[0]], 0.0, MASKED)
        ones = jnp.where(lax.broadcasted_iota(jnp.int32, (rows, HD), 1) == 0, 1.0, 0.0).astype(BF16)
        lse_out[0] = jnp.zeros(lse_out.shape[1:], F32)
        outs = []
        for h in range(heads):
            q, k, v = (p[:, i * cols + h * HD : i * cols + (h + 1) * HD] for i in range(3))
            scores = mm_t(k, q) * (0.125 * LOG2E) + dead
            top = jnp.max(scores, axis=0, keepdims=True)
            expo = jnp.exp2(scores - top).astype(BF16)
            both = mm(jnp.concatenate([v, ones], axis=1).T, expo)
            total = both[HD : HD + 1]
            lse_out[0, h : h + 1] = top + jnp.log2(total)
            outs.append((both[:HD] * (1.0 / total)).T.astype(BF16))
        mixed_out[0] = jnp.concatenate(outs, axis=1)

    run(has_own, body, own, low, high, slice(0, 3 * cols))


def run(has_own, body, own, low, high, cols):
    if has_own:
        half = low.shape[1]

        @pl.when(pl.program_id(0) == 0)
        def _():
            body(own[:half, cols], own[half:, cols])

        @pl.when(pl.program_id(0) > 0)
        def _():
            body(low[0, :, cols], high[0, :, cols])

    else:
        body(low[0, :, cols], high[0, :, cols])


def out_kernel(cols, hidden, mixed_a, mixed_b, x, own, low, high, up_own, up_low, up_high, tail, mid_out, two_out, total):
    step = pl.program_id(0)
    half = x.shape[1] // 2
    one, two = slice(3 * cols, None), slice(hidden, None)

    def body(heads, w0, w1, u0, u1):
        split = w0.shape[1]
        total[:, :half] += mm_t(heads[:, :split], w0) + mm_t(heads[:, split:], u0)
        total[:, half:] += mm_t(heads[:, :split], w1) + mm_t(heads[:, split:], u1)

    @pl.when(step == 0)
    def _():
        total[...] = x[...] + tail[0:1]
        body(mixed_a[0], own[:half, one], own[half:, one], up_own[:half, two], up_own[half:, two])

    @pl.when(step > 0)
    def _():
        body(jnp.where(step < 2, mixed_a[0], mixed_b[0]), low[0, :, one], high[0, :, one], up_low[0, :, two], up_high[0, :, two])

    @pl.when(step == pl.num_programs(0) - 1)
    def _():
        mid = total[...]
        mid_out[...] = mid
        two_out[...] = layer_norm(mid, tail[1:2], tail[2:3])[0].astype(BF16)


def feature_grad(left, right, grad0, grad1, at):
    half = grad0.shape[1]
    out = lax.dot_general(left, right, (((0,), (0,)), ((), ())), preferred_element_type=F32).astype(BF16)
    grad0[0, :, at] = out[:half]
    grad1[0, :, at] = out[half:]


def up_kernel(has_own, two, out_low, *refs):
    own, (low, high, bias, hidden_out, slope_out, grad0, grad1) = (refs[0], refs[1:]) if has_own else (None, refs)
    rows, width = two.shape
    half = width // 2
    cols = hidden_out.shape[2]
    c0, c1 = 0.7978845608028654, 0.7978845608028654 * 0.044715

    def body(w0, w1):
        for at in (slice(0, rows // 2), slice(rows // 2, rows)):
            v = mm(two[at, :half], w0) + mm(two[at, half:], w1) + bias[0]
            square = v * v
            t = jnp.tanh(v * (c0 + c1 * square))
            grow = 0.5 + 0.5 * t
            hidden_out[0, at] = (v * grow).astype(BF16)
            slope_out[0, at] = (grow + v * (0.5 - 0.5 * t * t) * (c0 + 3 * c1 * square)).astype(BF16)
        feature_grad(out_low[...], hidden_out[0], grad0, grad1, slice(0, cols))

    run(has_own, body, own, low, high, slice(0, cols))


def pre_kernel(last, two, out_low, *refs):
    if last:
        (own, low, high, down_own, down_low, down_high, slope, two_in, mid, tail), refs = refs[:10], refs[10:]
        grad0, grad1, bias_sum, grad_mid_out, low_mid_out, sums, two_sum = refs
    else:
        low, high, down_low, down_high, slope, grad0, grad1, bias_sum, two_sum = refs
    step = pl.program_id(0)
    half = two.shape[1] // 2
    cols = slope.shape[2]
    ours = slice(0, cols)

    @pl.when(step == 0)
    def _():
        two_sum[...] = two_in[...] if last else jnp.zeros(two_sum.shape, F32)

    def body(w0, w1, d0, d1):
        a = out_low[...]
        grad = ((mm(a[:, :half], d0) + mm(a[:, half:], d1)) * slope[0].astype(F32)).astype(BF16)
        bias_sum[0] = jnp.sum(grad.astype(F32), axis=0, keepdims=True)
        feature_grad(two[...], grad, grad0, grad1, ours)
        two_sum[:, :half] += mm_t(grad, w0)
        two_sum[:, half:] += mm_t(grad, w1)

    if last:

        @pl.when(step == 0)
        def _():
            body(own[:half, ours], own[half:, ours], down_own[:half], down_own[half:])

        @pl.when(step > 0)
        def _():
            body(low[0, :, ours], high[0, :, ours], down_low[0], down_high[0])

        @pl.when(step == pl.num_programs(0) - 1)
        def _():
            grad = two_sum[...]
            _, normalized, scale = layer_norm(mid[...], tail[1:2], tail[2:3])
            rows_out = out_low[...].astype(F32)
            grad_mid = rows_out + norm_back(grad, normalized, scale, tail[1:2])
            low_mid = grad_mid.astype(BF16)
            grad_mid_out[...] = grad_mid
            low_mid_out[...] = low_mid
            sums[0:1] = jnp.sum(low_mid.astype(F32), axis=0, keepdims=True)
            sums[1:2] = jnp.sum(grad * normalized, axis=0, keepdims=True)
            sums[2:3] = jnp.sum(grad, axis=0, keepdims=True)
            sums[3:4] = jnp.sum(rows_out, axis=0, keepdims=True)

    else:
        body(low[0, :, ours], high[0, :, ours], down_low[0], down_high[0])


def attention_back_kernel(cols, hidden, has_own, across, lengths, one, low_mid, *refs):
    own, up_own, refs = (refs[0], refs[1], refs[2:]) if has_own else (None, None, refs)
    low, high, up_low, up_high, proj, mixed, lse, proj_out, grad0, grad1, sums = refs
    rows = one.shape[0]
    half = one.shape[1] // 2
    heads = cols // HD
    first, second = slice(3 * cols, None), slice(hidden, None)

    def body(w0, w1, u0, u1):
        a = low_mid[...]
        grad_mixed = mm(a[:, :half], jnp.concatenate([w0, u0], axis=1)) + mm(a[:, half:], jnp.concatenate([w1, u1], axis=1))
        grad_mixed = grad_mixed.astype(BF16)
        p = proj[0]
        dead = jnp.where(lax.broadcasted_iota(jnp.int32, (rows, 1), 0) < lengths[across[0]], 0.0, MASKED)
        grads = [[], [], []]
        for h in range(heads):
            q, k, v = (p[:, i * cols + h * HD : i * cols + (h + 1) * HD] for i in range(3))
            out = grad_mixed[:, h * HD : (h + 1) * HD]
            probs = jnp.exp2((mm_t(k, q) * (0.125 * LOG2E) + dead) - lse[0, h : h + 1])
            grad_probs = mm_t(v, out)
            inner = jnp.sum(probs * grad_probs, axis=0, keepdims=True)
            grad_scores = (probs * (grad_probs - inner)).astype(BF16)
            grads[2].append(mm(probs.astype(BF16), out).astype(BF16))
            grads[1].append((mm(grad_scores, q) * 0.125).astype(BF16))
            grads[0].append((mm(k.T, grad_scores) * 0.125).T.astype(BF16))
        grad = jnp.concatenate(grads[0] + grads[1] + grads[2], axis=1)
        proj_out[0] = grad
        sums[0] = jnp.sum(grad.astype(F32), axis=0, keepdims=True)
        for left, right, at in ((one, grad, slice(0, 3 * cols)), (low_mid, mixed[0], slice(3 * cols, 4 * cols))):
            out = lax.dot_general(left[...], right, (((0,), (0,)), ((), ())), preferred_element_type=F32).astype(BF16)
            grad0[0, :, at] = out[:half]
            grad1[0, :, at] = out[half:]

    if has_own:

        @pl.when(pl.program_id(0) == 0)
        def _():
            body(own[:half, first], own[half:, first], up_own[:half, second], up_own[half:, second])

        @pl.when(pl.program_id(0) > 0)
        def _():
            body(low[0, :, first], high[0, :, first], up_low[0, :, second], up_high[0, :, second])

    else:
        body(low[0, :, first], high[0, :, first], up_low[0, :, second], up_high[0, :, second])


def unplace(value, place):
    high = value.astype(BF16)
    low = (value - high.astype(F32)).astype(BF16)
    return mm_t(high, place) + mm_t(low, place)


def first_kernel(cols, grad_a, grad_b, own, low, high, x, grad_mid, place, tail, rows_out, sums, total):
    step = pl.program_id(0)
    half = x.shape[1] // 2

    @pl.when(step == 0)
    def _():
        total[...] = jnp.zeros(total.shape, F32)

    def body(w0, w1):
        grad = jnp.where(step < 2, grad_a[0], grad_b[0])
        total[:, :half] += mm_t(grad, w0)
        total[:, half:] += mm_t(grad, w1)

    run(True, body, own, low, high, slice(0, 3 * cols))

    @pl.when(step == pl.num_programs(0) - 1)
    def _():
        grad = total[...]
        _, normalized, scale = layer_norm(x[...], tail[4:5], tail[5:6])
        stream = grad_mid[...] + norm_back(grad, normalized, scale, tail[4:5])
        sums[0:1] = jnp.sum(grad * normalized, axis=0, keepdims=True)
        sums[1:2] = jnp.sum(grad, axis=0, keepdims=True)
        sums[2:3] = jnp.sum(stream, axis=0, keepdims=True)
        rows_out[...] = unplace(stream, place[...])[: rows_out.shape[0]]


def block_kernel(hidden_a, hidden_b, own, low, high, mid, place, tail, rows_out, total):
    step = pl.program_id(0)
    half = mid.shape[1] // 2

    @pl.when(step == 0)
    def _():
        total[...] = mid[...] + tail[3:4]

    def body(w0, w1):
        hidden = jnp.where(step < 2, hidden_a[0], hidden_b[0])
        total[:, :half] += mm_t(hidden, w0)
        total[:, half:] += mm_t(hidden, w1)

    run(True, body, own, low, high, slice(None))

    @pl.when(step == pl.num_programs(0) - 1)
    def _():
        rows_out[...] = unplace(total[...], place[...])[: rows_out.shape[0]]


def blocked(kernel, inputs, outputs, scratch, steps, flops, transcendentals=0, at=0, vmem=20):
    def spec(shape, kind):
        if kind == SCALAR:
            return pl.BlockSpec(memory_space=pltpu.SMEM)
        zeros = (0,) * (len(shape) - 1)
        if kind == ALL:
            return pl.BlockSpec(shape, lambda s: (0,) + zeros, pipeline_mode=pl.Buffered(1))
        back = {STEP: 0, REST: 1 - at}.get(kind, kind)
        return pl.BlockSpec((1,) + shape[1:], lambda s: (jnp.clip(s - back, 0, shape[0] - 1),) + zeros)

    arrays = [a for a, _ in inputs]
    nbytes = sum(a.size * a.dtype.itemsize for a in arrays) + sum(int(np.prod(s)) * jnp.dtype(d).itemsize for s, d, _ in outputs)
    return pl.pallas_call(
        kernel,
        grid=(steps,),
        in_specs=[spec(a.shape, k) for a, k in inputs],
        out_specs=[spec(s, k) for s, _, k in outputs],
        out_shape=[jax.ShapeDtypeStruct(s, d) for s, d, _ in outputs],
        scratch_shapes=scratch,
        compiler_params=pltpu.CompilerParams(dimension_semantics=("arbitrary",), vmem_limit_bytes=vmem * 1024 * 1024),
        cost_estimate=pl.CostEstimate(flops=int(flops), bytes_accessed=nbytes, transcendentals=int(transcendentals)),
    )(*arrays)


CHUNK = 32


class Leaving:
    def __init__(self, bag):
        self._bag = bag

    def __getattr__(self, name):
        return vars(self._bag).pop(name)


class Bag(types.SimpleNamespace):
    @property
    def out(self):
        return Leaving(self)


class Ring:
    def __init__(self, dp, mp):
        self.dp, self.mp = dp, mp
        bits = list(range(1, dp.bit_length() - 1))
        self.orders = (bits, bits[::-1])
        self.stages = [[(i, i ^ (1 << self.orders[i & 1][t])) for i in range(dp)] for t in range(len(bits))]
        cut = (len(self.stages) + 1) // 2
        self.rounds = [self.stages[:cut], self.stages[cut:]]
        self.pair = [(i, i ^ 1) for i in range(dp)]
        self.blocks = [[(i, i ^ (1 << b)) for i in range(mp)] for b in range(mp.bit_length() - 1)][::-1]
        self.block_masks = [0]
        for b in reversed(range(mp.bit_length() - 1)):
            self.block_masks += [m ^ (1 << b) for m in self.block_masks]
        halves = []
        for order in self.orders:
            masks = [0]
            for bit in order:
                masks = masks + [m | (1 << bit) for m in masks]
            halves.append(masks)
        self.masks = np.array([halves[0] + [1 ^ m for m in halves[1]], halves[1] + [1 ^ m for m in halves[0]]], np.int32)


class Gather:
    def __init__(self, ring, piece, share):
        self.share = share
        self.v = Bag(held=piece[None])
        self.left = [(MP, [s]) for s in ring.blocks] + [(DP, g) for g in ring.rounds] + [(PAIR, [ring.pair])]

    def step(self):
        axis, stages = self.left.pop(0)
        if axis == PAIR:
            self.v.high = lax.ppermute(self.v.held, DP, stages[0])
            return
        held = self.v.held
        for stage in stages:
            held = jnp.concatenate([held, lax.ppermute(held, axis, stage)], axis=0 if axis == MP else 1)
        if axis == MP and self.left[0][0] != MP:
            if held.shape[1] > self.share:
                self.v.extra = held[:, self.share :]
            held = held[1:, : self.share]
        self.v.held = held

    def specs(self, own):
        return ([(own, ALL)] if own is not None else []) + [(self.v.held, REST), (self.v.high, REST)]


class Scatter:
    def __init__(self, ring, low_half, high_half):
        self.v = Bag(held=low_half, send=high_half)
        self.axis, self.stage = DP, ring.pair
        self.left = [(DP, 1, group[::-1]) for group in ring.rounds[::-1]]

    def go(self):
        self.v.got = lax.ppermute(self.v.out.send, self.axis, self.stage)

    def add(self, at, size, dim):
        a, b = (lax.slice_in_dim(v, at, at + size, axis=dim).astype(F32) for v in (self.v.held, self.v.got))
        return (a + b).astype(self.v.held.dtype)

    def fold(self):
        self.axis, dim, stages = self.left.pop(0)
        for i, stage in enumerate(stages):
            if i:
                self.go()
            self.stage = stage
            size = self.v.held.shape[dim] // 2
            self.v = Bag(send=self.add(size, size, dim), held=self.add(0, size, dim))

    def settle(self):
        return self.add(0, self.v.held.shape[0], 0)

    def take_rest(self, rest, stage):
        self.v = Bag(held=self.settle(), got=rest)
        self.left = [(MP, 0, [stage])]
        self.fold()

    def join(self, other, blocks):
        self.v = Bag(held=jnp.concatenate([self.v.held, other.v.held]), got=jnp.concatenate([self.v.got, other.v.got]))
        self.left += [(MP, 0, [stage]) for stage in blocks[::-1]]

    def total(self):
        return self.v.held[0].astype(F32) + self.v.got[0].astype(F32)


def meet(live, *moving):
    bags = [live] + [m.v for m in moving]
    for bag, values in zip(bags, lax.optimization_barrier([vars(b) for b in bags])):
        vars(bag).update(values)


def on_device(
    patches,
    script_ids,
    lengths,
    script_embed,
    norm1_gain,
    norm1_shift,
    query_key_value_weight,
    b_qv,
    attention_out_weight,
    attention_out_bias,
    norm2_gain,
    norm2_shift,
    up_weight,
    up_proj_bias,
    down_weight,
    down_proj_bias,
    out_grad,
):
    dp, mp = lax.axis_size(DP), lax.axis_size(MP)
    ring = Ring(dp, mp)
    here, across = lax.axis_index(DP), lax.axis_index(MP)
    rows_all, width = patches.shape
    rows = rows_all // mp
    share = width // dp
    head_cols = query_key_value_weight.shape[2]
    hidden_cols = up_weight.shape[1]
    heads = head_cols // HD
    kinds = script_embed.shape[0]

    order = jnp.where((here & 1) == 0, ring.masks[0], ring.masks[1]) ^ here
    source = (order[:, None] * share + jnp.arange(share, dtype=jnp.int32)[None, :]).reshape(width)
    place = (lax.broadcasted_iota(jnp.int32, (width, width), 0) == source[None, :]).astype(BF16)
    mine = (
        lax.broadcasted_iota(jnp.int32, (share, width), 1) == here * share + lax.broadcasted_iota(jnp.int32, (share, width), 0)
    ).astype(BF16)

    def take(rows_of, block, features):
        out = lax.dot_general(rows_of, block, (((1,), (features,)), ((), ())), preferred_element_type=F32)
        return out.astype(BF16)

    def put(v):
        parts = jnp.concatenate(split3(v), axis=0)
        return sum(jnp.split(jnp.dot(parts, place, preferred_element_type=F32), 3))

    qkv_cols = 3 * head_cols
    behind = -qkv_cols % 128
    att_own = query_key_value_weight.reshape(width, qkv_cols)
    out_a, out_b = attention_out_weight[:behind], attention_out_weight[behind:]
    att_cols, up_cols_all = qkv_cols + behind, hidden_cols + head_cols - behind
    zeros = jnp.zeros((head_cols,), F32)
    per_row = hidden_cols // head_cols
    flat = jnp.concatenate([b_qv[0], zeros, b_qv[1], zeros[:behind]] + [
        piece for i in range(per_row) for piece in (up_proj_bias[i * head_cols : (i + 1) * head_cols], jnp.zeros((att_cols - head_cols,), F32))
    ]).reshape(1 + per_row, att_cols)
    bias_rows = jnp.concatenate(split3(flat))
    n_bias = 1 + per_row
    bias_rows = jnp.pad(bias_rows, ((0, -bias_rows.shape[0] % 16), (0, 0)))

    padded = -(-rows // CHUNK) * CHUNK
    grow = ((0, padded - rows), (0, 0))
    real_rows, rows = rows, padded
    vmem = pltpu.VMEM
    dense = 2 * rows * width
    live = 2 * mp * heads * rows * rows * HD
    part = mp // 2
    which = across.reshape(1)

    q = Gather(ring, jnp.concatenate([jnp.concatenate([take(mine, att_own, 0), take(mine, out_a, 1)], axis=1), bias_rows]), share)
    q.step()
    now = Bag(up=jnp.concatenate([take(mine, up_weight, 0), take(mine, out_b, 1)], axis=1))
    meet(now, q)
    u = Gather(ring, now.out.up, share)
    q.step()
    u.step()
    now.rows = jnp.pad(lax.dynamic_slice_in_dim(patches, across * real_rows, real_rows, 0), grow)
    now.cotangent = jnp.pad(lax.dynamic_slice_in_dim(out_grad, across * real_rows, real_rows, 0), grow)
    now.place = place
    meet(now, q, u)
    q.step()
    u.step()
    now.down = take(mine, down_weight, 1)
    now.stream, now.one, now.out_low, now.tail = blocked(
        start_kernel,
        [(which, SCALAR), (script_ids, SCALAR), (now.out.rows, ALL), (now.out.cotangent, ALL), (script_embed, ALL)]
        + [(v, ALL) for v in (attention_out_bias, norm2_gain, norm2_shift, down_proj_bias, norm1_gain, norm1_shift)]
        + [(now.place, ALL)],
        [((rows, width), F32, ALL), ((rows, width), BF16, ALL), ((rows, width), BF16, ALL), ((8, width), F32, ALL)],
        [],
        1,
        2 * dense * width,
    )
    meet(now, q, u)
    n = Gather(ring, now.out.down, share)
    q.step()
    n.step()
    now.own_att = jnp.concatenate([take(now.place.T, att_own, 0), take(now.place.T, out_a, 1)], axis=1)
    bias_all = q.v.out.extra.astype(F32)
    bias_all = bias_all[:, :n_bias] + bias_all[:, n_bias : 2 * n_bias] + bias_all[:, 2 * n_bias : 3 * n_bias]
    now.qkv_bias = bias_all[:, 0:1, :qkv_cols]
    now.up_bias = bias_all[:, 1:, :head_cols].reshape(mp, 1, hidden_cols)
    meet(now, q, u, n)
    q.step()
    u.step()
    n.step()
    order_t = now.place.T
    now.own_up = jnp.concatenate([take(order_t, up_weight, 0), take(order_t, out_b, 1)], axis=1)
    meet(now, q, u, n)
    u.step()

    def attention(at, own):
        return blocked(
            functools.partial(attention_kernel, head_cols, at == 0),
            [(which, SCALAR), (lengths, SCALAR), (now.one, ALL)] + q.specs(own) + [(now.qkv_bias, -at)],
            [((part, rows, qkv_cols), BF16, STEP), ((part, 8, rows), F32, STEP), ((part, rows, head_cols), BF16, STEP)],
            [],
            part,
            (dense * mp * qkv_cols + 2 * live) // 2,
            mp * heads * rows * rows // 2,
            at=at,
        )

    now.proj_b, now.lse_b, now.mixed_b = attention(part, None)
    now.proj_a, now.lse_a, now.mixed_a = attention(0, now.own_att)
    meet(now, q, u, n)
    u.step()
    n.step()
    now.own_down = take(now.place.T, down_weight, 1)
    meet(now, q, u, n)
    n.step()
    now.middle, now.two = blocked(
        functools.partial(out_kernel, head_cols, hidden_cols),
        [(now.mixed_a, STEP), (now.mixed_b, part), (now.stream, ALL)]
        + q.specs(now.own_att) + u.specs(now.own_up) + [(now.tail, ALL)],
        [((rows, width), F32, ALL), ((rows, width), BF16, ALL)],
        [vmem((rows, width), F32)],
        mp,
        dense * mp * head_cols,
    )

    def half_shape(cols):
        return ((part, width // 2, cols), BF16, STEP)

    hidden_shape = ((part, rows, hidden_cols), BF16, STEP)

    def up_part(at, own):
        hidden, slope, low_half, high_half = blocked(
            functools.partial(up_kernel, at == 0),
            [(now.two, ALL), (now.out_low, ALL)] + u.specs(own) + [(now.up_bias, -at)],
            [hidden_shape, hidden_shape, half_shape(hidden_cols), half_shape(hidden_cols)],
            [],
            part,
            2 * dense * part * hidden_cols,
            rows * part * hidden_cols,
            at=at,
        )
        return hidden, slope, Scatter(ring, low_half, high_half)

    def pre_part(at, own_up, own_down, more, outputs, scratch):
        return blocked(
            functools.partial(pre_kernel, at == 0),
            [(now.two, ALL), (now.out_low, ALL)] + u.specs(own_up) + n.specs(own_down) + more,
            [half_shape(hidden_cols), half_shape(hidden_cols), ((part, 1, hidden_cols), F32, STEP)] + outputs,
            scratch,
            part,
            3 * dense * part * hidden_cols,
            at=at,
        )

    now.hidden_b, now.slope_b, cb = up_part(part, None)
    meet(now, q, u, n, cb)
    n.step()
    cb.go()
    now.hidden_a, now.slope_a, ca = up_part(0, now.own_up)
    meet(now, q, u, n, ca, cb)
    cb.fold()
    cb.go()
    ca.go()
    low_half, high_half, now.up_sum_b, now.two_sum = pre_part(
        part, None, None, [(now.out.slope_b, STEP)], [((rows, width), F32, ALL)], []
    )
    bb = Scatter(ring, low_half, high_half)
    meet(now, q, u, n, ca, cb, bb)
    for each in (ca, cb):
        each.fold()
        each.go()
    bb.go()
    low_half, high_half, now.up_sum_a, now.grad_mid, now.mid, now.mid_sums = pre_part(
        0,
        now.own_up,
        now.own_down,
        [(now.out.slope_a, STEP), (now.out.two_sum, ALL), (now.middle, ALL), (now.tail, ALL)],
        [((rows, width), F32, ALL), ((rows, width), BF16, ALL), ((8, width), F32, ALL)],
        [vmem((rows, width), F32)],
    )
    ba = Scatter(ring, low_half, high_half)
    meet(now, q, u, n, ca, cb, ba, bb)
    for each in (bb, ca):
        each.fold()
        each.go()
    ba.go()
    rest_c = lax.ppermute(cb.settle(), MP, ring.blocks[-1])

    def attention_back(at, own, made):
        own_att, own_up = own
        q_specs, u_specs = q.specs(own_att), u.specs(own_up)
        weights = q_specs[:1] + u_specs[:1] + q_specs[1:] + u_specs[1:] if at == 0 else q_specs + u_specs
        return blocked(
            functools.partial(attention_back_kernel, head_cols, hidden_cols, at == 0),
            [(which, SCALAR), (lengths, SCALAR), (now.one, ALL), (now.mid, ALL)] + weights
            + [(a, STEP) for a in made],
            [((part, rows, qkv_cols), BF16, STEP), half_shape(4 * head_cols), half_shape(4 * head_cols), ((part, 1, qkv_cols), F32, STEP)],
            [],
            part,
            (dense * mp * 5 * head_cols + 5 * live) // 2,
            mp * heads * rows * rows // 2,
            at=at,
        )

    now.grad_b, low_half, high_half, now.proj_sum_b = attention_back(part, (None, None), (now.out.proj_b, now.out.mixed_b, now.out.lse_b))
    ab = Scatter(ring, low_half, high_half)
    now.rest_c = rest_c
    meet(now, q, u, n, ca, ba, bb, ab)
    for each in (ba, bb):
        each.fold()
        each.go()
    ab.go()
    ca.take_rest(now.out.rest_c, ring.blocks[0])
    ca.go()
    now.grad_a, low_half, high_half, now.proj_sum_a = attention_back(
        0, (now.own_att, now.out.own_up), (now.out.proj_a, now.out.mixed_a, now.out.lse_a)
    )
    aa = Scatter(ring, low_half, high_half)
    meet(now, q, n, ca, ba, bb, ab, aa)
    aa.go()
    ab.fold()
    ab.go()
    meet(now, q, n, aa, ba, bb, ca)
    aa.fold()
    aa.go()
    ba.fold()
    ba.go()
    rest_b = lax.ppermute(bb.settle(), MP, ring.blocks[-1])
    now.stream_grad, now.first_sums = blocked(
        functools.partial(first_kernel, head_cols),
        [(now.out.grad_a, STEP), (now.out.grad_b, part)] + q.specs(now.out.own_att)
        + [(a, ALL) for a in (now.stream, now.grad_mid, now.place, now.tail)],
        [((real_rows, width), F32, ALL), ((8, width), F32, ALL)],
        [vmem((rows, width), F32)],
        mp,
        dense * mp * qkv_cols,
        vmem=60,
    )
    now.rest_b = rest_b
    meet(now, n, ab, aa, ba, ca)
    aa.join(ab, ring.blocks)
    aa.fold()
    aa.go()
    ba.take_rest(now.out.rest_b, ring.blocks[0])
    ba.go()

    script = lax.dynamic_slice_in_dim(script_ids, across, 1, 0)[0]
    kind = (lax.broadcasted_iota(jnp.int32, (kinds, 1), 0) == script).astype(F32)
    first_sums = now.first_sums
    rows_of = jnp.concatenate([first_sums[0:2], now.mid_sums[0:4], kind * first_sums[2:3]], axis=0)
    n_vec = rows_of.shape[0]
    sub = head_cols // dp
    proj_sum = jnp.concatenate([now.proj_sum_a, now.proj_sum_b]).reshape(mp, 3, head_cols)
    qv = jnp.stack([proj_sum[:, 0], proj_sum[:, 2]], axis=1).reshape(mp * 2, dp, sub)
    qv = jnp.pad(qv, ((0, 0), (0, 0), (0, share - sub))).reshape(mp * 2, width)
    up_sum = jnp.concatenate([now.up_sum_a, now.up_sum_b])[:, 0]
    parts = jnp.concatenate(split3(jnp.concatenate([up_sum, qv], axis=0)), axis=0)
    cols = sum(jnp.split(jnp.dot(parts, now.place, preferred_element_type=F32), 3))
    small = jnp.concatenate([rows_of, cols], axis=0).T[None]
    ss = Scatter(ring, small[:, : width // 2], small[:, width // 2 :])
    ss.go()
    ss.fold()
    ss.go()
    (block,) = blocked(
        block_kernel,
        [(now.hidden_a, STEP), (now.hidden_b, part)] + n.specs(now.own_down) + [(a, ALL) for a in (now.middle, now.place, now.tail)],
        [((real_rows, width), F32, ALL)],
        [vmem((rows, width), F32)],
        mp,
        dense * mp * hidden_cols,
    )
    now = Bag(block=block, stream_grad=now.stream_grad)
    meet(now, aa, ss)
    aa.fold()
    aa.go()
    while ss.left:
        ss.fold()
        ss.go()
    sums = ss.settle()
    sums = jnp.concatenate([sums, lax.ppermute(sums, MP, ring.blocks[0])], axis=0)
    now.sums = sums
    meet(now, aa, ba)
    aa.fold()
    aa.go()
    sums = now.sums
    parts = jnp.concatenate([sums, lax.ppermute(sums, MP, ring.blocks[1])], axis=0)
    vectors = sum(p[:, :n_vec] for p in parts)
    vectors = lax.dynamic_slice_in_dim(vectors, across * (share // mp), share // mp, 0).T
    up_bias_grad = sum(p[:, n_vec + s] for s, p in enumerate(parts))
    qv_grad = sum(p[:sub, n_vec + mp + 2 * s : n_vec + mp + 2 * s + 2] for s, p in enumerate(parts)).T
    grad_down, grad_up = ca.total(), ba.total()
    grad_att = aa.total()
    block, stream_grad = now.block, now.stream_grad

    return (
        block,
        stream_grad,
        vectors[6:],
        vectors[0],
        vectors[1],
        grad_att[:, : 3 * head_cols].reshape(share, 3, head_cols),
        qv_grad,
        grad_att[:, 3 * head_cols :].T,
        vectors[2],
        vectors[3],
        vectors[4],
        grad_up,
        up_bias_grad,
        grad_down.T,
        vectors[5],
    )


def solution(mesh):
    placed = (
        P(DP, None),
        P(DP),
        P(DP),
        P(),
        P(),
        P(),
        P(None, None, MP),
        P(None, MP),
        P(MP, None),
        P(),
        P(),
        P(),
        P(None, MP),
        P(MP),
        P(MP, None),
        P(),
        P(DP, None),
    )
    return jax.shard_map(
        on_device,
        mesh=mesh,
        in_specs=placed,
        out_specs=(
            P((DP, MP), None),
            P((DP, MP), None),
            P(None, (DP, MP)),
            P((DP, MP)),
            P((DP, MP)),
            P(DP, None, MP),
            P(None, (MP, DP)),
            P(MP, DP),
            P((DP, MP)),
            P((DP, MP)),
            P((DP, MP)),
            P(DP, MP),
            P((MP, DP)),
            P(MP, DP),
            P((DP, MP)),
        ),
        check_vma=False,
    )
```

```python
import functools
import types

import numpy as np
import jax
import jax.numpy as jnp
from jax import lax
from jax.experimental import pallas as pl
from jax.experimental.pallas import tpu as pltpu
from jax.sharding import PartitionSpec as P

HD = 64
DP, MP, PAIR, KEPT = "dp", "mp", "pair", "kept"
ALL, STEP, REST, SCALAR = "all", "step", "rest", "scalar"
EPS = 1e-05
MASKED = -1e30
BF16 = jnp.bfloat16
F32 = jnp.float32


LOG2E = 1.4426950408889634
LN2 = 0.6931471805599453


def layer_norm(rows, gain, shift):
    center = rows - jnp.mean(rows, axis=-1, keepdims=True)
    scale = lax.rsqrt(jnp.mean(center * center, axis=-1, keepdims=True) + EPS)
    normalized = center * scale
    return (normalized * gain + shift, normalized, scale)


def norm_back(grad_out, normalized, scale, gain):
    scaled = grad_out * gain
    first_mean = jnp.mean(scaled, axis=-1, keepdims=True)
    second_mean = jnp.mean(scaled * normalized, axis=-1, keepdims=True)
    return scale * (scaled - first_mean - normalized * second_mean)


def mm(a, b):
    return lax.dot_general(a, b, (((1,), (0,)), ((), ())), preferred_element_type=F32)


def mm_t(a, b):
    return lax.dot_general(a, b, (((1,), (1,)), ((), ())), preferred_element_type=F32)


def start_kernel(across, script_ids, rows_in, rows_out, embed, *refs):
    vectors, (place, stream, low_one, low_out, tail) = refs[:6], refs[6:]
    width = rows_in.shape[1]
    kind = lax.broadcasted_iota(jnp.int32, embed.shape, 0) == script_ids[across[0]]
    added = jnp.sum(jnp.where(kind, embed[...].astype(F32), 0.0), axis=0, keepdims=True)
    table = jnp.concatenate([v[...].reshape(1, width) for v in vectors] + [added, jnp.zeros((1, width), F32)], axis=0)
    order = place[...]
    table = sum(mm(piece, order) for piece in split3(table))
    tail[...] = table
    x = mm(rows_in[...], order) + table[6:7]
    stream[...] = x
    low_one[...] = layer_norm(x, table[4:5], table[5:6])[0].astype(BF16)
    low_out[...] = mm(rows_out[...], order).astype(BF16)


def split3(v):
    high = v.astype(BF16)
    rest = v - high.astype(F32)
    mid = rest.astype(BF16)
    return [high, mid, (rest - mid.astype(F32)).astype(BF16)]


def attention_kernel(cols, has_own, across, lengths, one, *refs):
    own, (low, high, bias, proj_out, lse_out, mixed_out) = (refs[0], refs[1:]) if has_own else (None, refs)
    rows = one.shape[0]
    half = one.shape[1] // 2
    heads = cols // HD

    def body(w0, w1):
        a = one[...]
        p = mm(a[:, :half], w0) + mm(a[:, half:], w1) + bias[0]
        p = p.astype(BF16)
        proj_out[0] = p
        dead = jnp.where(lax.broadcasted_iota(jnp.int32, (rows, 1), 0) < lengths[across[0]], 0.0, MASKED)
        ones = jnp.where(lax.broadcasted_iota(jnp.int32, (rows, HD), 1) == 0, 1.0, 0.0).astype(BF16)
        lse_out[0] = jnp.zeros(lse_out.shape[1:], F32)
        outs = []
        for h in range(heads):
            q, k, v = (p[:, i * cols + h * HD : i * cols + (h + 1) * HD] for i in range(3))
            scores = mm_t(k, q) * (0.125 * LOG2E) + dead
            top = jnp.max(scores, axis=0, keepdims=True)
            expo = jnp.exp2(scores - top).astype(BF16)
            both = mm(jnp.concatenate([v, ones], axis=1).T, expo)
            total = both[HD : HD + 1]
            lse_out[0, h : h + 1] = top + jnp.log2(total)
            outs.append((both[:HD] * (1.0 / total)).T.astype(BF16))
        mixed_out[0] = jnp.concatenate(outs, axis=1)

    run(has_own, body, own, low, high, slice(0, 3 * cols))


def run(has_own, body, own, low, high, cols):
    if has_own:
        half = low.shape[1]

        @pl.when(pl.program_id(0) == 0)
        def _():
            body(own[:half, cols], own[half:, cols])

        @pl.when(pl.program_id(0) > 0)
        def _():
            body(low[0, :, cols], high[0, :, cols])

    else:
        body(low[0, :, cols], high[0, :, cols])


def out_kernel(cols, hidden, mixed_a, mixed_b, x, own, low, high, up_own, up_low, up_high, tail, mid_out, two_out, total):
    step = pl.program_id(0)
    half = x.shape[1] // 2
    one, two = slice(3 * cols, None), slice(hidden, None)

    def body(heads, w0, w1, u0, u1):
        split = w0.shape[1]
        total[:, :half] += mm_t(heads[:, :split], w0) + mm_t(heads[:, split:], u0)
        total[:, half:] += mm_t(heads[:, :split], w1) + mm_t(heads[:, split:], u1)

    @pl.when(step == 0)
    def _():
        total[...] = x[...] + tail[0:1]
        body(mixed_a[0], own[:half, one], own[half:, one], up_own[:half, two], up_own[half:, two])

    @pl.when(step > 0)
    def _():
        body(jnp.where(step < 2, mixed_a[0], mixed_b[0]), low[0, :, one], high[0, :, one], up_low[0, :, two], up_high[0, :, two])

    @pl.when(step == pl.num_programs(0) - 1)
    def _():
        mid = total[...]
        mid_out[...] = mid
        two_out[...] = layer_norm(mid, tail[1:2], tail[2:3])[0].astype(BF16)


def feature_grad(left, right, grad0, grad1, at):
    half = grad0.shape[1]
    out = lax.dot_general(left, right, (((0,), (0,)), ((), ())), preferred_element_type=F32).astype(BF16)
    grad0[0, :, at] = out[:half]
    grad1[0, :, at] = out[half:]


def up_kernel(has_own, two, out_low, *refs):
    own, (low, high, bias, hidden_out, slope_out, grad0, grad1) = (refs[0], refs[1:]) if has_own else (None, refs)
    rows, width = two.shape
    half = width // 2
    cols = hidden_out.shape[2]
    c0, c1 = 0.7978845608028654, 0.7978845608028654 * 0.044715

    def body(w0, w1):
        for at in (slice(0, rows // 2), slice(rows // 2, rows)):
            v = mm(two[at, :half], w0) + mm(two[at, half:], w1) + bias[0]
            square = v * v
            t = jnp.tanh(v * (c0 + c1 * square))
            grow = 0.5 + 0.5 * t
            hidden_out[0, at] = (v * grow).astype(BF16)
            slope_out[0, at] = (grow + v * (0.5 - 0.5 * t * t) * (c0 + 3 * c1 * square)).astype(BF16)
        feature_grad(out_low[...], hidden_out[0], grad0, grad1, slice(0, cols))

    run(has_own, body, own, low, high, slice(0, cols))


def pre_kernel(last, two, out_low, *refs):
    if last:
        (own, low, high, down_own, down_low, down_high, slope, two_in, mid, tail), refs = refs[:10], refs[10:]
        grad0, grad1, bias_sum, grad_mid_out, low_mid_out, sums, two_sum = refs
    else:
        low, high, down_low, down_high, slope, grad0, grad1, bias_sum, two_sum = refs
    step = pl.program_id(0)
    half = two.shape[1] // 2
    cols = slope.shape[2]
    ours = slice(0, cols)

    @pl.when(step == 0)
    def _():
        two_sum[...] = two_in[...] if last else jnp.zeros(two_sum.shape, F32)

    def body(w0, w1, d0, d1):
        a = out_low[...]
        grad = ((mm(a[:, :half], d0) + mm(a[:, half:], d1)) * slope[0].astype(F32)).astype(BF16)
        bias_sum[0] = jnp.sum(grad.astype(F32), axis=0, keepdims=True)
        feature_grad(two[...], grad, grad0, grad1, ours)
        two_sum[:, :half] += mm_t(grad, w0)
        two_sum[:, half:] += mm_t(grad, w1)

    if last:

        @pl.when(step == 0)
        def _():
            body(own[:half, ours], own[half:, ours], down_own[:half], down_own[half:])

        @pl.when(step > 0)
        def _():
            body(low[0, :, ours], high[0, :, ours], down_low[0], down_high[0])

        @pl.when(step == pl.num_programs(0) - 1)
        def _():
            grad = two_sum[...]
            _, normalized, scale = layer_norm(mid[...], tail[1:2], tail[2:3])
            rows_out = out_low[...].astype(F32)
            grad_mid = rows_out + norm_back(grad, normalized, scale, tail[1:2])
            low_mid = grad_mid.astype(BF16)
            grad_mid_out[...] = grad_mid
            low_mid_out[...] = low_mid
            sums[0:1] = jnp.sum(low_mid.astype(F32), axis=0, keepdims=True)
            sums[1:2] = jnp.sum(grad * normalized, axis=0, keepdims=True)
            sums[2:3] = jnp.sum(grad, axis=0, keepdims=True)
            sums[3:4] = jnp.sum(rows_out, axis=0, keepdims=True)

    else:
        body(low[0, :, ours], high[0, :, ours], down_low[0], down_high[0])


def attention_back_kernel(cols, hidden, has_own, across, lengths, one, low_mid, *refs):
    own, up_own, refs = (refs[0], refs[1], refs[2:]) if has_own else (None, None, refs)
    low, high, up_low, up_high, proj, mixed, lse, proj_out, grad0, grad1, sums = refs
    rows = one.shape[0]
    half = one.shape[1] // 2
    heads = cols // HD
    first, second = slice(3 * cols, None), slice(hidden, None)

    def body(w0, w1, u0, u1):
        a = low_mid[...]
        grad_mixed = mm(a[:, :half], jnp.concatenate([w0, u0], axis=1)) + mm(a[:, half:], jnp.concatenate([w1, u1], axis=1))
        grad_mixed = grad_mixed.astype(BF16)
        p = proj[0]
        dead = jnp.where(lax.broadcasted_iota(jnp.int32, (rows, 1), 0) < lengths[across[0]], 0.0, MASKED)
        grads = [[], [], []]
        for h in range(heads):
            q, k, v = (p[:, i * cols + h * HD : i * cols + (h + 1) * HD] for i in range(3))
            out = grad_mixed[:, h * HD : (h + 1) * HD]
            probs = jnp.exp2((mm_t(k, q) * (0.125 * LOG2E) + dead) - lse[0, h : h + 1])
            grad_probs = mm_t(v, out)
            inner = jnp.sum(probs * grad_probs, axis=0, keepdims=True)
            grad_scores = (probs * (grad_probs - inner)).astype(BF16)
            grads[2].append(mm(probs.astype(BF16), out).astype(BF16))
            grads[1].append((mm(grad_scores, q) * 0.125).astype(BF16))
            grads[0].append((mm(k.T, grad_scores) * 0.125).T.astype(BF16))
        grad = jnp.concatenate(grads[0] + grads[1] + grads[2], axis=1)
        proj_out[0] = grad
        sums[0] = jnp.sum(grad.astype(F32), axis=0, keepdims=True)
        for left, right, at in ((one, grad, slice(0, 3 * cols)), (low_mid, mixed[0], slice(3 * cols, 4 * cols))):
            out = lax.dot_general(left[...], right, (((0,), (0,)), ((), ())), preferred_element_type=F32).astype(BF16)
            grad0[0, :, at] = out[:half]
            grad1[0, :, at] = out[half:]

    if has_own:

        @pl.when(pl.program_id(0) == 0)
        def _():
            body(own[:half, first], own[half:, first], up_own[:half, second], up_own[half:, second])

        @pl.when(pl.program_id(0) > 0)
        def _():
            body(low[0, :, first], high[0, :, first], up_low[0, :, second], up_high[0, :, second])

    else:
        body(low[0, :, first], high[0, :, first], up_low[0, :, second], up_high[0, :, second])


def unplace(value, place):
    high = value.astype(BF16)
    low = (value - high.astype(F32)).astype(BF16)
    return mm_t(high, place) + mm_t(low, place)


def first_kernel(cols, across, script_ids, mid_sums, grad_a, grad_b, own, low, high, x, grad_mid, tail, rows_out, sums, total):
    step = pl.program_id(0)
    half = x.shape[1] // 2

    @pl.when(step == 0)
    def _():
        total[...] = jnp.zeros(total.shape, F32)

    def body(w0, w1):
        grad = jnp.where(step < 2, grad_a[0], grad_b[0])
        total[:, :half] += mm_t(grad, w0)
        total[:, half:] += mm_t(grad, w1)

    run(True, body, own, low, high, slice(0, 3 * cols))

    @pl.when(step == pl.num_programs(0) - 1)
    def _():
        grad = total[...]
        _, normalized, scale = layer_norm(x[...], tail[4:5], tail[5:6])
        stream = grad_mid[...] + norm_back(grad, normalized, scale, tail[4:5])
        kinds = sums.shape[0] - 8
        kind = lax.broadcasted_iota(jnp.int32, (kinds, 1), 0) == script_ids[across[0]]
        sums[0:kinds] = jnp.where(kind, jnp.sum(stream, axis=0, keepdims=True), 0.0)
        sums[kinds : kinds + 4] = mid_sums[0:4]
        sums[kinds + 4 : kinds + 5] = jnp.sum(grad * normalized, axis=0, keepdims=True)
        sums[kinds + 5 : kinds + 6] = jnp.sum(grad, axis=0, keepdims=True)
        sums[kinds + 6 :] = jnp.zeros((2, sums.shape[1]), F32)
        rows_out[...] = stream


def back_kernel(stream, place, rows_out):
    rows_out[...] = unplace(stream[...], place[...])[: rows_out.shape[0]]


def block_kernel(hidden_a, hidden_b, own, low, high, mid, place, tail, rows_out, total):
    step = pl.program_id(0)
    half = mid.shape[1] // 2

    @pl.when(step == 0)
    def _():
        total[...] = mid[...] + tail[3:4]

    def body(w0, w1):
        hidden = jnp.where(step < 2, hidden_a[0], hidden_b[0])
        total[:, :half] += mm_t(hidden, w0)
        total[:, half:] += mm_t(hidden, w1)

    run(True, body, own, low, high, slice(None))

    @pl.when(step == pl.num_programs(0) - 1)
    def _():
        rows_out[...] = unplace(total[...], place[...])[: rows_out.shape[0]]


def blocked(kernel, inputs, outputs, scratch, steps, flops, transcendentals=0, at=0, vmem=20):
    def spec(shape, kind):
        if kind == SCALAR:
            return pl.BlockSpec(memory_space=pltpu.SMEM)
        zeros = (0,) * (len(shape) - 1)
        if kind == ALL:
            return pl.BlockSpec(shape, lambda s: (0,) + zeros, pipeline_mode=pl.Buffered(1))
        back = {STEP: 0, REST: 1 - at}.get(kind, kind)
        return pl.BlockSpec((1,) + shape[1:], lambda s: (jnp.clip(s - back, 0, shape[0] - 1),) + zeros)

    arrays = [a for a, _ in inputs]
    nbytes = sum(a.size * a.dtype.itemsize for a in arrays) + sum(int(np.prod(s)) * jnp.dtype(d).itemsize for s, d, _ in outputs)
    return pl.pallas_call(
        kernel,
        grid=(steps,),
        in_specs=[spec(a.shape, k) for a, k in inputs],
        out_specs=[spec(s, k) for s, _, k in outputs],
        out_shape=[jax.ShapeDtypeStruct(s, d) for s, d, _ in outputs],
        scratch_shapes=scratch,
        compiler_params=pltpu.CompilerParams(dimension_semantics=("arbitrary",), vmem_limit_bytes=vmem * 1024 * 1024),
        cost_estimate=pl.CostEstimate(flops=int(flops), bytes_accessed=nbytes, transcendentals=int(transcendentals)),
    )(*arrays)


CHUNK = 32


class Leaving:
    def __init__(self, bag):
        self._bag = bag

    def __getattr__(self, name):
        return vars(self._bag).pop(name)


class Bag(types.SimpleNamespace):
    @property
    def out(self):
        return Leaving(self)


class Ring:
    def __init__(self, dp, mp):
        self.dp, self.mp = dp, mp
        bits = list(range(1, dp.bit_length() - 1))
        self.orders = (bits, bits[::-1])
        self.stages = [[(i, i ^ (1 << self.orders[i & 1][t])) for i in range(dp)] for t in range(len(bits))]
        cut = (len(self.stages) + 1) // 2
        self.rounds = [self.stages[:cut], self.stages[cut:]]
        self.pair = [(i, i ^ 1) for i in range(dp)]
        self.blocks = [[(i, i ^ (1 << b)) for i in range(mp)] for b in range(mp.bit_length() - 1)][::-1]
        self.block_masks = [0]
        for b in reversed(range(mp.bit_length() - 1)):
            self.block_masks += [m ^ (1 << b) for m in self.block_masks]
        self.direct = [[(i, i ^ m) for i in range(mp)] for m in self.block_masks[1:]]
        halves = []
        for order in self.orders:
            masks = [0]
            for bit in order:
                masks = masks + [m | (1 << bit) for m in masks]
            halves.append(masks)
        self.masks = np.array([halves[0] + [1 ^ m for m in halves[1]], halves[1] + [1 ^ m for m in halves[0]]], np.int32)


class Gather:
    def __init__(self, ring, piece, share, direct=False):
        self.share = share
        self.v = Bag(held=piece[None])
        blocks = [(MP, ring.direct)] if direct else [(MP, [s]) for s in ring.blocks]
        self.left = blocks + [(DP, g) for g in ring.rounds] + [(PAIR, [ring.pair])]

    def step(self):
        axis, stages = self.left.pop(0)
        if axis == PAIR:
            self.v.high = lax.ppermute(self.v.held, DP, stages[0])
            return
        held = self.v.held
        if len(stages) > 1 and axis == MP:
            self.v.held = jnp.concatenate([lax.ppermute(held, axis, stage) for stage in stages])
            return
        for stage in stages:
            held = jnp.concatenate([held, lax.ppermute(held, axis, stage)], axis=0 if axis == MP else 1)
        if axis == MP and self.left[0][0] != MP:
            if held.shape[1] > self.share:
                self.v.extra = held[:, self.share :]
            held = held[1:, : self.share]
        self.v.held = held

    def specs(self, own):
        return ([(own, ALL)] if own is not None else []) + [(self.v.held, REST), (self.v.high, REST)]


class Scatter:
    def __init__(self, ring, low_half, high_half):
        self.v = Bag(held=low_half, send=high_half)
        self.axis, self.stage = DP, ring.pair
        self.left = [(DP, 1, group[::-1]) for group in ring.rounds[::-1]]

    def go(self):
        self.v.got = lax.ppermute(self.v.out.send, self.axis, self.stage)

    def add(self, at, size, dim):
        a, b = (lax.slice_in_dim(v, at, at + size, axis=dim).astype(F32) for v in (self.v.held, self.v.got))
        return (a + b).astype(self.v.held.dtype)

    def fold(self):
        self.axis, dim, stages = self.left.pop(0)
        for i, stage in enumerate(stages):
            if i:
                self.go()
            self.stage = stage
            size = self.v.held.shape[dim] // 2
            self.v = Bag(send=self.add(size, size, dim), held=self.add(0, size, dim))

    def cut(self):
        self.axis, dim, stages = self.left.pop(0)
        size = self.v.held.shape[dim] // 2
        parts = [lax.slice_in_dim(self.v.held, i * size, (i + 1) * size, axis=dim) for i in range(2)]
        self.v, self.stage = Bag(held=parts[0], send=parts[1]), stages[0]
        if len(stages) > 1:
            self.left.insert(0, (self.axis, dim, stages[1:]))
            self.go()
            self.fold()

    def settle(self):
        return self.add(0, self.v.held.shape[0], 0)

    def take_rest(self, rest, stage):
        self.v = Bag(held=self.settle(), got=rest)
        self.left = [(MP, 0, [stage])]
        self.fold()

    def total(self):
        return self.v.held[0].astype(F32) + self.v.got[0].astype(F32)


def meet(live, *moving):
    bags = [live] + [m.v for m in moving]
    for bag, values in zip(bags, lax.optimization_barrier([vars(b) for b in bags])):
        vars(bag).update(values)


def meet_kept(moving, *flows):
    kept = Bag(**{KEPT + str(i): f.v.held for i, f in enumerate(flows)})
    meet(kept, moving)
    for f, held in zip(flows, vars(kept).values()):
        f.v.held = held


def on_device(
    patches,
    script_ids,
    lengths,
    script_embed,
    norm1_gain,
    norm1_shift,
    query_key_value_weight,
    b_qv,
    attention_out_weight,
    attention_out_bias,
    norm2_gain,
    norm2_shift,
    up_weight,
    up_proj_bias,
    down_weight,
    down_proj_bias,
    out_grad,
):
    dp, mp = lax.axis_size(DP), lax.axis_size(MP)
    ring = Ring(dp, mp)
    here, across = lax.axis_index(DP), lax.axis_index(MP)
    rows_all, width = patches.shape
    rows = rows_all // mp
    share = width // dp
    head_cols = query_key_value_weight.shape[2]
    hidden_cols = up_weight.shape[1]
    heads = head_cols // HD
    kinds = script_embed.shape[0]

    order = jnp.where((here & 1) == 0, ring.masks[0], ring.masks[1]) ^ here
    source = (order[:, None] * share + jnp.arange(share, dtype=jnp.int32)[None, :]).reshape(width)
    place = (lax.broadcasted_iota(jnp.int32, (width, width), 0) == source[None, :]).astype(BF16)
    mine = (
        lax.broadcasted_iota(jnp.int32, (share, width), 1) == here * share + lax.broadcasted_iota(jnp.int32, (share, width), 0)
    ).astype(BF16)

    def take(rows_of, block, features):
        out = lax.dot_general(rows_of, block, (((1,), (features,)), ((), ())), preferred_element_type=F32)
        return out.astype(BF16)

    def put(v):
        parts = jnp.concatenate(split3(v), axis=0)
        return sum(jnp.split(jnp.dot(parts, place, preferred_element_type=F32), 3))

    qkv_cols = 3 * head_cols
    behind = -qkv_cols % 128
    att_own = query_key_value_weight.reshape(width, qkv_cols)
    out_a, out_b = attention_out_weight[:behind], attention_out_weight[behind:]
    up_cols = hidden_cols + head_cols - behind
    zeros = jnp.zeros((head_cols,), F32)
    spare = jnp.zeros((up_cols - qkv_cols,), F32)
    flat = jnp.concatenate([b_qv[0], zeros, b_qv[1], spare, up_proj_bias, jnp.zeros((up_cols - hidden_cols,), F32)]).reshape(2, up_cols)
    bias_rows = jnp.concatenate(split3(flat))
    bias_rows = jnp.pad(bias_rows, ((0, -bias_rows.shape[0] % 16), (0, 0)))

    padded = -(-rows // CHUNK) * CHUNK
    grow = ((0, padded - rows), (0, 0))
    real_rows, rows = rows, padded
    vmem = pltpu.VMEM
    dense = 2 * rows * width
    live = 2 * mp * heads * rows * rows * HD
    part = mp // 2
    which = across.reshape(1)

    q = Gather(ring, jnp.concatenate([take(mine, att_own, 0), take(mine, out_a, 1)], axis=1), share, direct=True)
    q.step()
    up_piece = jnp.concatenate([take(mine, up_weight, 0), take(mine, out_b, 1)], axis=1)
    now = Bag(
        up=jnp.concatenate([up_piece, bias_rows]),
        rows=jnp.pad(lax.dynamic_slice_in_dim(patches, across * real_rows, real_rows, 0), grow),
        cotangent=jnp.pad(lax.dynamic_slice_in_dim(out_grad, across * real_rows, real_rows, 0), grow),
        place=place,
    )
    meet(now, q)
    u = Gather(ring, now.out.up, share)
    q.step()
    u.step()
    now.down = take(mine, down_weight, 1)
    now.stream, now.one, now.out_low, now.tail = blocked(
        start_kernel,
        [(which, SCALAR), (script_ids, SCALAR), (now.out.rows, ALL), (now.out.cotangent, ALL), (script_embed, ALL)]
        + [(v, ALL) for v in (attention_out_bias, norm2_gain, norm2_shift, down_proj_bias, norm1_gain, norm1_shift)]
        + [(now.place, ALL)],
        [((rows, width), F32, ALL), ((rows, width), BF16, ALL), ((rows, width), BF16, ALL), ((8, width), F32, ALL)],
        [],
        1,
        2 * dense * width,
    )
    meet(now, q, u)
    q.step()
    u.step()
    now.own_att = jnp.concatenate([take(now.place.T, att_own, 0), take(now.place.T, out_a, 1)], axis=1)
    meet(now, q, u)
    n = Gather(ring, now.out.down, share)
    bias_all = u.v.out.extra.astype(F32)
    bias_all = bias_all[:, 0:2] + bias_all[:, 2:4] + bias_all[:, 4:6]
    now.qkv_bias = bias_all[:, 0:1, :qkv_cols]
    now.up_bias = bias_all[:, 1:2, :hidden_cols]
    q.step()
    u.step()
    n.step()
    meet(now, q, u, n)
    u.step()
    n.step()

    def attention(at, own):
        return blocked(
            functools.partial(attention_kernel, head_cols, at == 0),
            [(which, SCALAR), (lengths, SCALAR), (now.one, ALL)] + q.specs(own) + [(now.qkv_bias, -at)],
            [((part, rows, qkv_cols), BF16, STEP), ((part, 8, rows), F32, STEP), ((part, rows, head_cols), BF16, STEP)],
            [],
            part,
            (dense * mp * qkv_cols + 2 * live) // 2,
            mp * heads * rows * rows // 2,
            at=at,
        )

    now.proj_b, now.lse_b, now.mixed_b = attention(part, None)
    now.proj_a, now.lse_a, now.mixed_a = attention(0, now.own_att)
    meet(now, q, u, n)
    u.step()
    n.step()
    order_t = now.place.T
    now.own_up = jnp.concatenate([take(order_t, up_weight, 0), take(order_t, out_b, 1)], axis=1)
    now.own_down = take(order_t, down_weight, 1)
    meet(now, q, u, n)
    n.step()
    now.middle, now.two = blocked(
        functools.partial(out_kernel, head_cols, hidden_cols),
        [(now.mixed_a, STEP), (now.mixed_b, part), (now.stream, ALL)]
        + q.specs(now.own_att) + u.specs(now.own_up) + [(now.tail, ALL)],
        [((rows, width), F32, ALL), ((rows, width), BF16, ALL)],
        [vmem((rows, width), F32)],
        mp,
        dense * mp * head_cols,
    )

    def half_shape(cols):
        return ((part, width // 2, cols), BF16, STEP)

    hidden_shape = ((part, rows, hidden_cols), BF16, STEP)

    def up_part(at, own):
        hidden, slope, low_half, high_half = blocked(
            functools.partial(up_kernel, at == 0),
            [(now.two, ALL), (now.out_low, ALL)] + u.specs(own) + [(now.up_bias, -at)],
            [hidden_shape, hidden_shape, half_shape(hidden_cols), half_shape(hidden_cols)],
            [],
            part,
            2 * dense * part * hidden_cols,
            rows * part * hidden_cols,
            at=at,
        )
        return hidden, slope, Scatter(ring, low_half, high_half)

    def pre_part(at, own_up, own_down, more, outputs, scratch):
        return blocked(
            functools.partial(pre_kernel, at == 0),
            [(now.two, ALL), (now.out_low, ALL)] + u.specs(own_up) + n.specs(own_down) + more,
            [half_shape(hidden_cols), half_shape(hidden_cols), ((part, 1, hidden_cols), F32, STEP)] + outputs,
            scratch,
            part,
            3 * dense * part * hidden_cols,
            at=at,
        )

    now.hidden_b, now.slope_b, cb = up_part(part, None)
    meet(now, q, u, n, cb)
    n.step()
    cb.go()
    now.hidden_a, now.slope_a, ca = up_part(0, now.own_up)
    meet(now, q, u, n, ca, cb)
    cb.fold()
    cb.go()
    ca.go()
    low_half, high_half, now.up_sum_b, now.two_sum = pre_part(
        part, None, None, [(now.out.slope_b, STEP)], [((rows, width), F32, ALL)], []
    )
    bb = Scatter(ring, low_half, high_half)
    meet(now, q, u, n, ca, cb, bb)
    for each in (ca, cb):
        each.fold()
        each.go()
    bb.go()
    low_half, high_half, now.up_sum_a, now.grad_mid, now.mid, now.mid_sums = pre_part(
        0,
        now.own_up,
        now.own_down,
        [(now.out.slope_a, STEP), (now.out.two_sum, ALL), (now.middle, ALL), (now.tail, ALL)],
        [((rows, width), F32, ALL), ((rows, width), BF16, ALL), ((8, width), F32, ALL)],
        [vmem((rows, width), F32)],
    )
    ba = Scatter(ring, low_half, high_half)
    meet(now, q, u, n, ca, cb, ba, bb)
    for each in (bb, ca):
        each.fold()
        each.go()
    ba.go()
    rest_c = lax.ppermute(cb.settle(), MP, ring.blocks[-1])

    def attention_back(at, own, made):
        own_att, own_up = own
        q_specs, u_specs = q.specs(own_att), u.specs(own_up)
        weights = q_specs[:1] + u_specs[:1] + q_specs[1:] + u_specs[1:] if at == 0 else q_specs + u_specs
        return blocked(
            functools.partial(attention_back_kernel, head_cols, hidden_cols, at == 0),
            [(which, SCALAR), (lengths, SCALAR), (now.one, ALL), (now.mid, ALL)] + weights
            + [(a, STEP) for a in made],
            [((part, rows, qkv_cols), BF16, STEP), half_shape(4 * head_cols), half_shape(4 * head_cols), ((part, 1, qkv_cols), F32, STEP)],
            [],
            part,
            (dense * mp * 5 * head_cols + 5 * live) // 2,
            mp * heads * rows * rows // 2,
            at=at,
        )

    now.grad_b, low_half, high_half, now.proj_sum_b = attention_back(part, (None, None), (now.out.proj_b, now.out.mixed_b, now.out.lse_b))
    ab = Scatter(ring, low_half, high_half)
    now.rest_c = rest_c
    meet(now, q, u, n, ca, ba, bb, ab)
    for each in (ba, bb):
        each.fold()
        each.go()
    ab.go()
    ca.take_rest(now.out.rest_c, ring.blocks[0])
    ca.go()
    now.grad_a, low_half, high_half, now.proj_sum_a = attention_back(
        0, (now.own_att, now.out.own_up), (now.out.proj_a, now.out.mixed_a, now.out.lse_a)
    )
    aa = Scatter(ring, low_half, high_half)
    meet(now, q, n, ca, ba, bb, ab, aa)
    aa.go()
    ab.fold()
    ab.go()
    ba.fold()
    ba.go()
    rest_b = lax.ppermute(bb.settle(), MP, ring.blocks[-1])
    now.stream_grad, now.sums = blocked(
        functools.partial(first_kernel, head_cols),
        [(which, SCALAR), (script_ids, SCALAR), (now.out.mid_sums, ALL), (now.out.grad_a, STEP), (now.out.grad_b, part)]
        + q.specs(now.out.own_att)
        + [(a, ALL) for a in (now.stream, now.grad_mid, now.tail)],
        [((rows, width), F32, ALL), ((kinds + 8, width), F32, ALL)],
        [vmem((rows, width), F32)],
        mp,
        dense * mp * qkv_cols,
        vmem=60,
    )
    now.rest_b = rest_b
    meet(now, n, ab, aa, ba, ca)
    n_vec = kinds + 8
    sub = head_cols // dp
    proj_sum = jnp.concatenate([now.proj_sum_a, now.proj_sum_b]).reshape(mp, 3, head_cols)
    qv = jnp.stack([proj_sum[:, 0], proj_sum[:, 2]], axis=1).reshape(mp * 2, dp, sub)
    qv = jnp.pad(qv, ((0, 0), (0, 0), (0, share - sub))).reshape(mp * 2, width)
    up_sum = jnp.concatenate([now.up_sum_a, now.up_sum_b])[:, 0]
    parts = jnp.concatenate(split3(jnp.concatenate([up_sum, qv], axis=0)), axis=0)
    cols = sum(jnp.split(jnp.dot(parts, now.place, preferred_element_type=F32), 3))
    small = jnp.concatenate([now.out.sums, cols], axis=0).T[None]
    ss = Scatter(ring, small[:, : width // 2], small[:, width // 2 :])
    ss.go()
    aa.fold()
    aa.go()
    meet_kept(ss, aa)
    ss.v = Bag(held=ss.settle())
    ss.v.got = lax.ppermute(ss.v.held, MP, ring.blocks[0])
    ab.fold()
    ab.go()
    meet_kept(ss, ab)
    ss.v = Bag(held=jnp.concatenate([ss.v.held, ss.v.got]))
    ss.v.got = lax.ppermute(ss.v.held, MP, ring.blocks[1])
    (block,) = blocked(
        block_kernel,
        [(now.hidden_a, STEP), (now.hidden_b, part)] + n.specs(now.own_down) + [(a, ALL) for a in (now.middle, now.place, now.tail)],
        [((real_rows, width), F32, ALL)],
        [vmem((rows, width), F32)],
        mp,
        dense * mp * hidden_cols,
    )
    now = Bag(block=block, stream_grad=now.stream_grad, place=now.place, rest_b=now.rest_b)
    meet(now, aa, ab, ba, ca, ss)
    parts = jnp.concatenate([ss.v.held, ss.v.got])
    own_sums = [sum(p[:, :n_vec] for p in parts), sum(p[:, n_vec + i : n_vec + i + 1] for i, p in enumerate(parts))]
    own_sums.append(sum(p[:, n_vec + mp + 2 * i : n_vec + mp + 2 * i + 2] for i, p in enumerate(parts)))
    ss.v = Bag(held=jnp.concatenate(own_sums, axis=1)[None])
    ss.cut()
    ss.go()
    aa.fold()
    aa.go()
    rest_a = lax.ppermute(ab.settle(), MP, ring.blocks[-1])
    meet_kept(ss, aa, ba)
    ss.fold()
    ss.go()
    ba.take_rest(now.out.rest_b, ring.blocks[0])
    ba.go()
    (now.stream_grad,) = blocked(
        back_kernel, [(now.stream_grad, ALL), (now.out.place, ALL)], [((real_rows, width), F32, ALL)], [], 1, 2 * dense * width
    )
    now.grad_down = ca.total()
    now.rest_a = rest_a
    meet(now, aa, ba, ss)
    aa.take_rest(now.out.rest_a, ring.blocks[0])
    aa.go()
    now.grad_up = ba.total()
    sums = ss.settle()[0]
    now.vectors = lax.dynamic_slice_in_dim(sums[:, :n_vec], across * (share // mp), share // mp, 0).T
    now.up_bias_grad = sums[:, n_vec]
    now.qv_grad = sums[:sub, n_vec + 1 :].T
    meet(now, aa)
    grad_down, grad_up, vectors, up_bias_grad, qv_grad = now.grad_down, now.grad_up, now.vectors, now.up_bias_grad, now.qv_grad
    grad_att = aa.total()
    block, stream_grad = now.block, now.stream_grad

    return (
        block,
        stream_grad,
        vectors[:kinds],
        vectors[kinds + 4],
        vectors[kinds + 5],
        grad_att[:, : 3 * head_cols].reshape(share, 3, head_cols),
        qv_grad,
        grad_att[:, 3 * head_cols :].T,
        vectors[kinds + 0],
        vectors[kinds + 1],
        vectors[kinds + 2],
        grad_up,
        up_bias_grad,
        grad_down.T,
        vectors[kinds + 3],
    )


def solution(mesh):
    placed = (
        P(DP, None),
        P(DP),
        P(DP),
        P(),
        P(),
        P(),
        P(None, None, MP),
        P(None, MP),
        P(MP, None),
        P(),
        P(),
        P(),
        P(None, MP),
        P(MP),
        P(MP, None),
        P(),
        P(DP, None),
    )
    return jax.shard_map(
        on_device,
        mesh=mesh,
        in_specs=placed,
        out_specs=(
            P((DP, MP), None),
            P((DP, MP), None),
            P(None, (DP, MP)),
            P((DP, MP)),
            P((DP, MP)),
            P(DP, None, MP),
            P(None, (MP, DP)),
            P(MP, DP),
            P((DP, MP)),
            P((DP, MP)),
            P((DP, MP)),
            P(DP, MP),
            P((MP, DP)),
            P(MP, DP),
            P((DP, MP)),
        ),
        check_vma=False,
    )
```

```python
import functools
import types

import numpy as np
import jax
import jax.numpy as jnp
from jax import lax
from jax.experimental import pallas as pl
from jax.experimental.pallas import tpu as pltpu
from jax.sharding import PartitionSpec as P

HD = 64
DP, MP, PAIR, KEPT = "dp", "mp", "pair", "kept"
ALL, STEP, REST, SCALAR = "all", "step", "rest", "scalar"
EPS = 1e-05
MASKED = -1e30
BF16 = jnp.bfloat16
F32 = jnp.float32


LOG2E = 1.4426950408889634
LN2 = 0.6931471805599453


def layer_norm(rows, gain, shift):
    center = rows - jnp.mean(rows, axis=-1, keepdims=True)
    scale = lax.rsqrt(jnp.mean(center * center, axis=-1, keepdims=True) + EPS)
    normalized = center * scale
    return (normalized * gain + shift, normalized, scale)


def norm_back(grad_out, normalized, scale, gain):
    scaled = grad_out * gain
    first_mean = jnp.mean(scaled, axis=-1, keepdims=True)
    second_mean = jnp.mean(scaled * normalized, axis=-1, keepdims=True)
    return scale * (scaled - first_mean - normalized * second_mean)


def mm(a, b):
    return lax.dot_general(a, b, (((1,), (0,)), ((), ())), preferred_element_type=F32)


def mm_t(a, b):
    return lax.dot_general(a, b, (((1,), (1,)), ((), ())), preferred_element_type=F32)


def start_kernel(across, script_ids, rows_in, rows_out, embed, *refs):
    vectors, (place, stream, low_one, low_out, tail) = refs[:6], refs[6:]
    width = rows_in.shape[1]
    kind = lax.broadcasted_iota(jnp.int32, embed.shape, 0) == script_ids[across[0]]
    added = jnp.sum(jnp.where(kind, embed[...].astype(F32), 0.0), axis=0, keepdims=True)
    table = jnp.concatenate([v[...].reshape(1, width) for v in vectors] + [added, jnp.zeros((1, width), F32)], axis=0)
    order = place[...]
    table = sum(mm(piece, order) for piece in split3(table))
    tail[...] = table
    x = mm(rows_in[...], order) + table[6:7]
    stream[...] = x
    low_one[...] = layer_norm(x, table[4:5], table[5:6])[0].astype(BF16)
    low_out[...] = mm(rows_out[...], order).astype(BF16)


def split3(v):
    high = v.astype(BF16)
    rest = v - high.astype(F32)
    mid = rest.astype(BF16)
    return [high, mid, (rest - mid.astype(F32)).astype(BF16)]


def attention_kernel(cols, has_own, across, lengths, one, *refs):
    own, (low, high, bias, proj_out, lse_out, mixed_out) = (refs[0], refs[1:]) if has_own else (None, refs)
    rows = one.shape[0]
    half = one.shape[1] // 2
    heads = cols // HD

    def body(w0, w1):
        a = one[...]
        p = mm(a[:, :half], w0) + mm(a[:, half:], w1) + bias[0]
        p = p.astype(BF16)
        proj_out[0] = p
        dead = jnp.where(lax.broadcasted_iota(jnp.int32, (rows, 1), 0) < lengths[across[0]], 0.0, MASKED)
        ones = jnp.where(lax.broadcasted_iota(jnp.int32, (rows, HD), 1) == 0, 1.0, 0.0).astype(BF16)
        lse_out[0] = jnp.zeros(lse_out.shape[1:], F32)
        outs = []
        for h in range(heads):
            q, k, v = (p[:, i * cols + h * HD : i * cols + (h + 1) * HD] for i in range(3))
            scores = mm_t(k, q) * (0.125 * LOG2E) + dead
            top = jnp.max(scores, axis=0, keepdims=True)
            expo = jnp.exp2(scores - top).astype(BF16)
            both = mm(jnp.concatenate([v, ones], axis=1).T, expo)
            total = both[HD : HD + 1]
            lse_out[0, h : h + 1] = top + jnp.log2(total)
            outs.append((both[:HD] * (1.0 / total)).T.astype(BF16))
        mixed_out[0] = jnp.concatenate(outs, axis=1)

    run(has_own, body, own, low, high, slice(0, 3 * cols))


def run(has_own, body, own, low, high, cols):
    if has_own:
        half = low.shape[1]

        @pl.when(pl.program_id(0) == 0)
        def _():
            body(own[:half, cols], own[half:, cols])

        @pl.when(pl.program_id(0) > 0)
        def _():
            body(low[0, :, cols], high[0, :, cols])

    else:
        body(low[0, :, cols], high[0, :, cols])


def out_kernel(cols, hidden, mixed_a, mixed_b, x, own, low, high, up_own, up_low, up_high, tail, mid_out, two_out, total):
    step = pl.program_id(0)
    half = x.shape[1] // 2
    one, two = slice(3 * cols, None), slice(hidden, None)

    def body(heads, w0, w1, u0, u1):
        split = w0.shape[1]
        total[:, :half] += mm_t(heads[:, :split], w0) + mm_t(heads[:, split:], u0)
        total[:, half:] += mm_t(heads[:, :split], w1) + mm_t(heads[:, split:], u1)

    @pl.when(step == 0)
    def _():
        total[...] = x[...] + tail[0:1]
        body(mixed_a[0], own[:half, one], own[half:, one], up_own[:half, two], up_own[half:, two])

    @pl.when(step > 0)
    def _():
        body(jnp.where(step < 2, mixed_a[0], mixed_b[0]), low[0, :, one], high[0, :, one], up_low[0, :, two], up_high[0, :, two])

    @pl.when(step == pl.num_programs(0) - 1)
    def _():
        mid = total[...]
        mid_out[...] = mid
        two_out[...] = layer_norm(mid, tail[1:2], tail[2:3])[0].astype(BF16)


def feature_grad(left, right, grad0, grad1, at):
    half = grad0.shape[1]
    out = lax.dot_general(left, right, (((0,), (0,)), ((), ())), preferred_element_type=F32).astype(BF16)
    grad0[0, :, at] = out[:half]
    grad1[0, :, at] = out[half:]


def up_kernel(has_own, two, out_low, *refs):
    own, (low, high, bias, hidden_out, slope_out, grad0, grad1) = (refs[0], refs[1:]) if has_own else (None, refs)
    rows, width = two.shape
    half = width // 2
    cols = hidden_out.shape[2]
    c0, c1 = 0.7978845608028654, 0.7978845608028654 * 0.044715

    def body(w0, w1):
        for at in (slice(0, rows // 2), slice(rows // 2, rows)):
            v = mm(two[at, :half], w0) + mm(two[at, half:], w1) + bias[0]
            square = v * v
            t = jnp.tanh(v * (c0 + c1 * square))
            grow = 0.5 + 0.5 * t
            hidden_out[0, at] = (v * grow).astype(BF16)
            slope_out[0, at] = (grow + v * (0.5 - 0.5 * t * t) * (c0 + 3 * c1 * square)).astype(BF16)
        feature_grad(out_low[...], hidden_out[0], grad0, grad1, slice(0, cols))

    run(has_own, body, own, low, high, slice(0, cols))


def pre_kernel(last, two, out_low, *refs):
    if last:
        (own, low, high, down_own, down_low, down_high, slope, hidden, two_in, block_in, mid, tail), refs = refs[:12], refs[12:]
        grad0, grad1, bias_sum, block_sum, grad_mid_out, low_mid_out, sums, two_sum = refs
    else:
        low, high, down_low, down_high, slope, hidden, grad0, grad1, bias_sum, block_sum, two_sum = refs
    step = pl.program_id(0)
    half = two.shape[1] // 2
    cols = slope.shape[2]
    ours = slice(0, cols)

    @pl.when(step == 0)
    def _():
        two_sum[...] = two_in[...] if last else jnp.zeros(two_sum.shape, F32)
        block_sum[...] = block_in[...] + mid[...] + tail[3:4] if last else jnp.zeros(block_sum.shape, F32)

    def body(w0, w1, d0, d1):
        a = out_low[...]
        grad = ((mm(a[:, :half], d0) + mm(a[:, half:], d1)) * slope[0].astype(F32)).astype(BF16)
        bias_sum[0] = jnp.sum(grad.astype(F32), axis=0, keepdims=True)
        feature_grad(two[...], grad, grad0, grad1, ours)
        two_sum[:, :half] += mm_t(grad, w0)
        two_sum[:, half:] += mm_t(grad, w1)
        block_sum[:, :half] += mm_t(hidden[0], d0)
        block_sum[:, half:] += mm_t(hidden[0], d1)

    if last:

        @pl.when(step == 0)
        def _():
            body(own[:half, ours], own[half:, ours], down_own[:half], down_own[half:])

        @pl.when(step > 0)
        def _():
            body(low[0, :, ours], high[0, :, ours], down_low[0], down_high[0])

        @pl.when(step == pl.num_programs(0) - 1)
        def _():
            grad = two_sum[...]
            _, normalized, scale = layer_norm(mid[...], tail[1:2], tail[2:3])
            rows_out = out_low[...].astype(F32)
            grad_mid = rows_out + norm_back(grad, normalized, scale, tail[1:2])
            low_mid = grad_mid.astype(BF16)
            grad_mid_out[...] = grad_mid
            low_mid_out[...] = low_mid
            sums[0:1] = jnp.sum(low_mid.astype(F32), axis=0, keepdims=True)
            sums[1:2] = jnp.sum(grad * normalized, axis=0, keepdims=True)
            sums[2:3] = jnp.sum(grad, axis=0, keepdims=True)
            sums[3:4] = jnp.sum(rows_out, axis=0, keepdims=True)

    else:
        body(low[0, :, ours], high[0, :, ours], down_low[0], down_high[0])


def attention_back_kernel(cols, hidden, has_own, across, lengths, one, low_mid, *refs):
    own, up_own, refs = (refs[0], refs[1], refs[2:]) if has_own else (None, None, refs)
    low, high, up_low, up_high, proj, mixed, lse, proj_out, grad0, grad1, sums = refs
    rows = one.shape[0]
    half = one.shape[1] // 2
    heads = cols // HD
    first, second = slice(3 * cols, None), slice(hidden, None)

    def body(w0, w1, u0, u1):
        a = low_mid[...]
        grad_mixed = mm(a[:, :half], jnp.concatenate([w0, u0], axis=1)) + mm(a[:, half:], jnp.concatenate([w1, u1], axis=1))
        grad_mixed = grad_mixed.astype(BF16)
        p = proj[0]
        dead = jnp.where(lax.broadcasted_iota(jnp.int32, (rows, 1), 0) < lengths[across[0]], 0.0, MASKED)
        grads = [[], [], []]
        for h in range(heads):
            q, k, v = (p[:, i * cols + h * HD : i * cols + (h + 1) * HD] for i in range(3))
            out = grad_mixed[:, h * HD : (h + 1) * HD]
            probs = jnp.exp2((mm_t(k, q) * (0.125 * LOG2E) + dead) - lse[0, h : h + 1])
            grad_probs = mm_t(v, out)
            inner = jnp.sum(probs * grad_probs, axis=0, keepdims=True)
            grad_scores = (probs * (grad_probs - inner)).astype(BF16)
            grads[2].append(mm(probs.astype(BF16), out).astype(BF16))
            grads[1].append((mm(grad_scores, q) * 0.125).astype(BF16))
            grads[0].append((mm(k.T, grad_scores) * 0.125).T.astype(BF16))
        grad = jnp.concatenate(grads[0] + grads[1] + grads[2], axis=1)
        proj_out[0] = grad
        sums[0] = jnp.sum(grad.astype(F32), axis=0, keepdims=True)
        for left, right, at in ((one, grad, slice(0, 3 * cols)), (low_mid, mixed[0], slice(3 * cols, 4 * cols))):
            out = lax.dot_general(left[...], right, (((0,), (0,)), ((), ())), preferred_element_type=F32).astype(BF16)
            grad0[0, :, at] = out[:half]
            grad1[0, :, at] = out[half:]

    if has_own:

        @pl.when(pl.program_id(0) == 0)
        def _():
            body(own[:half, first], own[half:, first], up_own[:half, second], up_own[half:, second])

        @pl.when(pl.program_id(0) > 0)
        def _():
            body(low[0, :, first], high[0, :, first], up_low[0, :, second], up_high[0, :, second])

    else:
        body(low[0, :, first], high[0, :, first], up_low[0, :, second], up_high[0, :, second])


def unplace(value, place):
    high = value.astype(BF16)
    low = (value - high.astype(F32)).astype(BF16)
    return mm_t(high, place) + mm_t(low, place)


def first_kernel(cols, across, script_ids, mid_sums, grad_a, grad_b, own, low, high, x, grad_mid, tail, rows_out, sums, total):
    step = pl.program_id(0)
    half = x.shape[1] // 2

    @pl.when(step == 0)
    def _():
        total[...] = jnp.zeros(total.shape, F32)

    def body(w0, w1):
        grad = jnp.where(step < 2, grad_a[0], grad_b[0])
        total[:, :half] += mm_t(grad, w0)
        total[:, half:] += mm_t(grad, w1)

    run(True, body, own, low, high, slice(0, 3 * cols))

    @pl.when(step == pl.num_programs(0) - 1)
    def _():
        grad = total[...]
        _, normalized, scale = layer_norm(x[...], tail[4:5], tail[5:6])
        stream = grad_mid[...] + norm_back(grad, normalized, scale, tail[4:5])
        kinds = sums.shape[0] - 8
        kind = lax.broadcasted_iota(jnp.int32, (kinds, 1), 0) == script_ids[across[0]]
        sums[0:kinds] = jnp.where(kind, jnp.sum(stream, axis=0, keepdims=True), 0.0)
        sums[kinds : kinds + 4] = mid_sums[0:4]
        sums[kinds + 4 : kinds + 5] = jnp.sum(grad * normalized, axis=0, keepdims=True)
        sums[kinds + 5 : kinds + 6] = jnp.sum(grad, axis=0, keepdims=True)
        sums[kinds + 6 :] = jnp.zeros((2, sums.shape[1]), F32)
        rows_out[...] = stream


def back_kernel(value, place, rows_out):
    rows_out[...] = unplace(value[...], place[...])[: rows_out.shape[0]]


def blocked(kernel, inputs, outputs, scratch, steps, flops, transcendentals=0, at=0, vmem=20):
    def spec(shape, kind):
        if kind == SCALAR:
            return pl.BlockSpec(memory_space=pltpu.SMEM)
        zeros = (0,) * (len(shape) - 1)
        if kind == ALL:
            return pl.BlockSpec(shape, lambda s: (0,) + zeros, pipeline_mode=pl.Buffered(1))
        back = {STEP: 0, REST: 1 - at}.get(kind, kind)
        return pl.BlockSpec((1,) + shape[1:], lambda s: (jnp.clip(s - back, 0, shape[0] - 1),) + zeros)

    arrays = [a for a, _ in inputs]
    nbytes = sum(a.size * a.dtype.itemsize for a in arrays) + sum(int(np.prod(s)) * jnp.dtype(d).itemsize for s, d, _ in outputs)
    return pl.pallas_call(
        kernel,
        grid=(steps,),
        in_specs=[spec(a.shape, k) for a, k in inputs],
        out_specs=[spec(s, k) for s, _, k in outputs],
        out_shape=[jax.ShapeDtypeStruct(s, d) for s, d, _ in outputs],
        scratch_shapes=scratch,
        compiler_params=pltpu.CompilerParams(dimension_semantics=("arbitrary",), vmem_limit_bytes=vmem * 1024 * 1024),
        cost_estimate=pl.CostEstimate(flops=int(flops), bytes_accessed=nbytes, transcendentals=int(transcendentals)),
    )(*arrays)


CHUNK = 32


class Leaving:
    def __init__(self, bag):
        self._bag = bag

    def __getattr__(self, name):
        return vars(self._bag).pop(name)


class Bag(types.SimpleNamespace):
    @property
    def out(self):
        return Leaving(self)


class Ring:
    def __init__(self, dp, mp):
        self.dp, self.mp = dp, mp
        bits = list(range(1, dp.bit_length() - 1))
        self.orders = (bits, bits[::-1])
        self.stages = [[(i, i ^ (1 << self.orders[i & 1][t])) for i in range(dp)] for t in range(len(bits))]
        cut = (len(self.stages) + 1) // 2
        self.rounds = [self.stages[:cut], self.stages[cut:]]
        self.pair = [(i, i ^ 1) for i in range(dp)]
        self.blocks = [[(i, i ^ (1 << b)) for i in range(mp)] for b in range(mp.bit_length() - 1)][::-1]
        self.block_masks = [0]
        for b in reversed(range(mp.bit_length() - 1)):
            self.block_masks += [m ^ (1 << b) for m in self.block_masks]
        self.direct = [[(i, i ^ m) for i in range(mp)] for m in self.block_masks[1:]]
        halves = []
        for order in self.orders:
            masks = [0]
            for bit in order:
                masks = masks + [m | (1 << bit) for m in masks]
            halves.append(masks)
        self.masks = np.array([halves[0] + [1 ^ m for m in halves[1]], halves[1] + [1 ^ m for m in halves[0]]], np.int32)


class Gather:
    def __init__(self, ring, piece, share, direct=False, near_first=False):
        self.share, self.near_first = share, near_first
        self.v = Bag(held=piece[None])
        blocks = [(MP, ring.direct)] if direct else [(MP, [s]) for s in (ring.blocks[::-1] if near_first else ring.blocks)]
        self.left = blocks + [(DP, g) for g in ring.rounds] + [(PAIR, [ring.pair])]

    def step(self):
        axis, stages = self.left.pop(0)
        if axis == PAIR:
            self.v.high = lax.ppermute(self.v.held, DP, stages[0])
            return
        held = self.v.held
        if len(stages) > 1 and axis == MP:
            self.v.held = jnp.concatenate([lax.ppermute(held, axis, stage) for stage in stages])
            return
        for stage in stages:
            held = jnp.concatenate([held, lax.ppermute(held, axis, stage)], axis=0 if axis == MP else 1)
        if axis == MP and self.left[0][0] != MP:
            if self.near_first:
                held = jnp.concatenate([held[0:1], held[2:3], held[1:2], held[3:]])
            if held.shape[1] > self.share:
                self.v.extra = held[:, self.share :]
            held = held[1:, : self.share]
        self.v.held = held

    def specs(self, own):
        return ([(own, ALL)] if own is not None else []) + [(self.v.held, REST), (self.v.high, REST)]


class Scatter:
    def __init__(self, ring, low_half, high_half):
        self.v = Bag(held=low_half, send=high_half)
        self.axis, self.stage = DP, ring.pair
        self.left = [(DP, 1, group[::-1]) for group in ring.rounds[::-1]]

    def go(self):
        self.v.got = lax.ppermute(self.v.out.send, self.axis, self.stage)

    def add(self, at, size, dim):
        a, b = (lax.slice_in_dim(v, at, at + size, axis=dim).astype(F32) for v in (self.v.held, self.v.got))
        return (a + b).astype(self.v.held.dtype)

    def fold(self):
        self.axis, dim, stages = self.left.pop(0)
        for i, stage in enumerate(stages):
            if i:
                self.go()
            self.stage = stage
            size = self.v.held.shape[dim] // 2
            self.v = Bag(send=self.add(size, size, dim), held=self.add(0, size, dim))

    def settle(self):
        return self.add(0, self.v.held.shape[0], 0)

    def take_rest(self, rest, stage):
        self.v = Bag(held=self.settle(), got=rest)
        self.left = [(MP, 0, [stage])]
        self.fold()

    def total(self):
        return self.v.held[0].astype(F32) + self.v.got[0].astype(F32)


def meet(live, *moving):
    bags = [live] + [m.v for m in moving]
    for bag, values in zip(bags, lax.optimization_barrier([vars(b) for b in bags])):
        vars(bag).update(values)


def meet_kept(moving, *flows):
    kept = Bag(**{KEPT + str(i): f.v.held for i, f in enumerate(flows)})
    meet(kept, moving)
    for f, held in zip(flows, vars(kept).values()):
        f.v.held = held


def on_device(
    patches,
    script_ids,
    lengths,
    script_embed,
    norm1_gain,
    norm1_shift,
    query_key_value_weight,
    b_qv,
    attention_out_weight,
    attention_out_bias,
    norm2_gain,
    norm2_shift,
    up_weight,
    up_proj_bias,
    down_weight,
    down_proj_bias,
    out_grad,
):
    dp, mp = lax.axis_size(DP), lax.axis_size(MP)
    ring = Ring(dp, mp)
    here, across = lax.axis_index(DP), lax.axis_index(MP)
    rows_all, width = patches.shape
    rows = rows_all // mp
    share = width // dp
    head_cols = query_key_value_weight.shape[2]
    hidden_cols = up_weight.shape[1]
    heads = head_cols // HD
    kinds = script_embed.shape[0]

    order = jnp.where((here & 1) == 0, ring.masks[0], ring.masks[1]) ^ here
    source = (order[:, None] * share + jnp.arange(share, dtype=jnp.int32)[None, :]).reshape(width)
    place = (lax.broadcasted_iota(jnp.int32, (width, width), 0) == source[None, :]).astype(BF16)
    mine = (
        lax.broadcasted_iota(jnp.int32, (share, width), 1) == here * share + lax.broadcasted_iota(jnp.int32, (share, width), 0)
    ).astype(BF16)

    def take(rows_of, block, features):
        out = lax.dot_general(rows_of, block, (((1,), (features,)), ((), ())), preferred_element_type=F32)
        return out.astype(BF16)

    def put(v):
        parts = jnp.concatenate(split3(v), axis=0)
        return sum(jnp.split(jnp.dot(parts, place, preferred_element_type=F32), 3))

    qkv_cols = 3 * head_cols
    behind = -qkv_cols % 128
    att_own = query_key_value_weight.reshape(width, qkv_cols)
    out_a, out_b = attention_out_weight[:behind], attention_out_weight[behind:]
    up_cols = hidden_cols + head_cols - behind
    zeros = jnp.zeros((head_cols,), F32)
    spare = jnp.zeros((up_cols - qkv_cols,), F32)
    flat = jnp.concatenate([b_qv[0], zeros, b_qv[1], spare, up_proj_bias, jnp.zeros((up_cols - hidden_cols,), F32)]).reshape(2, up_cols)
    bias_rows = jnp.concatenate(split3(flat))
    bias_rows = jnp.pad(bias_rows, ((0, -bias_rows.shape[0] % 16), (0, 0)))

    padded = -(-rows // CHUNK) * CHUNK
    grow = ((0, padded - rows), (0, 0))
    real_rows, rows = rows, padded
    vmem = pltpu.VMEM
    dense = 2 * rows * width
    live = 2 * mp * heads * rows * rows * HD
    part = mp // 2
    which = across.reshape(1)

    q = Gather(ring, jnp.concatenate([take(mine, att_own, 0), take(mine, out_a, 1)], axis=1), share, direct=True)
    q.step()
    up_piece = jnp.concatenate([take(mine, up_weight, 0), take(mine, out_b, 1)], axis=1)
    now = Bag(
        up=jnp.concatenate([up_piece, bias_rows]),
        rows=jnp.pad(lax.dynamic_slice_in_dim(patches, across * real_rows, real_rows, 0), grow),
        cotangent=jnp.pad(lax.dynamic_slice_in_dim(out_grad, across * real_rows, real_rows, 0), grow),
        place=place,
    )
    meet(now, q)
    u = Gather(ring, now.out.up, share)
    q.step()
    u.step()
    now.down = take(mine, down_weight, 1)
    now.stream, now.one, now.out_low, now.tail = blocked(
        start_kernel,
        [(which, SCALAR), (script_ids, SCALAR), (now.out.rows, ALL), (now.out.cotangent, ALL), (script_embed, ALL)]
        + [(v, ALL) for v in (attention_out_bias, norm2_gain, norm2_shift, down_proj_bias, norm1_gain, norm1_shift)]
        + [(now.place, ALL)],
        [((rows, width), F32, ALL), ((rows, width), BF16, ALL), ((rows, width), BF16, ALL), ((8, width), F32, ALL)],
        [],
        1,
        2 * dense * width,
    )
    meet(now, q, u)
    q.step()
    u.step()
    now.own_att = jnp.concatenate([take(now.place.T, att_own, 0), take(now.place.T, out_a, 1)], axis=1)
    meet(now, q, u)
    n = Gather(ring, now.out.down, share, near_first=True)
    bias_all = u.v.out.extra.astype(F32)
    bias_all = bias_all[:, 0:2] + bias_all[:, 2:4] + bias_all[:, 4:6]
    now.qkv_bias = bias_all[:, 0:1, :qkv_cols]
    now.up_bias = bias_all[:, 1:2, :hidden_cols]
    q.step()
    u.step()
    n.step()
    meet(now, q, u, n)
    u.step()
    n.step()

    def attention(at, own):
        return blocked(
            functools.partial(attention_kernel, head_cols, at == 0),
            [(which, SCALAR), (lengths, SCALAR), (now.one, ALL)] + q.specs(own) + [(now.qkv_bias, -at)],
            [((part, rows, qkv_cols), BF16, STEP), ((part, 8, rows), F32, STEP), ((part, rows, head_cols), BF16, STEP)],
            [],
            part,
            (dense * mp * qkv_cols + 2 * live) // 2,
            mp * heads * rows * rows // 2,
            at=at,
        )

    now.proj_b, now.lse_b, now.mixed_b = attention(part, None)
    now.proj_a, now.lse_a, now.mixed_a = attention(0, now.own_att)
    meet(now, q, u, n)
    u.step()
    n.step()
    order_t = now.place.T
    now.own_up = jnp.concatenate([take(order_t, up_weight, 0), take(order_t, out_b, 1)], axis=1)
    now.own_down = take(order_t, down_weight, 1)
    meet(now, q, u, n)
    n.step()
    now.middle, now.two = blocked(
        functools.partial(out_kernel, head_cols, hidden_cols),
        [(now.mixed_a, STEP), (now.mixed_b, part), (now.stream, ALL)]
        + q.specs(now.own_att) + u.specs(now.own_up) + [(now.tail, ALL)],
        [((rows, width), F32, ALL), ((rows, width), BF16, ALL)],
        [vmem((rows, width), F32)],
        mp,
        dense * mp * head_cols,
    )

    def half_shape(cols):
        return ((part, width // 2, cols), BF16, STEP)

    hidden_shape = ((part, rows, hidden_cols), BF16, STEP)

    def up_part(at, own):
        hidden, slope, low_half, high_half = blocked(
            functools.partial(up_kernel, at == 0),
            [(now.two, ALL), (now.out_low, ALL)] + u.specs(own) + [(now.up_bias, -at)],
            [hidden_shape, hidden_shape, half_shape(hidden_cols), half_shape(hidden_cols)],
            [],
            part,
            2 * dense * part * hidden_cols,
            rows * part * hidden_cols,
            at=at,
        )
        return hidden, slope, Scatter(ring, low_half, high_half)

    def pre_part(at, own_up, own_down, more, outputs, scratch):
        return blocked(
            functools.partial(pre_kernel, at == 0),
            [(now.two, ALL), (now.out_low, ALL)] + u.specs(own_up) + n.specs(own_down) + more,
            [half_shape(hidden_cols), half_shape(hidden_cols), ((part, 1, hidden_cols), F32, STEP), ((rows, width), F32, ALL)] + outputs,
            scratch,
            part,
            4 * dense * part * hidden_cols,
            at=at,
        )

    now.hidden_b, now.slope_b, cb = up_part(part, None)
    meet(now, q, u, n, cb)
    n.step()
    cb.go()
    now.hidden_a, now.slope_a, ca = up_part(0, now.own_up)
    meet(now, q, u, n, ca, cb)
    cb.fold()
    cb.go()
    ca.go()
    low_half, high_half, now.up_sum_b, now.block, now.two_sum = pre_part(
        part, None, None, [(now.out.slope_b, STEP), (now.out.hidden_b, STEP)], [((rows, width), F32, ALL)], []
    )
    bb = Scatter(ring, low_half, high_half)
    meet(now, q, u, n, ca, cb, bb)
    for each in (ca, cb):
        each.fold()
        each.go()
    bb.go()
    low_half, high_half, now.up_sum_a, now.block, now.grad_mid, now.mid, now.mid_sums = pre_part(
        0,
        now.own_up,
        now.out.own_down,
        [(now.out.slope_a, STEP), (now.out.hidden_a, STEP), (now.out.two_sum, ALL), (now.out.block, ALL), (now.out.middle, ALL), (now.tail, ALL)],
        [((rows, width), F32, ALL), ((rows, width), BF16, ALL), ((8, width), F32, ALL)],
        [vmem((rows, width), F32)],
    )
    ba = Scatter(ring, low_half, high_half)
    meet(now, q, u, ca, cb, ba, bb)
    for each in (bb, ca):
        each.fold()
        each.go()
    ba.go()
    rest_c = lax.ppermute(cb.settle(), MP, ring.blocks[-1])

    def attention_back(at, own, made):
        own_att, own_up = own
        q_specs, u_specs = q.specs(own_att), u.specs(own_up)
        weights = q_specs[:1] + u_specs[:1] + q_specs[1:] + u_specs[1:] if at == 0 else q_specs + u_specs
        return blocked(
            functools.partial(attention_back_kernel, head_cols, hidden_cols, at == 0),
            [(which, SCALAR), (lengths, SCALAR), (now.one, ALL), (now.mid, ALL)] + weights
            + [(a, STEP) for a in made],
            [((part, rows, qkv_cols), BF16, STEP), half_shape(4 * head_cols), half_shape(4 * head_cols), ((part, 1, qkv_cols), F32, STEP)],
            [],
            part,
            (dense * mp * 5 * head_cols + 5 * live) // 2,
            mp * heads * rows * rows // 2,
            at=at,
        )

    now.grad_b, low_half, high_half, now.proj_sum_b = attention_back(part, (None, None), (now.out.proj_b, now.out.mixed_b, now.out.lse_b))
    ab = Scatter(ring, low_half, high_half)
    now.rest_c = rest_c
    meet(now, q, u, ca, ba, bb, ab)
    for each in (ba, bb):
        each.fold()
        each.go()
    ab.go()
    ca.take_rest(now.out.rest_c, ring.blocks[0])
    ca.go()
    now.grad_a, low_half, high_half, now.proj_sum_a = attention_back(
        0, (now.own_att, now.out.own_up), (now.out.proj_a, now.out.mixed_a, now.out.lse_a)
    )
    aa = Scatter(ring, low_half, high_half)
    meet(now, q, ca, ba, bb, ab, aa)
    def back(value):
        return blocked(back_kernel, [(value, ALL), (now.place, ALL)], [((real_rows, width), F32, ALL)], [], 1, 2 * dense * width)[0]

    aa.go()
    ab.fold()
    ab.go()
    ba.fold()
    ba.go()
    rest_b = lax.ppermute(bb.settle(), MP, ring.blocks[-1])
    now.block = back(now.block)
    now.rest_b = rest_b
    meet(now, q, aa, ab, ba, ca)
    for each in (aa, ab):
        each.fold()
        each.go()
    ba.take_rest(now.out.rest_b, ring.blocks[0])
    ba.go()
    now.stream_grad, now.sums = blocked(
        functools.partial(first_kernel, head_cols),
        [(which, SCALAR), (script_ids, SCALAR), (now.out.mid_sums, ALL), (now.out.grad_a, STEP), (now.out.grad_b, part)]
        + q.specs(now.out.own_att)
        + [(a, ALL) for a in (now.out.stream, now.out.grad_mid, now.out.tail)],
        [((rows, width), F32, ALL), ((kinds + 8, width), F32, ALL)],
        [vmem((rows, width), F32)],
        mp,
        dense * mp * qkv_cols,
        vmem=60,
    )
    meet(now, aa, ab, ba, ca)

    n_vec = kinds + 8
    sub = head_cols // dp
    proj_sum = jnp.concatenate([now.out.proj_sum_a, now.out.proj_sum_b]).reshape(mp, 3, head_cols)
    qv = jnp.stack([proj_sum[:, 0], proj_sum[:, 2]], axis=1).reshape(mp * 2, dp, sub)
    qv = jnp.pad(qv, ((0, 0), (0, 0), (0, share - sub))).reshape(mp * 2, width)
    up_sum = jnp.concatenate([now.out.up_sum_a, now.out.up_sum_b])[:, 0]
    parts = jnp.concatenate(split3(jnp.concatenate([up_sum, qv], axis=0)), axis=0)
    cols = sum(jnp.split(jnp.dot(parts, now.place, preferred_element_type=F32), 3))
    small = jnp.concatenate([now.out.sums, cols], axis=0).T[None]
    ss = Scatter(ring, small[:, : width // 2], small[:, width // 2 :])
    ss.go()
    aa.fold()
    aa.go()
    rest_a = lax.ppermute(ab.settle(), MP, ring.blocks[-1])
    meet_kept(ss, aa)
    ss.fold()
    ss.go()
    kept = Bag(up=ba.total())
    meet(kept, ss)
    now.grad_up = kept.up
    ss.fold()
    ss.go()
    now.stream_grad = back(now.stream_grad)
    del now.place
    now.grad_down = ca.total()
    now.rest_a = rest_a
    meet(now, aa, ss)
    ss.v = Bag(held=ss.settle())
    ss.v.got = lax.ppermute(ss.v.held, MP, ring.blocks[0])
    aa.take_rest(now.out.rest_a, ring.blocks[0])
    aa.go()
    grad_down, grad_up = now.grad_down, now.grad_up
    meet_kept(ss, aa)
    parts = jnp.concatenate([ss.v.held, ss.v.got])
    parts = jnp.concatenate([parts, lax.ppermute(parts, MP, ring.blocks[1])])
    vectors = sum(p[:, :n_vec] for p in parts)
    vectors = lax.dynamic_slice_in_dim(vectors, across * (share // mp), share // mp, 0).T
    up_bias_grad = sum(p[:, n_vec + i] for i, p in enumerate(parts))
    qv_grad = sum(p[:sub, n_vec + mp + 2 * i : n_vec + mp + 2 * i + 2] for i, p in enumerate(parts)).T
    grad_att = aa.total()
    block, stream_grad = now.block, now.stream_grad

    return (
        block,
        stream_grad,
        vectors[:kinds],
        vectors[kinds + 4],
        vectors[kinds + 5],
        grad_att[:, : 3 * head_cols].reshape(share, 3, head_cols),
        qv_grad,
        grad_att[:, 3 * head_cols :].T,
        vectors[kinds + 0],
        vectors[kinds + 1],
        vectors[kinds + 2],
        grad_up,
        up_bias_grad,
        grad_down.T,
        vectors[kinds + 3],
    )


def solution(mesh):
    placed = (
        P(DP, None),
        P(DP),
        P(DP),
        P(),
        P(),
        P(),
        P(None, None, MP),
        P(None, MP),
        P(MP, None),
        P(),
        P(),
        P(),
        P(None, MP),
        P(MP),
        P(MP, None),
        P(),
        P(DP, None),
    )
    return jax.shard_map(
        on_device,
        mesh=mesh,
        in_specs=placed,
        out_specs=(
            P((DP, MP), None),
            P((DP, MP), None),
            P(None, (DP, MP)),
            P((DP, MP)),
            P((DP, MP)),
            P(DP, None, MP),
            P(None, (MP, DP)),
            P(MP, DP),
            P((DP, MP)),
            P((DP, MP)),
            P((DP, MP)),
            P(DP, MP),
            P((MP, DP)),
            P(MP, DP),
            P((DP, MP)),
        ),
        check_vma=False,
    )
```

```python
import functools
import types

import numpy as np
import jax
import jax.numpy as jnp
from jax import lax
from jax.experimental import pallas as pl
from jax.experimental.pallas import tpu as pltpu
from jax.sharding import PartitionSpec as P

HD = 64
DP, MP, PAIR, KEPT = "dp", "mp", "pair", "kept"
ALL, STEP, REST, SCALAR = "all", "step", "rest", "scalar"
EPS = 1e-05
MASKED = -1e30
BF16 = jnp.bfloat16
F32 = jnp.float32


LOG2E = 1.4426950408889634
LN2 = 0.6931471805599453


def layer_norm(rows, gain, shift):
    center = rows - jnp.mean(rows, axis=-1, keepdims=True)
    scale = lax.rsqrt(jnp.mean(center * center, axis=-1, keepdims=True) + EPS)
    normalized = center * scale
    return (normalized * gain + shift, normalized, scale)


def norm_back(grad_out, normalized, scale, gain):
    scaled = grad_out * gain
    first_mean = jnp.mean(scaled, axis=-1, keepdims=True)
    second_mean = jnp.mean(scaled * normalized, axis=-1, keepdims=True)
    return scale * (scaled - first_mean - normalized * second_mean)


def mm(a, b):
    return lax.dot_general(a, b, (((1,), (0,)), ((), ())), preferred_element_type=F32)


def mm_t(a, b):
    return lax.dot_general(a, b, (((1,), (1,)), ((), ())), preferred_element_type=F32)


def start_kernel(across, script_ids, rows_in, rows_out, embed, *refs):
    vectors, (place, stream, low_one, low_out, tail) = refs[:6], refs[6:]
    width = rows_in.shape[1]
    kind = lax.broadcasted_iota(jnp.int32, embed.shape, 0) == script_ids[across[0]]
    added = jnp.sum(jnp.where(kind, embed[...].astype(F32), 0.0), axis=0, keepdims=True)
    table = jnp.concatenate([v[...].reshape(1, width) for v in vectors] + [added, jnp.zeros((1, width), F32)], axis=0)
    order = place[...]
    table = sum(mm(piece, order) for piece in split3(table))
    tail[...] = table
    x = mm(rows_in[...], order) + table[6:7]
    stream[...] = x
    low_one[...] = layer_norm(x, table[4:5], table[5:6])[0].astype(BF16)
    low_out[...] = mm(rows_out[...], order).astype(BF16)


def split3(v):
    high = v.astype(BF16)
    rest = v - high.astype(F32)
    mid = rest.astype(BF16)
    return [high, mid, (rest - mid.astype(F32)).astype(BF16)]


def attention_kernel(cols, has_own, across, lengths, one, *refs):
    own, (low, high, bias, proj_out, lse_out, mixed_out) = (refs[0], refs[1:]) if has_own else (None, refs)
    rows = one.shape[0]
    half = one.shape[1] // 2
    heads = cols // HD

    def body(w0, w1):
        a = one[...]
        p = mm(a[:, :half], w0) + mm(a[:, half:], w1) + bias[0]
        p = p.astype(BF16)
        proj_out[0] = p
        dead = jnp.where(lax.broadcasted_iota(jnp.int32, (rows, 1), 0) < lengths[across[0]], 0.0, MASKED)
        ones = jnp.where(lax.broadcasted_iota(jnp.int32, (rows, HD), 1) == 0, 1.0, 0.0).astype(BF16)
        lse_out[0] = jnp.zeros(lse_out.shape[1:], F32)
        outs = []
        for h in range(heads):
            q, k, v = (p[:, i * cols + h * HD : i * cols + (h + 1) * HD] for i in range(3))
            scores = mm_t(k, q) * (0.125 * LOG2E) + dead
            top = jnp.max(scores, axis=0, keepdims=True)
            expo = jnp.exp2(scores - top).astype(BF16)
            both = mm(jnp.concatenate([v, ones], axis=1).T, expo)
            total = both[HD : HD + 1]
            lse_out[0, h : h + 1] = top + jnp.log2(total)
            outs.append((both[:HD] * (1.0 / total)).T.astype(BF16))
        mixed_out[0] = jnp.concatenate(outs, axis=1)

    run(has_own, body, own, low, high, slice(0, 3 * cols))


def run(has_own, body, own, low, high, cols):
    if has_own:
        half = low.shape[1]

        @pl.when(pl.program_id(0) == 0)
        def _():
            body(own[:half, cols], own[half:, cols])

        @pl.when(pl.program_id(0) > 0)
        def _():
            body(low[0, :, cols], high[0, :, cols])

    else:
        body(low[0, :, cols], high[0, :, cols])


def out_kernel(cols, hidden, mixed_a, mixed_b, x, own, low, high, up_own, up_low, up_high, tail, mid_out, two_out, total):
    step = pl.program_id(0)
    half = x.shape[1] // 2
    one, two = slice(3 * cols, None), slice(hidden, None)

    def body(heads, w0, w1, u0, u1):
        split = w0.shape[1]
        total[:, :half] += mm_t(heads[:, :split], w0) + mm_t(heads[:, split:], u0)
        total[:, half:] += mm_t(heads[:, :split], w1) + mm_t(heads[:, split:], u1)

    @pl.when(step == 0)
    def _():
        total[...] = x[...] + tail[0:1]
        body(mixed_a[0], own[:half, one], own[half:, one], up_own[:half, two], up_own[half:, two])

    @pl.when(step > 0)
    def _():
        body(jnp.where(step < 2, mixed_a[0], mixed_b[0]), low[0, :, one], high[0, :, one], up_low[0, :, two], up_high[0, :, two])

    @pl.when(step == pl.num_programs(0) - 1)
    def _():
        mid = total[...]
        mid_out[...] = mid
        two_out[...] = layer_norm(mid, tail[1:2], tail[2:3])[0].astype(BF16)


def feature_grad(left, right, grad0, grad1, at):
    half = grad0.shape[1]
    out = lax.dot_general(left, right, (((0,), (0,)), ((), ())), preferred_element_type=F32).astype(BF16)
    grad0[0, :, at] = out[:half]
    grad1[0, :, at] = out[half:]


def up_kernel(has_own, two, out_low, *refs):
    own, (low, high, bias, hidden_out, slope_out, grad0, grad1) = (refs[0], refs[1:]) if has_own else (None, refs)
    rows, width = two.shape
    half = width // 2
    cols = hidden_out.shape[2]
    c0, c1 = 0.7978845608028654, 0.7978845608028654 * 0.044715

    def body(w0, w1):
        for at in (slice(0, rows // 2), slice(rows // 2, rows)):
            v = mm(two[at, :half], w0) + mm(two[at, half:], w1) + bias[0]
            square = v * v
            t = jnp.tanh(v * (c0 + c1 * square))
            grow = 0.5 + 0.5 * t
            hidden_out[0, at] = (v * grow).astype(BF16)
            slope_out[0, at] = (grow + v * (0.5 - 0.5 * t * t) * (c0 + 3 * c1 * square)).astype(BF16)
        feature_grad(out_low[...], hidden_out[0], grad0, grad1, slice(0, cols))

    run(has_own, body, own, low, high, slice(0, cols))


def pre_kernel(last, two, out_low, *refs):
    if last:
        (own, low, high, down_own, down_low, down_high, slope, hidden, two_in, block_in, mid, tail), refs = refs[:12], refs[12:]
        grad0, grad1, bias_sum, block_sum, grad_mid_out, low_mid_out, sums, two_sum = refs
    else:
        low, high, down_low, down_high, slope, hidden, grad0, grad1, bias_sum, block_sum, two_sum = refs
    step = pl.program_id(0)
    half = two.shape[1] // 2
    cols = slope.shape[2]
    ours = slice(0, cols)

    @pl.when(step == 0)
    def _():
        two_sum[...] = two_in[...] if last else jnp.zeros(two_sum.shape, F32)
        block_sum[...] = block_in[...] + mid[...] + tail[3:4] if last else jnp.zeros(block_sum.shape, F32)

    def body(w0, w1, d0, d1):
        a = out_low[...]
        grad = ((mm(a[:, :half], d0) + mm(a[:, half:], d1)) * slope[0].astype(F32)).astype(BF16)
        bias_sum[0] = jnp.sum(grad.astype(F32), axis=0, keepdims=True)
        feature_grad(two[...], grad, grad0, grad1, ours)
        two_sum[:, :half] += mm_t(grad, w0)
        two_sum[:, half:] += mm_t(grad, w1)
        block_sum[:, :half] += mm_t(hidden[0], d0)
        block_sum[:, half:] += mm_t(hidden[0], d1)

    if last:

        @pl.when(step == 0)
        def _():
            body(own[:half, ours], own[half:, ours], down_own[:half], down_own[half:])

        @pl.when(step > 0)
        def _():
            body(low[0, :, ours], high[0, :, ours], down_low[0], down_high[0])

        @pl.when(step == pl.num_programs(0) - 1)
        def _():
            grad = two_sum[...]
            _, normalized, scale = layer_norm(mid[...], tail[1:2], tail[2:3])
            rows_out = out_low[...].astype(F32)
            grad_mid = rows_out + norm_back(grad, normalized, scale, tail[1:2])
            low_mid = grad_mid.astype(BF16)
            grad_mid_out[...] = grad_mid
            low_mid_out[...] = low_mid
            sums[0:1] = jnp.sum(low_mid.astype(F32), axis=0, keepdims=True)
            sums[1:2] = jnp.sum(grad * normalized, axis=0, keepdims=True)
            sums[2:3] = jnp.sum(grad, axis=0, keepdims=True)
            sums[3:4] = jnp.sum(rows_out, axis=0, keepdims=True)

    else:
        body(low[0, :, ours], high[0, :, ours], down_low[0], down_high[0])


def attention_back_kernel(cols, hidden, has_own, across, lengths, one, low_mid, *refs):
    own, up_own, refs = (refs[0], refs[1], refs[2:]) if has_own else (None, None, refs)
    low, high, up_low, up_high, proj, mixed, lse, proj_out, grad0, grad1, sums = refs
    rows = one.shape[0]
    half = one.shape[1] // 2
    heads = cols // HD
    first, second = slice(3 * cols, None), slice(hidden, None)

    def body(w0, w1, u0, u1):
        a = low_mid[...]
        grad_mixed = mm(a[:, :half], jnp.concatenate([w0, u0], axis=1)) + mm(a[:, half:], jnp.concatenate([w1, u1], axis=1))
        grad_mixed = grad_mixed.astype(BF16)
        p = proj[0]
        dead = jnp.where(lax.broadcasted_iota(jnp.int32, (rows, 1), 0) < lengths[across[0]], 0.0, MASKED)
        grads = [[], [], []]
        for h in range(heads):
            q, k, v = (p[:, i * cols + h * HD : i * cols + (h + 1) * HD] for i in range(3))
            out = grad_mixed[:, h * HD : (h + 1) * HD]
            probs = jnp.exp2((mm_t(k, q) * (0.125 * LOG2E) + dead) - lse[0, h : h + 1])
            grad_probs = mm_t(v, out)
            inner = jnp.sum(probs * grad_probs, axis=0, keepdims=True)
            grad_scores = (probs * (grad_probs - inner)).astype(BF16)
            grads[2].append(mm(probs.astype(BF16), out).astype(BF16))
            grads[1].append((mm(grad_scores, q) * 0.125).astype(BF16))
            grads[0].append((mm(k.T, grad_scores) * 0.125).T.astype(BF16))
        grad = jnp.concatenate(grads[0] + grads[1] + grads[2], axis=1)
        proj_out[0] = grad
        sums[0] = jnp.sum(grad.astype(F32), axis=0, keepdims=True)
        for left, right, at in ((one, grad, slice(0, 3 * cols)), (low_mid, mixed[0], slice(3 * cols, 4 * cols))):
            out = lax.dot_general(left[...], right, (((0,), (0,)), ((), ())), preferred_element_type=F32).astype(BF16)
            grad0[0, :, at] = out[:half]
            grad1[0, :, at] = out[half:]

    if has_own:

        @pl.when(pl.program_id(0) == 0)
        def _():
            body(own[:half, first], own[half:, first], up_own[:half, second], up_own[half:, second])

        @pl.when(pl.program_id(0) > 0)
        def _():
            body(low[0, :, first], high[0, :, first], up_low[0, :, second], up_high[0, :, second])

    else:
        body(low[0, :, first], high[0, :, first], up_low[0, :, second], up_high[0, :, second])


def unplace(value, place):
    high = value.astype(BF16)
    low = (value - high.astype(F32)).astype(BF16)
    return mm_t(high, place) + mm_t(low, place)


def first_kernel(cols, across, script_ids, mid_sums, grad_a, grad_b, own, low, high, x, grad_mid, tail, rows_out, sums, total):
    step = pl.program_id(0)
    half = x.shape[1] // 2

    @pl.when(step == 0)
    def _():
        total[...] = jnp.zeros(total.shape, F32)

    def body(w0, w1):
        grad = jnp.where(step < 2, grad_a[0], grad_b[0])
        total[:, :half] += mm_t(grad, w0)
        total[:, half:] += mm_t(grad, w1)

    run(True, body, own, low, high, slice(0, 3 * cols))

    @pl.when(step == pl.num_programs(0) - 1)
    def _():
        grad = total[...]
        _, normalized, scale = layer_norm(x[...], tail[4:5], tail[5:6])
        stream = grad_mid[...] + norm_back(grad, normalized, scale, tail[4:5])
        kinds = sums.shape[0] - 8
        kind = lax.broadcasted_iota(jnp.int32, (kinds, 1), 0) == script_ids[across[0]]
        sums[0:kinds] = jnp.where(kind, jnp.sum(stream, axis=0, keepdims=True), 0.0)
        sums[kinds : kinds + 4] = mid_sums[0:4]
        sums[kinds + 4 : kinds + 5] = jnp.sum(grad * normalized, axis=0, keepdims=True)
        sums[kinds + 5 : kinds + 6] = jnp.sum(grad, axis=0, keepdims=True)
        sums[kinds + 6 :] = jnp.zeros((2, sums.shape[1]), F32)
        rows_out[...] = stream


def back_kernel(value, place, rows_out):
    rows_out[...] = unplace(value[...], place[...])[: rows_out.shape[0]]


def blocked(kernel, inputs, outputs, scratch, steps, flops, transcendentals=0, at=0, vmem=20):
    def spec(shape, kind):
        if kind == SCALAR:
            return pl.BlockSpec(memory_space=pltpu.SMEM)
        zeros = (0,) * (len(shape) - 1)
        if kind == ALL:
            return pl.BlockSpec(shape, lambda s: (0,) + zeros, pipeline_mode=pl.Buffered(1))
        back = {STEP: 0, REST: 1 - at}.get(kind, kind)
        return pl.BlockSpec((1,) + shape[1:], lambda s: (jnp.clip(s - back, 0, shape[0] - 1),) + zeros)

    arrays = [a for a, _ in inputs]
    nbytes = sum(a.size * a.dtype.itemsize for a in arrays) + sum(int(np.prod(s)) * jnp.dtype(d).itemsize for s, d, _ in outputs)
    return pl.pallas_call(
        kernel,
        grid=(steps,),
        in_specs=[spec(a.shape, k) for a, k in inputs],
        out_specs=[spec(s, k) for s, _, k in outputs],
        out_shape=[jax.ShapeDtypeStruct(s, d) for s, d, _ in outputs],
        scratch_shapes=scratch,
        compiler_params=pltpu.CompilerParams(dimension_semantics=("arbitrary",), vmem_limit_bytes=vmem * 1024 * 1024),
        cost_estimate=pl.CostEstimate(flops=int(flops), bytes_accessed=nbytes, transcendentals=int(transcendentals)),
    )(*arrays)


CHUNK = 32


class Leaving:
    def __init__(self, bag):
        self._bag = bag

    def __getattr__(self, name):
        return vars(self._bag).pop(name)


class Bag(types.SimpleNamespace):
    @property
    def out(self):
        return Leaving(self)


class Ring:
    def __init__(self, dp, mp):
        self.dp, self.mp = dp, mp
        bits = list(range(1, dp.bit_length() - 1))
        self.orders = (bits, bits[::-1])
        self.stages = [[(i, i ^ (1 << self.orders[i & 1][t])) for i in range(dp)] for t in range(len(bits))]
        cut = (len(self.stages) + 1) // 2
        self.rounds = [self.stages[:cut], self.stages[cut:]]
        self.pair = [(i, i ^ 1) for i in range(dp)]
        self.blocks = [[(i, i ^ (1 << b)) for i in range(mp)] for b in range(mp.bit_length() - 1)][::-1]
        self.block_masks = [0]
        for b in reversed(range(mp.bit_length() - 1)):
            self.block_masks += [m ^ (1 << b) for m in self.block_masks]
        self.direct = [[(i, i ^ m) for i in range(mp)] for m in self.block_masks[1:]]
        halves = []
        for order in self.orders:
            masks = [0]
            for bit in order:
                masks = masks + [m | (1 << bit) for m in masks]
            halves.append(masks)
        self.masks = np.array([halves[0] + [1 ^ m for m in halves[1]], halves[1] + [1 ^ m for m in halves[0]]], np.int32)


class Gather:
    def __init__(self, ring, piece, share, direct=False, near_first=False):
        self.share, self.near_first = share, near_first
        self.v = Bag(held=piece[None])
        blocks = [(MP, ring.direct)] if direct else [(MP, [s]) for s in (ring.blocks[::-1] if near_first else ring.blocks)]
        self.left = blocks + [(DP, g) for g in ring.rounds] + [(PAIR, [ring.pair])]

    def step(self):
        axis, stages = self.left.pop(0)
        if axis == PAIR:
            self.v.high = lax.ppermute(self.v.held, DP, stages[0])
            return
        held = self.v.held
        if len(stages) > 1 and axis == MP:
            self.v.held = jnp.concatenate([lax.ppermute(held, axis, stage) for stage in stages])
            return
        for stage in stages:
            held = jnp.concatenate([held, lax.ppermute(held, axis, stage)], axis=0 if axis == MP else 1)
        if axis == MP and self.left[0][0] != MP:
            if self.near_first:
                held = jnp.concatenate([held[0:1], held[2:3], held[1:2], held[3:]])
            if held.shape[1] > self.share:
                self.v.extra = held[:, self.share :]
            held = held[1:, : self.share]
        self.v.held = held

    def specs(self, own):
        return ([(own, ALL)] if own is not None else []) + [(self.v.held, REST), (self.v.high, REST)]


class Scatter:
    def __init__(self, ring, low_half, high_half):
        self.v = Bag(held=low_half, send=high_half)
        self.axis, self.stage = DP, ring.pair
        self.left = [(DP, 1, group[::-1]) for group in ring.rounds[::-1]]

    def go(self):
        self.v.got = lax.ppermute(self.v.out.send, self.axis, self.stage)

    def add(self, at, size, dim):
        a, b = (lax.slice_in_dim(v, at, at + size, axis=dim).astype(F32) for v in (self.v.held, self.v.got))
        return (a + b).astype(self.v.held.dtype)

    def fold(self):
        self.axis, dim, stages = self.left.pop(0)
        for i, stage in enumerate(stages):
            if i:
                self.go()
            self.stage = stage
            size = self.v.held.shape[dim] // 2
            self.v = Bag(send=self.add(size, size, dim), held=self.add(0, size, dim))

    def settle(self):
        return self.add(0, self.v.held.shape[0], 0)

    def take_rest(self, rest, stage):
        self.v = Bag(held=self.settle(), got=rest)
        self.left = [(MP, 0, [stage])]
        self.fold()

    def total(self):
        return self.v.held[0].astype(F32) + self.v.got[0].astype(F32)


def meet(live, *moving):
    bags = [live] + [m.v for m in moving]
    for bag, values in zip(bags, lax.optimization_barrier([vars(b) for b in bags])):
        vars(bag).update(values)


def meet_kept(moving, *flows):
    kept = Bag(**{KEPT + str(i): f.v.held for i, f in enumerate(flows)})
    meet(kept, moving)
    for f, held in zip(flows, vars(kept).values()):
        f.v.held = held


def on_device(
    patches,
    script_ids,
    lengths,
    script_embed,
    norm1_gain,
    norm1_shift,
    query_key_value_weight,
    b_qv,
    attention_out_weight,
    attention_out_bias,
    norm2_gain,
    norm2_shift,
    up_weight,
    up_proj_bias,
    down_weight,
    down_proj_bias,
    out_grad,
):
    dp, mp = lax.axis_size(DP), lax.axis_size(MP)
    ring = Ring(dp, mp)
    here, across = lax.axis_index(DP), lax.axis_index(MP)
    rows_all, width = patches.shape
    rows = rows_all // mp
    share = width // dp
    head_cols = query_key_value_weight.shape[2]
    hidden_cols = up_weight.shape[1]
    heads = head_cols // HD
    kinds = script_embed.shape[0]

    order = jnp.where((here & 1) == 0, ring.masks[0], ring.masks[1]) ^ here
    source = (order[:, None] * share + jnp.arange(share, dtype=jnp.int32)[None, :]).reshape(width)
    place = (lax.broadcasted_iota(jnp.int32, (width, width), 0) == source[None, :]).astype(BF16)
    mine = (
        lax.broadcasted_iota(jnp.int32, (share, width), 1) == here * share + lax.broadcasted_iota(jnp.int32, (share, width), 0)
    ).astype(BF16)

    def take(rows_of, block, features):
        out = lax.dot_general(rows_of, block, (((1,), (features,)), ((), ())), preferred_element_type=F32)
        return out.astype(BF16)

    def put(v):
        parts = jnp.concatenate(split3(v), axis=0)
        return sum(jnp.split(jnp.dot(parts, place, preferred_element_type=F32), 3))

    qkv_cols = 3 * head_cols
    behind = -qkv_cols % 128
    att_own = query_key_value_weight.reshape(width, qkv_cols)
    out_a, out_b = attention_out_weight[:behind], attention_out_weight[behind:]
    up_cols = hidden_cols + head_cols - behind
    zeros = jnp.zeros((head_cols,), F32)
    spare = jnp.zeros((up_cols - qkv_cols,), F32)
    flat = jnp.concatenate([b_qv[0], zeros, b_qv[1], spare, up_proj_bias, jnp.zeros((up_cols - hidden_cols,), F32)]).reshape(2, up_cols)
    bias_rows = jnp.concatenate(split3(flat))
    bias_rows = jnp.pad(bias_rows, ((0, -bias_rows.shape[0] % 16), (0, 0)))

    padded = -(-rows // CHUNK) * CHUNK
    grow = ((0, padded - rows), (0, 0))
    real_rows, rows = rows, padded
    vmem = pltpu.VMEM
    dense = 2 * rows * width
    live = 2 * mp * heads * rows * rows * HD
    part = mp // 2
    which = across.reshape(1)

    q = Gather(ring, jnp.concatenate([take(mine, att_own, 0), take(mine, out_a, 1)], axis=1), share, direct=True)
    q.step()
    up_piece = jnp.concatenate([take(mine, up_weight, 0), take(mine, out_b, 1)], axis=1)
    now = Bag(
        up=jnp.concatenate([up_piece, bias_rows]),
        rows=jnp.pad(lax.dynamic_slice_in_dim(patches, across * real_rows, real_rows, 0), grow),
        cotangent=jnp.pad(lax.dynamic_slice_in_dim(out_grad, across * real_rows, real_rows, 0), grow),
        place=place,
    )
    meet(now, q)
    u = Gather(ring, now.out.up, share)
    q.step()
    u.step()
    now.down = take(mine, down_weight, 1)
    now.stream, now.one, now.out_low, now.tail = blocked(
        start_kernel,
        [(which, SCALAR), (script_ids, SCALAR), (now.out.rows, ALL), (now.out.cotangent, ALL), (script_embed, ALL)]
        + [(v, ALL) for v in (attention_out_bias, norm2_gain, norm2_shift, down_proj_bias, norm1_gain, norm1_shift)]
        + [(now.place, ALL)],
        [((rows, width), F32, ALL), ((rows, width), BF16, ALL), ((rows, width), BF16, ALL), ((8, width), F32, ALL)],
        [],
        1,
        2 * dense * width,
    )
    meet(now, q, u)
    q.step()
    u.step()
    now.own_att = jnp.concatenate([take(now.place.T, att_own, 0), take(now.place.T, out_a, 1)], axis=1)
    meet(now, q, u)
    n = Gather(ring, now.out.down, share, near_first=True)
    bias_all = u.v.out.extra.astype(F32)
    bias_all = bias_all[:, 0:2] + bias_all[:, 2:4] + bias_all[:, 4:6]
    now.qkv_bias = bias_all[:, 0:1, :qkv_cols]
    now.up_bias = bias_all[:, 1:2, :hidden_cols]
    q.step()
    u.step()
    n.step()
    meet(now, q, u, n)
    u.step()
    n.step()

    def attention(at, own):
        return blocked(
            functools.partial(attention_kernel, head_cols, at == 0),
            [(which, SCALAR), (lengths, SCALAR), (now.one, ALL)] + q.specs(own) + [(now.qkv_bias, -at)],
            [((part, rows, qkv_cols), BF16, STEP), ((part, 8, rows), F32, STEP), ((part, rows, head_cols), BF16, STEP)],
            [],
            part,
            (dense * mp * qkv_cols + 2 * live) // 2,
            mp * heads * rows * rows // 2,
            at=at,
        )

    now.proj_b, now.lse_b, now.mixed_b = attention(part, None)
    now.proj_a, now.lse_a, now.mixed_a = attention(0, now.own_att)
    meet(now, q, u, n)
    u.step()
    n.step()
    order_t = now.place.T
    now.own_up = jnp.concatenate([take(order_t, up_weight, 0), take(order_t, out_b, 1)], axis=1)
    now.own_down = take(order_t, down_weight, 1)
    meet(now, q, u, n)
    n.step()
    now.middle, now.two = blocked(
        functools.partial(out_kernel, head_cols, hidden_cols),
        [(now.mixed_a, STEP), (now.mixed_b, part), (now.stream, ALL)]
        + q.specs(now.own_att) + u.specs(now.own_up) + [(now.tail, ALL)],
        [((rows, width), F32, ALL), ((rows, width), BF16, ALL)],
        [vmem((rows, width), F32)],
        mp,
        dense * mp * head_cols,
    )

    def half_shape(cols):
        return ((part, width // 2, cols), BF16, STEP)

    hidden_shape = ((part, rows, hidden_cols), BF16, STEP)

    def up_part(at, own):
        hidden, slope, low_half, high_half = blocked(
            functools.partial(up_kernel, at == 0),
            [(now.two, ALL), (now.out_low, ALL)] + u.specs(own) + [(now.up_bias, -at)],
            [hidden_shape, hidden_shape, half_shape(hidden_cols), half_shape(hidden_cols)],
            [],
            part,
            2 * dense * part * hidden_cols,
            rows * part * hidden_cols,
            at=at,
        )
        return hidden, slope, Scatter(ring, low_half, high_half)

    def pre_part(at, own_up, own_down, more, outputs, scratch):
        return blocked(
            functools.partial(pre_kernel, at == 0),
            [(now.two, ALL), (now.out_low, ALL)] + u.specs(own_up) + n.specs(own_down) + more,
            [half_shape(hidden_cols), half_shape(hidden_cols), ((part, 1, hidden_cols), F32, STEP), ((rows, width), F32, ALL)] + outputs,
            scratch,
            part,
            4 * dense * part * hidden_cols,
            at=at,
        )

    now.hidden_b, now.slope_b, cb = up_part(part, None)
    meet(now, q, u, n, cb)
    n.step()
    cb.go()
    now.hidden_a, now.slope_a, ca = up_part(0, now.own_up)
    meet(now, q, u, n, ca, cb)
    cb.fold()
    cb.go()
    ca.go()
    low_half, high_half, now.up_sum_b, now.block, now.two_sum = pre_part(
        part, None, None, [(now.out.slope_b, STEP), (now.out.hidden_b, STEP)], [((rows, width), F32, ALL)], []
    )
    bb = Scatter(ring, low_half, high_half)
    meet(now, q, u, n, ca, cb, bb)
    for each in (ca, cb):
        each.fold()
        each.go()
    bb.go()
    low_half, high_half, now.up_sum_a, now.block, now.grad_mid, now.mid, now.mid_sums = pre_part(
        0,
        now.own_up,
        now.out.own_down,
        [(now.out.slope_a, STEP), (now.out.hidden_a, STEP), (now.out.two_sum, ALL), (now.out.block, ALL), (now.out.middle, ALL), (now.tail, ALL)],
        [((rows, width), F32, ALL), ((rows, width), BF16, ALL), ((8, width), F32, ALL)],
        [vmem((rows, width), F32)],
    )
    ba = Scatter(ring, low_half, high_half)
    meet(now, q, u, ca, cb, ba, bb)
    for each in (bb, ca):
        each.fold()
        each.go()
    ba.go()
    rest_c = lax.ppermute(cb.settle(), MP, ring.blocks[-1])

    def attention_back(at, own, made):
        own_att, own_up = own
        q_specs, u_specs = q.specs(own_att), u.specs(own_up)
        weights = q_specs[:1] + u_specs[:1] + q_specs[1:] + u_specs[1:] if at == 0 else q_specs + u_specs
        return blocked(
            functools.partial(attention_back_kernel, head_cols, hidden_cols, at == 0),
            [(which, SCALAR), (lengths, SCALAR), (now.one, ALL), (now.mid, ALL)] + weights
            + [(a, STEP) for a in made],
            [((part, rows, qkv_cols), BF16, STEP), half_shape(4 * head_cols), half_shape(4 * head_cols), ((part, 1, qkv_cols), F32, STEP)],
            [],
            part,
            (dense * mp * 5 * head_cols + 5 * live) // 2,
            mp * heads * rows * rows // 2,
            at=at,
        )

    now.grad_b, low_half, high_half, now.proj_sum_b = attention_back(part, (None, None), (now.out.proj_b, now.out.mixed_b, now.out.lse_b))
    ab = Scatter(ring, low_half, high_half)
    now.rest_c = rest_c
    meet(now, q, u, ca, ba, bb, ab)
    for each in (ba, bb):
        each.fold()
        each.go()
    ab.go()
    ca.take_rest(now.out.rest_c, ring.blocks[0])
    ca.go()
    now.grad_a, low_half, high_half, now.proj_sum_a = attention_back(
        0, (now.own_att, now.out.own_up), (now.out.proj_a, now.out.mixed_a, now.out.lse_a)
    )
    aa = Scatter(ring, low_half, high_half)
    meet(now, q, ca, ba, bb, ab, aa)
    def back(value):
        return blocked(back_kernel, [(value, ALL), (now.place, ALL)], [((real_rows, width), F32, ALL)], [], 1, 2 * dense * width)[0]

    aa.go()
    ab.fold()
    ab.go()
    ba.fold()
    ba.go()
    rest_b = lax.ppermute(bb.settle(), MP, ring.blocks[-1])
    now.block = back(now.block)
    now.rest_b = rest_b
    meet(now, q, aa, ab, ba, ca)
    for each in (aa, ab):
        each.fold()
        each.go()
    ba.take_rest(now.out.rest_b, ring.blocks[0])
    ba.go()
    now.stream_grad, now.sums = blocked(
        functools.partial(first_kernel, head_cols),
        [(which, SCALAR), (script_ids, SCALAR), (now.out.mid_sums, ALL), (now.out.grad_a, STEP), (now.out.grad_b, part)]
        + q.specs(now.out.own_att)
        + [(a, ALL) for a in (now.out.stream, now.out.grad_mid, now.out.tail)],
        [((rows, width), F32, ALL), ((kinds + 8, width), F32, ALL)],
        [vmem((rows, width), F32)],
        mp,
        dense * mp * qkv_cols,
        vmem=60,
    )
    meet(now, aa, ab, ba, ca)

    n_vec = kinds + 8
    sub = head_cols // dp
    proj_sum = jnp.concatenate([now.out.proj_sum_a, now.out.proj_sum_b]).reshape(mp, 3, head_cols)
    qv = jnp.stack([proj_sum[:, 0], proj_sum[:, 2]], axis=1).reshape(mp * 2, dp, sub)
    qv = jnp.pad(qv, ((0, 0), (0, 0), (0, share - sub))).reshape(mp * 2, width)
    up_sum = jnp.concatenate([now.out.up_sum_a, now.out.up_sum_b])[:, 0]
    parts = jnp.concatenate(split3(jnp.concatenate([up_sum, qv], axis=0)), axis=0)
    cols = sum(jnp.split(jnp.dot(parts, now.place, preferred_element_type=F32), 3))
    small = jnp.concatenate([now.out.sums, cols], axis=0).T[None]
    ss = Scatter(ring, small[:, : width // 2], small[:, width // 2 :])
    ss.go()
    aa.fold()
    aa.go()
    rest_a = lax.ppermute(ab.settle(), MP, ring.blocks[-1])
    meet_kept(ss, aa)
    ss.fold()
    ss.go()
    kept = Bag(up=ba.total())
    meet(kept, ss)
    now.grad_up = kept.up
    ss.fold()
    ss.go()
    now.stream_grad = back(now.stream_grad)
    del now.place
    now.grad_down = ca.total()
    now.rest_a = rest_a
    meet(now, aa, ss)
    aa.take_rest(now.out.rest_a, ring.blocks[0])
    aa.go()
    sums = ss.settle()
    last = Bag(parts=[sums] + [lax.ppermute(sums, MP, stage) for stage in ring.direct])
    grad_down, grad_up = now.grad_down, now.grad_up
    meet(last, aa)
    parts = [p[0] for p in last.parts]
    vectors = sum(p[:, :n_vec] for p in parts)
    vectors = lax.dynamic_slice_in_dim(vectors, across * (share // mp), share // mp, 0).T
    up_bias_grad = sum(p[:, n_vec + i] for i, p in enumerate(parts))
    qv_grad = sum(p[:sub, n_vec + mp + 2 * i : n_vec + mp + 2 * i + 2] for i, p in enumerate(parts)).T
    grad_att = aa.total()
    block, stream_grad = now.block, now.stream_grad

    return (
        block,
        stream_grad,
        vectors[:kinds],
        vectors[kinds + 4],
        vectors[kinds + 5],
        grad_att[:, : 3 * head_cols].reshape(share, 3, head_cols),
        qv_grad,
        grad_att[:, 3 * head_cols :].T,
        vectors[kinds + 0],
        vectors[kinds + 1],
        vectors[kinds + 2],
        grad_up,
        up_bias_grad,
        grad_down.T,
        vectors[kinds + 3],
    )


def solution(mesh):
    placed = (
        P(DP, None),
        P(DP),
        P(DP),
        P(),
        P(),
        P(),
        P(None, None, MP),
        P(None, MP),
        P(MP, None),
        P(),
        P(),
        P(),
        P(None, MP),
        P(MP),
        P(MP, None),
        P(),
        P(DP, None),
    )
    return jax.shard_map(
        on_device,
        mesh=mesh,
        in_specs=placed,
        out_specs=(
            P((DP, MP), None),
            P((DP, MP), None),
            P(None, (DP, MP)),
            P((DP, MP)),
            P((DP, MP)),
            P(DP, None, MP),
            P(None, (MP, DP)),
            P(MP, DP),
            P((DP, MP)),
            P((DP, MP)),
            P((DP, MP)),
            P(DP, MP),
            P((MP, DP)),
            P(MP, DP),
            P((DP, MP)),
        ),
        check_vma=False,
    )
```

```python
import functools
import types

import numpy as np
import jax
import jax.numpy as jnp
from jax import lax
from jax.experimental import pallas as pl
from jax.experimental.pallas import tpu as pltpu
from jax.sharding import PartitionSpec as P

HD = 64
DP, MP, PAIR, KEPT = "dp", "mp", "pair", "kept"
ALL, STEP, REST, SCALAR = "all", "step", "rest", "scalar"
EPS = 1e-05
MASKED = -1e30
BF16 = jnp.bfloat16
F32 = jnp.float32


LOG2E = 1.4426950408889634
LN2 = 0.6931471805599453


def layer_norm(rows, gain, shift):
    center = rows - jnp.mean(rows, axis=-1, keepdims=True)
    scale = lax.rsqrt(jnp.mean(center * center, axis=-1, keepdims=True) + EPS)
    normalized = center * scale
    return (normalized * gain + shift, normalized, scale)


def norm_back(grad_out, normalized, scale, gain):
    scaled = grad_out * gain
    first_mean = jnp.mean(scaled, axis=-1, keepdims=True)
    second_mean = jnp.mean(scaled * normalized, axis=-1, keepdims=True)
    return scale * (scaled - first_mean - normalized * second_mean)


def mm(a, b):
    return lax.dot_general(a, b, (((1,), (0,)), ((), ())), preferred_element_type=F32)


def mm_t(a, b):
    return lax.dot_general(a, b, (((1,), (1,)), ((), ())), preferred_element_type=F32)


def start_kernel(across, script_ids, rows_in, rows_out, embed, *refs):
    vectors, (place, stream, low_one, low_out, tail) = refs[:6], refs[6:]
    width = rows_in.shape[1]
    kind = lax.broadcasted_iota(jnp.int32, embed.shape, 0) == script_ids[across[0]]
    added = jnp.sum(jnp.where(kind, embed[...].astype(F32), 0.0), axis=0, keepdims=True)
    table = jnp.concatenate([v[...].reshape(1, width) for v in vectors] + [added, jnp.zeros((1, width), F32)], axis=0)
    order = place[...]
    table = sum(mm(piece, order) for piece in split3(table))
    tail[...] = table
    x = mm(rows_in[...], order) + table[6:7]
    stream[...] = x
    low_one[...] = layer_norm(x, table[4:5], table[5:6])[0].astype(BF16)
    low_out[...] = mm(rows_out[...], order).astype(BF16)


def split3(v):
    high = v.astype(BF16)
    rest = v - high.astype(F32)
    mid = rest.astype(BF16)
    return [high, mid, (rest - mid.astype(F32)).astype(BF16)]


def attention_kernel(cols, has_own, across, lengths, one, *refs):
    own, (low, high, bias, proj_out, lse_out, mixed_out) = (refs[0], refs[1:]) if has_own else (None, refs)
    rows = one.shape[0]
    half = one.shape[1] // 2
    heads = cols // HD

    def body(w0, w1):
        a = one[...]
        p = mm(a[:, :half], w0) + mm(a[:, half:], w1) + bias[0]
        p = p.astype(BF16)
        proj_out[0] = p
        dead = jnp.where(lax.broadcasted_iota(jnp.int32, (rows, 1), 0) < lengths[across[0]], 0.0, MASKED)
        ones = jnp.where(lax.broadcasted_iota(jnp.int32, (rows, HD), 1) == 0, 1.0, 0.0).astype(BF16)
        lse_out[0] = jnp.zeros(lse_out.shape[1:], F32)
        outs = []
        for h in range(heads):
            q, k, v = (p[:, i * cols + h * HD : i * cols + (h + 1) * HD] for i in range(3))
            scores = mm_t(k, q) * (0.125 * LOG2E) + dead
            top = jnp.max(scores, axis=0, keepdims=True)
            expo = jnp.exp2(scores - top).astype(BF16)
            both = mm(jnp.concatenate([v, ones], axis=1).T, expo)
            total = both[HD : HD + 1]
            lse_out[0, h : h + 1] = top + jnp.log2(total)
            outs.append((both[:HD] * (1.0 / total)).T.astype(BF16))
        mixed_out[0] = jnp.concatenate(outs, axis=1)

    run(has_own, body, own, low, high, slice(0, 3 * cols))


def run(has_own, body, own, low, high, cols):
    if has_own:
        half = low.shape[1]

        @pl.when(pl.program_id(0) == 0)
        def _():
            body(own[:half, cols], own[half:, cols])

        @pl.when(pl.program_id(0) > 0)
        def _():
            body(low[0, :, cols], high[0, :, cols])

    else:
        body(low[0, :, cols], high[0, :, cols])


def out_kernel(cols, hidden, mixed_a, mixed_b, x, own, low, high, up_own, up_low, up_high, tail, mid_out, two_out, total):
    step = pl.program_id(0)
    half = x.shape[1] // 2
    one, two = slice(3 * cols, None), slice(hidden, None)

    def body(heads, w0, w1, u0, u1):
        split = w0.shape[1]
        total[:, :half] += mm_t(heads[:, :split], w0) + mm_t(heads[:, split:], u0)
        total[:, half:] += mm_t(heads[:, :split], w1) + mm_t(heads[:, split:], u1)

    @pl.when(step == 0)
    def _():
        total[...] = x[...] + tail[0:1]
        body(mixed_a[0], own[:half, one], own[half:, one], up_own[:half, two], up_own[half:, two])

    @pl.when(step > 0)
    def _():
        body(jnp.where(step < 2, mixed_a[0], mixed_b[0]), low[0, :, one], high[0, :, one], up_low[0, :, two], up_high[0, :, two])

    @pl.when(step == pl.num_programs(0) - 1)
    def _():
        mid = total[...]
        mid_out[...] = mid
        two_out[...] = layer_norm(mid, tail[1:2], tail[2:3])[0].astype(BF16)


def feature_grad(left, right, grad0, grad1, at):
    half = grad0.shape[1]
    out = lax.dot_general(left, right, (((0,), (0,)), ((), ())), preferred_element_type=F32).astype(BF16)
    grad0[0, :, at] = out[:half]
    grad1[0, :, at] = out[half:]


def up_kernel(has_own, two, out_low, *refs):
    own, (low, high, bias, hidden_out, slope_out, grad0, grad1) = (refs[0], refs[1:]) if has_own else (None, refs)
    rows, width = two.shape
    half = width // 2
    cols = hidden_out.shape[2]
    c0, c1 = 0.7978845608028654, 0.7978845608028654 * 0.044715

    def body(w0, w1):
        for at in (slice(0, rows // 2), slice(rows // 2, rows)):
            v = mm(two[at, :half], w0) + mm(two[at, half:], w1) + bias[0]
            square = v * v
            t = jnp.tanh(v * (c0 + c1 * square))
            grow = 0.5 + 0.5 * t
            hidden_out[0, at] = (v * grow).astype(BF16)
            slope_out[0, at] = (grow + v * (0.5 - 0.5 * t * t) * (c0 + 3 * c1 * square)).astype(BF16)
        feature_grad(out_low[...], hidden_out[0], grad0, grad1, slice(0, cols))

    run(has_own, body, own, low, high, slice(0, cols))


def pre_kernel(last, two, out_low, *refs):
    if last:
        (own, low, high, down_own, down_low, down_high, slope, hidden, two_in, block_in, mid, tail), refs = refs[:12], refs[12:]
        grad0, grad1, bias_sum, block_sum, grad_mid_out, low_mid_out, sums, two_sum = refs
    else:
        low, high, down_low, down_high, slope, hidden, grad0, grad1, bias_sum, block_sum, two_sum = refs
    step = pl.program_id(0)
    half = two.shape[1] // 2
    cols = slope.shape[2]
    ours = slice(0, cols)

    @pl.when(step == 0)
    def _():
        two_sum[...] = two_in[...] if last else jnp.zeros(two_sum.shape, F32)
        block_sum[...] = block_in[...] + mid[...] + tail[3:4] if last else jnp.zeros(block_sum.shape, F32)

    def body(w0, w1, d0, d1):
        a = out_low[...]
        grad = ((mm(a[:, :half], d0) + mm(a[:, half:], d1)) * slope[0].astype(F32)).astype(BF16)
        bias_sum[0] = jnp.sum(grad.astype(F32), axis=0, keepdims=True)
        feature_grad(two[...], grad, grad0, grad1, ours)
        two_sum[:, :half] += mm_t(grad, w0)
        two_sum[:, half:] += mm_t(grad, w1)
        block_sum[:, :half] += mm_t(hidden[0], d0)
        block_sum[:, half:] += mm_t(hidden[0], d1)

    if last:

        @pl.when(step == 0)
        def _():
            body(own[:half, ours], own[half:, ours], down_own[:half], down_own[half:])

        @pl.when(step > 0)
        def _():
            body(low[0, :, ours], high[0, :, ours], down_low[0], down_high[0])

        @pl.when(step == pl.num_programs(0) - 1)
        def _():
            grad = two_sum[...]
            _, normalized, scale = layer_norm(mid[...], tail[1:2], tail[2:3])
            rows_out = out_low[...].astype(F32)
            grad_mid = rows_out + norm_back(grad, normalized, scale, tail[1:2])
            low_mid = grad_mid.astype(BF16)
            grad_mid_out[...] = grad_mid
            low_mid_out[...] = low_mid
            sums[0:1] = jnp.sum(low_mid.astype(F32), axis=0, keepdims=True)
            sums[1:2] = jnp.sum(grad * normalized, axis=0, keepdims=True)
            sums[2:3] = jnp.sum(grad, axis=0, keepdims=True)
            sums[3:4] = jnp.sum(rows_out, axis=0, keepdims=True)

    else:
        body(low[0, :, ours], high[0, :, ours], down_low[0], down_high[0])


def attention_back_kernel(cols, hidden, has_own, across, lengths, one, low_mid, *refs):
    own, up_own, refs = (refs[0], refs[1], refs[2:]) if has_own else (None, None, refs)
    low, high, up_low, up_high, proj, mixed, lse, proj_out, grad0, grad1, sums = refs
    rows = one.shape[0]
    half = one.shape[1] // 2
    heads = cols // HD
    first, second = slice(3 * cols, None), slice(hidden, None)

    def body(w0, w1, u0, u1):
        a = low_mid[...]
        grad_mixed = mm(a[:, :half], jnp.concatenate([w0, u0], axis=1)) + mm(a[:, half:], jnp.concatenate([w1, u1], axis=1))
        grad_mixed = grad_mixed.astype(BF16)
        p = proj[0]
        dead = jnp.where(lax.broadcasted_iota(jnp.int32, (rows, 1), 0) < lengths[across[0]], 0.0, MASKED)
        grads = [[], [], []]
        for h in range(heads):
            q, k, v = (p[:, i * cols + h * HD : i * cols + (h + 1) * HD] for i in range(3))
            out = grad_mixed[:, h * HD : (h + 1) * HD]
            probs = jnp.exp2((mm_t(k, q) * (0.125 * LOG2E) + dead) - lse[0, h : h + 1])
            grad_probs = mm_t(v, out)
            inner = jnp.sum(probs * grad_probs, axis=0, keepdims=True)
            grad_scores = (probs * (grad_probs - inner)).astype(BF16)
            grads[2].append(mm(probs.astype(BF16), out).astype(BF16))
            grads[1].append((mm(grad_scores, q) * 0.125).astype(BF16))
            grads[0].append((mm(k.T, grad_scores) * 0.125).T.astype(BF16))
        grad = jnp.concatenate(grads[0] + grads[1] + grads[2], axis=1)
        proj_out[0] = grad
        sums[0] = jnp.sum(grad.astype(F32), axis=0, keepdims=True)
        for left, right, at in ((one, grad, slice(0, 3 * cols)), (low_mid, mixed[0], slice(3 * cols, 4 * cols))):
            out = lax.dot_general(left[...], right, (((0,), (0,)), ((), ())), preferred_element_type=F32).astype(BF16)
            grad0[0, :, at] = out[:half]
            grad1[0, :, at] = out[half:]

    if has_own:

        @pl.when(pl.program_id(0) == 0)
        def _():
            body(own[:half, first], own[half:, first], up_own[:half, second], up_own[half:, second])

        @pl.when(pl.program_id(0) > 0)
        def _():
            body(low[0, :, first], high[0, :, first], up_low[0, :, second], up_high[0, :, second])

    else:
        body(low[0, :, first], high[0, :, first], up_low[0, :, second], up_high[0, :, second])


def unplace(value, place):
    high = value.astype(BF16)
    low = (value - high.astype(F32)).astype(BF16)
    return mm_t(high, place) + mm_t(low, place)


def first_kernel(cols, across, script_ids, mid_sums, grad_a, grad_b, own, low, high, x, grad_mid, tail, rows_out, sums, total):
    step = pl.program_id(0)
    half = x.shape[1] // 2

    @pl.when(step == 0)
    def _():
        total[...] = jnp.zeros(total.shape, F32)

    def body(w0, w1):
        grad = jnp.where(step < 2, grad_a[0], grad_b[0])
        total[:, :half] += mm_t(grad, w0)
        total[:, half:] += mm_t(grad, w1)

    run(True, body, own, low, high, slice(0, 3 * cols))

    @pl.when(step == pl.num_programs(0) - 1)
    def _():
        grad = total[...]
        _, normalized, scale = layer_norm(x[...], tail[4:5], tail[5:6])
        stream = grad_mid[...] + norm_back(grad, normalized, scale, tail[4:5])
        kinds = sums.shape[0] - 8
        kind = lax.broadcasted_iota(jnp.int32, (kinds, 1), 0) == script_ids[across[0]]
        sums[0:kinds] = jnp.where(kind, jnp.sum(stream, axis=0, keepdims=True), 0.0)
        sums[kinds : kinds + 4] = mid_sums[0:4]
        sums[kinds + 4 : kinds + 5] = jnp.sum(grad * normalized, axis=0, keepdims=True)
        sums[kinds + 5 : kinds + 6] = jnp.sum(grad, axis=0, keepdims=True)
        sums[kinds + 6 :] = jnp.zeros((2, sums.shape[1]), F32)
        rows_out[...] = stream


def back_kernel(value, place, rows_out):
    rows_out[...] = unplace(value[...], place[...])[: rows_out.shape[0]]


def blocked(kernel, inputs, outputs, scratch, steps, flops, transcendentals=0, at=0, vmem=20):
    def spec(shape, kind):
        if kind == SCALAR:
            return pl.BlockSpec(memory_space=pltpu.SMEM)
        zeros = (0,) * (len(shape) - 1)
        if kind == ALL:
            return pl.BlockSpec(shape, lambda s: (0,) + zeros, pipeline_mode=pl.Buffered(1))
        back = {STEP: 0, REST: 1 - at}.get(kind, kind)
        return pl.BlockSpec((1,) + shape[1:], lambda s: (jnp.clip(s - back, 0, shape[0] - 1),) + zeros)

    arrays = [a for a, _ in inputs]
    nbytes = sum(a.size * a.dtype.itemsize for a in arrays) + sum(int(np.prod(s)) * jnp.dtype(d).itemsize for s, d, _ in outputs)
    return pl.pallas_call(
        kernel,
        grid=(steps,),
        in_specs=[spec(a.shape, k) for a, k in inputs],
        out_specs=[spec(s, k) for s, _, k in outputs],
        out_shape=[jax.ShapeDtypeStruct(s, d) for s, d, _ in outputs],
        scratch_shapes=scratch,
        compiler_params=pltpu.CompilerParams(dimension_semantics=("arbitrary",), vmem_limit_bytes=vmem * 1024 * 1024),
        cost_estimate=pl.CostEstimate(flops=int(flops), bytes_accessed=nbytes, transcendentals=int(transcendentals)),
    )(*arrays)


CHUNK = 32


class Leaving:
    def __init__(self, bag):
        self._bag = bag

    def __getattr__(self, name):
        return vars(self._bag).pop(name)


class Bag(types.SimpleNamespace):
    @property
    def out(self):
        return Leaving(self)


class Ring:
    def __init__(self, dp, mp):
        self.dp, self.mp = dp, mp
        bits = list(range(1, dp.bit_length() - 1))
        self.orders = (bits, bits[::-1])
        self.stages = [[(i, i ^ (1 << self.orders[i & 1][t])) for i in range(dp)] for t in range(len(bits))]
        cut = (len(self.stages) + 1) // 2
        self.rounds = [self.stages[:cut], self.stages[cut:]]
        self.pair = [(i, i ^ 1) for i in range(dp)]
        self.blocks = [[(i, i ^ (1 << b)) for i in range(mp)] for b in range(mp.bit_length() - 1)][::-1]
        self.block_masks = [0]
        for b in reversed(range(mp.bit_length() - 1)):
            self.block_masks += [m ^ (1 << b) for m in self.block_masks]
        self.direct = [[(i, i ^ m) for i in range(mp)] for m in self.block_masks[1:]]
        halves = []
        for order in self.orders:
            masks = [0]
            for bit in order:
                masks = masks + [m | (1 << bit) for m in masks]
            halves.append(masks)
        self.masks = np.array([halves[0] + [1 ^ m for m in halves[1]], halves[1] + [1 ^ m for m in halves[0]]], np.int32)


class Gather:
    def __init__(self, ring, piece, share, direct=False, near_first=False):
        self.share, self.near_first = share, near_first
        self.v = Bag(held=piece[None])
        blocks = [(MP, ring.direct)] if direct else [(MP, [s]) for s in (ring.blocks[::-1] if near_first else ring.blocks)]
        self.left = blocks + [(DP, g) for g in ring.rounds] + [(PAIR, [ring.pair])]

    def step(self):
        axis, stages = self.left.pop(0)
        if axis == PAIR:
            self.v.high = lax.ppermute(self.v.held, DP, stages[0])
            return
        held = self.v.held
        if len(stages) > 1 and axis == MP:
            self.v.held = jnp.concatenate([lax.ppermute(held, axis, stage) for stage in stages])
            return
        for stage in stages:
            held = jnp.concatenate([held, lax.ppermute(held, axis, stage)], axis=0 if axis == MP else 1)
        if axis == MP and self.left[0][0] != MP:
            if self.near_first:
                held = jnp.concatenate([held[0:1], held[2:3], held[1:2], held[3:]])
            if held.shape[1] > self.share:
                self.v.extra = held[:, self.share :]
            held = held[1:, : self.share]
        self.v.held = held

    def specs(self, own):
        return ([(own, ALL)] if own is not None else []) + [(self.v.held, REST), (self.v.high, REST)]


class Scatter:
    def __init__(self, ring, low_half, high_half):
        self.v = Bag(held=low_half, send=high_half)
        self.axis, self.stage = DP, ring.pair
        self.left = [(DP, 1, group[::-1]) for group in ring.rounds[::-1]]

    def go(self):
        self.v.got = lax.ppermute(self.v.out.send, self.axis, self.stage)

    def add(self, at, size, dim):
        a, b = (lax.slice_in_dim(v, at, at + size, axis=dim).astype(F32) for v in (self.v.held, self.v.got))
        return (a + b).astype(self.v.held.dtype)

    def fold(self):
        self.axis, dim, stages = self.left.pop(0)
        for i, stage in enumerate(stages):
            if i:
                self.go()
            self.stage = stage
            size = self.v.held.shape[dim] // 2
            self.v = Bag(send=self.add(size, size, dim), held=self.add(0, size, dim))

    def settle(self):
        return self.add(0, self.v.held.shape[0], 0)

    def take_rest(self, rest, stage):
        self.v = Bag(held=self.settle(), got=rest)
        self.left = [(MP, 0, [stage])]
        self.fold()

    def total(self):
        return self.v.held[0].astype(F32) + self.v.got[0].astype(F32)


def meet(live, *moving):
    bags = [live] + [m.v for m in moving]
    for bag, values in zip(bags, lax.optimization_barrier([vars(b) for b in bags])):
        vars(bag).update(values)


def meet_kept(moving, *flows):
    kept = Bag(**{KEPT + str(i): f.v.held for i, f in enumerate(flows)})
    meet(kept, moving)
    for f, held in zip(flows, vars(kept).values()):
        f.v.held = held


def on_device(
    patches,
    script_ids,
    lengths,
    script_embed,
    norm1_gain,
    norm1_shift,
    query_key_value_weight,
    b_qv,
    attention_out_weight,
    attention_out_bias,
    norm2_gain,
    norm2_shift,
    up_weight,
    up_proj_bias,
    down_weight,
    down_proj_bias,
    out_grad,
):
    dp, mp = lax.axis_size(DP), lax.axis_size(MP)
    ring = Ring(dp, mp)
    here, across = lax.axis_index(DP), lax.axis_index(MP)
    rows_all, width = patches.shape
    rows = rows_all // mp
    share = width // dp
    head_cols = query_key_value_weight.shape[2]
    hidden_cols = up_weight.shape[1]
    heads = head_cols // HD
    kinds = script_embed.shape[0]

    order = jnp.where((here & 1) == 0, ring.masks[0], ring.masks[1]) ^ here
    source = (order[:, None] * share + jnp.arange(share, dtype=jnp.int32)[None, :]).reshape(width)
    place = (lax.broadcasted_iota(jnp.int32, (width, width), 0) == source[None, :]).astype(BF16)
    mine = (
        lax.broadcasted_iota(jnp.int32, (share, width), 1) == here * share + lax.broadcasted_iota(jnp.int32, (share, width), 0)
    ).astype(BF16)

    def take(rows_of, block, features):
        out = lax.dot_general(rows_of, block, (((1,), (features,)), ((), ())), preferred_element_type=F32)
        return out.astype(BF16)

    def put(v):
        parts = jnp.concatenate(split3(v), axis=0)
        return sum(jnp.split(jnp.dot(parts, place, preferred_element_type=F32), 3))

    qkv_cols = 3 * head_cols
    behind = -qkv_cols % 128
    att_own = query_key_value_weight.reshape(width, qkv_cols)
    out_a, out_b = attention_out_weight[:behind], attention_out_weight[behind:]
    up_cols = hidden_cols + head_cols - behind
    zeros = jnp.zeros((head_cols,), F32)
    spare = jnp.zeros((up_cols - qkv_cols,), F32)
    flat = jnp.concatenate([b_qv[0], zeros, b_qv[1], spare, up_proj_bias, jnp.zeros((up_cols - hidden_cols,), F32)]).reshape(2, up_cols)
    bias_rows = jnp.concatenate(split3(flat))
    bias_rows = jnp.pad(bias_rows, ((0, -bias_rows.shape[0] % 16), (0, 0)))

    padded = -(-rows // CHUNK) * CHUNK
    grow = ((0, padded - rows), (0, 0))
    real_rows, rows = rows, padded
    vmem = pltpu.VMEM
    dense = 2 * rows * width
    live = 2 * mp * heads * rows * rows * HD
    part = mp // 2
    which = across.reshape(1)

    q = Gather(ring, jnp.concatenate([take(mine, att_own, 0), take(mine, out_a, 1)], axis=1), share, direct=True)
    q.step()
    up_piece = jnp.concatenate([take(mine, up_weight, 0), take(mine, out_b, 1)], axis=1)
    now = Bag(
        up=jnp.concatenate([up_piece, bias_rows]),
        rows=jnp.pad(lax.dynamic_slice_in_dim(patches, across * real_rows, real_rows, 0), grow),
        cotangent=jnp.pad(lax.dynamic_slice_in_dim(out_grad, across * real_rows, real_rows, 0), grow),
        place=place,
    )
    meet(now, q)
    u = Gather(ring, now.out.up, share)
    q.step()
    u.step()
    now.down = take(mine, down_weight, 1)
    now.stream, now.one, now.out_low, now.tail = blocked(
        start_kernel,
        [(which, SCALAR), (script_ids, SCALAR), (now.out.rows, ALL), (now.out.cotangent, ALL), (script_embed, ALL)]
        + [(v, ALL) for v in (attention_out_bias, norm2_gain, norm2_shift, down_proj_bias, norm1_gain, norm1_shift)]
        + [(now.place, ALL)],
        [((rows, width), F32, ALL), ((rows, width), BF16, ALL), ((rows, width), BF16, ALL), ((8, width), F32, ALL)],
        [],
        1,
        2 * dense * width,
    )
    meet(now, q, u)
    q.step()
    u.step()
    now.own_att = jnp.concatenate([take(now.place.T, att_own, 0), take(now.place.T, out_a, 1)], axis=1)
    meet(now, q, u)
    n = Gather(ring, now.out.down, share, near_first=True)
    bias_all = u.v.out.extra.astype(F32)
    bias_all = bias_all[:, 0:2] + bias_all[:, 2:4] + bias_all[:, 4:6]
    now.qkv_bias = bias_all[:, 0:1, :qkv_cols]
    now.up_bias = bias_all[:, 1:2, :hidden_cols]
    q.step()
    u.step()
    n.step()
    meet(now, q, u, n)
    u.step()
    n.step()

    def attention(at, own):
        return blocked(
            functools.partial(attention_kernel, head_cols, at == 0),
            [(which, SCALAR), (lengths, SCALAR), (now.one, ALL)] + q.specs(own) + [(now.qkv_bias, -at)],
            [((part, rows, qkv_cols), BF16, STEP), ((part, 8, rows), F32, STEP), ((part, rows, head_cols), BF16, STEP)],
            [],
            part,
            (dense * mp * qkv_cols + 2 * live) // 2,
            mp * heads * rows * rows // 2,
            at=at,
        )

    now.proj_b, now.lse_b, now.mixed_b = attention(part, None)
    now.proj_a, now.lse_a, now.mixed_a = attention(0, now.own_att)
    meet(now, q, u, n)
    u.step()
    n.step()
    order_t = now.place.T
    now.own_up = jnp.concatenate([take(order_t, up_weight, 0), take(order_t, out_b, 1)], axis=1)
    now.own_down = take(order_t, down_weight, 1)
    meet(now, q, u, n)
    n.step()
    now.middle, now.two = blocked(
        functools.partial(out_kernel, head_cols, hidden_cols),
        [(now.mixed_a, STEP), (now.mixed_b, part), (now.stream, ALL)]
        + q.specs(now.own_att) + u.specs(now.own_up) + [(now.tail, ALL)],
        [((rows, width), F32, ALL), ((rows, width), BF16, ALL)],
        [vmem((rows, width), F32)],
        mp,
        dense * mp * head_cols,
    )

    def half_shape(cols):
        return ((part, width // 2, cols), BF16, STEP)

    hidden_shape = ((part, rows, hidden_cols), BF16, STEP)

    def up_part(at, own):
        hidden, slope, low_half, high_half = blocked(
            functools.partial(up_kernel, at == 0),
            [(now.two, ALL), (now.out_low, ALL)] + u.specs(own) + [(now.up_bias, -at)],
            [hidden_shape, hidden_shape, half_shape(hidden_cols), half_shape(hidden_cols)],
            [],
            part,
            2 * dense * part * hidden_cols,
            rows * part * hidden_cols,
            at=at,
        )
        return hidden, slope, Scatter(ring, low_half, high_half)

    def pre_part(at, own_up, own_down, more, outputs, scratch):
        return blocked(
            functools.partial(pre_kernel, at == 0),
            [(now.two, ALL), (now.out_low, ALL)] + u.specs(own_up) + n.specs(own_down) + more,
            [half_shape(hidden_cols), half_shape(hidden_cols), ((part, 1, hidden_cols), F32, STEP), ((rows, width), F32, ALL)] + outputs,
            scratch,
            part,
            4 * dense * part * hidden_cols,
            at=at,
        )

    now.hidden_b, now.slope_b, cb = up_part(part, None)
    meet(now, q, u, n, cb)
    n.step()
    cb.go()
    now.hidden_a, now.slope_a, ca = up_part(0, now.own_up)
    meet(now, q, u, n, ca, cb)
    cb.fold()
    cb.go()
    ca.go()
    low_half, high_half, now.up_sum_b, now.block, now.two_sum = pre_part(
        part, None, None, [(now.out.slope_b, STEP), (now.out.hidden_b, STEP)], [((rows, width), F32, ALL)], []
    )
    bb = Scatter(ring, low_half, high_half)
    meet(now, q, u, n, ca, cb, bb)
    for each in (ca, cb):
        each.fold()
        each.go()
    bb.go()
    low_half, high_half, now.up_sum_a, now.block, now.grad_mid, now.mid, now.mid_sums = pre_part(
        0,
        now.own_up,
        now.out.own_down,
        [(now.out.slope_a, STEP), (now.out.hidden_a, STEP), (now.out.two_sum, ALL), (now.out.block, ALL), (now.out.middle, ALL), (now.tail, ALL)],
        [((rows, width), F32, ALL), ((rows, width), BF16, ALL), ((8, width), F32, ALL)],
        [vmem((rows, width), F32)],
    )
    ba = Scatter(ring, low_half, high_half)
    meet(now, q, u, ca, cb, ba, bb)
    for each in (bb, ca):
        each.fold()
        each.go()
    ba.go()
    rest_c = lax.ppermute(cb.settle(), MP, ring.blocks[-1])

    def attention_back(at, own, made):
        own_att, own_up = own
        q_specs, u_specs = q.specs(own_att), u.specs(own_up)
        weights = q_specs[:1] + u_specs[:1] + q_specs[1:] + u_specs[1:] if at == 0 else q_specs + u_specs
        return blocked(
            functools.partial(attention_back_kernel, head_cols, hidden_cols, at == 0),
            [(which, SCALAR), (lengths, SCALAR), (now.one, ALL), (now.mid, ALL)] + weights
            + [(a, STEP) for a in made],
            [((part, rows, qkv_cols), BF16, STEP), half_shape(4 * head_cols), half_shape(4 * head_cols), ((part, 1, qkv_cols), F32, STEP)],
            [],
            part,
            (dense * mp * 5 * head_cols + 5 * live) // 2,
            mp * heads * rows * rows // 2,
            at=at,
        )

    now.grad_b, low_half, high_half, now.proj_sum_b = attention_back(part, (None, None), (now.out.proj_b, now.out.mixed_b, now.out.lse_b))
    ab = Scatter(ring, low_half, high_half)
    now.rest_c = rest_c
    meet(now, q, u, ca, ba, bb, ab)
    for each in (ba, bb):
        each.fold()
        each.go()
    ab.go()
    ca.take_rest(now.out.rest_c, ring.blocks[0])
    ca.go()
    now.grad_a, low_half, high_half, now.proj_sum_a = attention_back(
        0, (now.own_att, now.out.own_up), (now.out.proj_a, now.out.mixed_a, now.out.lse_a)
    )
    aa = Scatter(ring, low_half, high_half)
    meet(now, q, ca, ba, bb, ab, aa)
    def back(value):
        return blocked(back_kernel, [(value, ALL), (now.place, ALL)], [((real_rows, width), F32, ALL)], [], 1, 2 * dense * width)[0]

    aa.go()
    ab.fold()
    ab.go()
    ba.fold()
    ba.go()
    rest_b = lax.ppermute(bb.settle(), MP, ring.blocks[-1])
    now.block = back(now.block)
    now.rest_b = rest_b
    meet(now, q, aa, ab, ba, ca)
    for each in (aa, ab):
        each.fold()
        each.go()
    ba.take_rest(now.out.rest_b, ring.blocks[0])
    ba.go()
    now.stream_grad, now.sums = blocked(
        functools.partial(first_kernel, head_cols),
        [(which, SCALAR), (script_ids, SCALAR), (now.out.mid_sums, ALL), (now.out.grad_a, STEP), (now.out.grad_b, part)]
        + q.specs(now.out.own_att)
        + [(a, ALL) for a in (now.out.stream, now.out.grad_mid, now.out.tail)],
        [((rows, width), F32, ALL), ((kinds + 8, width), F32, ALL)],
        [vmem((rows, width), F32)],
        mp,
        dense * mp * qkv_cols,
        vmem=60,
    )
    meet(now, aa, ab, ba, ca)

    n_vec = kinds + 8
    sub = head_cols // dp
    proj_sum = jnp.concatenate([now.out.proj_sum_a, now.out.proj_sum_b]).reshape(mp, 3, head_cols)
    qv = jnp.stack([proj_sum[:, 0], proj_sum[:, 2]], axis=1).reshape(mp * 2, dp, sub)
    qv = jnp.pad(qv, ((0, 0), (0, 0), (0, share - sub))).reshape(mp * 2, width)
    up_sum = jnp.concatenate([now.out.up_sum_a, now.out.up_sum_b])[:, 0]
    parts = jnp.concatenate(split3(jnp.concatenate([up_sum, qv], axis=0)), axis=0)
    cols = sum(jnp.split(jnp.dot(parts, now.place, preferred_element_type=F32), 3))
    small = jnp.concatenate([now.out.sums, cols], axis=0).T[None]
    ss = Scatter(ring, small[:, : width // 2], small[:, width // 2 :])
    ss.go()
    aa.fold()
    aa.go()
    rest_a = lax.ppermute(ab.settle(), MP, ring.blocks[-1])
    meet_kept(ss, aa)
    ss.fold()
    ss.go()
    kept = Bag(up=ba.total())
    meet(kept, ss)
    now.grad_up = kept.up
    ss.fold()
    ss.go()
    now.stream_grad = back(now.stream_grad)
    del now.place
    now.grad_down = ca.total()
    now.rest_a = rest_a
    meet(now, aa, ss)
    ss.v = Bag(held=ss.settle())
    aa.v.rest = now.out.rest_a
    meet(ss.v, aa)
    sums = ss.v.held
    aa.take_rest(aa.v.out.rest, ring.blocks[0])
    aa.go()
    last = Bag(parts=[sums] + [lax.ppermute(sums, MP, stage) for stage in ring.direct])
    grad_down, grad_up = now.grad_down, now.grad_up
    meet(last, aa)
    parts = [p[0] for p in last.parts]
    vectors = sum(p[:, :n_vec] for p in parts)
    vectors = lax.dynamic_slice_in_dim(vectors, across * (share // mp), share // mp, 0).T
    up_bias_grad = sum(p[:, n_vec + i] for i, p in enumerate(parts))
    qv_grad = sum(p[:sub, n_vec + mp + 2 * i : n_vec + mp + 2 * i + 2] for i, p in enumerate(parts)).T
    grad_att = aa.total()
    block, stream_grad = now.block, now.stream_grad

    return (
        block,
        stream_grad,
        vectors[:kinds],
        vectors[kinds + 4],
        vectors[kinds + 5],
        grad_att[:, : 3 * head_cols].reshape(share, 3, head_cols),
        qv_grad,
        grad_att[:, 3 * head_cols :].T,
        vectors[kinds + 0],
        vectors[kinds + 1],
        vectors[kinds + 2],
        grad_up,
        up_bias_grad,
        grad_down.T,
        vectors[kinds + 3],
    )


def solution(mesh):
    placed = (
        P(DP, None),
        P(DP),
        P(DP),
        P(),
        P(),
        P(),
        P(None, None, MP),
        P(None, MP),
        P(MP, None),
        P(),
        P(),
        P(),
        P(None, MP),
        P(MP),
        P(MP, None),
        P(),
        P(DP, None),
    )
    return jax.shard_map(
        on_device,
        mesh=mesh,
        in_specs=placed,
        out_specs=(
            P((DP, MP), None),
            P((DP, MP), None),
            P(None, (DP, MP)),
            P((DP, MP)),
            P((DP, MP)),
            P(DP, None, MP),
            P(None, (MP, DP)),
            P(MP, DP),
            P((DP, MP)),
            P((DP, MP)),
            P((DP, MP)),
            P(DP, MP),
            P((MP, DP)),
            P(MP, DP),
            P((DP, MP)),
        ),
        check_vma=False,
    )
```
